32 devices in a mesh: dp: 8 (over z, x), tensor: 4 (over y, core).
Axes of the slice: x: 2, y: 2, z: 4, core: 2. Of those that a mesh axis runs over, the one named last changes fastest.
Arguments:
- layer_inputs: bfloat16 [64, 512, 768], P(('dp', 'tensor')), may hold values from -6 to 6
- lengths: int32 [64], P(('dp', 'tensor')), may hold values from 64 to 512, as said below
- first_norm1_gain: float32 [768], replicated, may hold values from 0.1 to 1.9
- second_norm2_gain: float32 [768], replicated, may hold values from 0.1 to 1.9
- router: bfloat16 [768, 10], replicated, may hold values from -0.099609375 to 0.099609375
- query_key_value_weight: bfloat16 [3, 768, 768], P(None, None, 'tensor'), may hold values from -0.078125 to 0.078125
- relative_position_bias: bfloat16 [32, 12], P(None, 'tensor'), may hold values from -4 to 4
- attention_output_weight: bfloat16 [768, 768], P('tensor'), may hold values from -1.75 to 1.75
- input_weight: bfloat16 [768, 3072], P(None, 'tensor'), may hold values from -0.21875 to 0.21875
- output_weight: bfloat16 [3072, 768], P('tensor'), may hold values from -0.109375 to 0.109375
- adapter_down_input: bfloat16 [4, 768, 40], replicated, may hold values from -0.21875 to 0.21875
- adapter_down_attention: bfloat16 [768, 40], replicated, may hold values from -1.75 to 1.75
- adapter_down_output: bfloat16 [3072, 40], replicated, may hold values from -0.109375 to 0.109375
- adapter_up_query_key_value: bfloat16 [3, 40, 768], P(None, None, 'tensor'), may hold values from -3 to 3
- adapter_up_attention: bfloat16 [40, 768], replicated, may hold values from -3 to 3
- adapter_up_input: bfloat16 [40, 3072], P(None, 'tensor'), may hold values from -3 to 3
- adapter_up_output: bfloat16 [40, 768], replicated, may hold values from -3 to 3
- cotangent: bfloat16 [64, 512, 768], P(('dp', 'tensor')), may hold values from -6 to 6
Outputs:
- layer_output: bfloat16 [64, 512, 768], P(('dp', 'tensor'))
- grad_input: float32 [64, 512, 768], P(('dp', 'tensor'))
- grad_router: float32 [768, 10], replicated
- grad_lora_a_in: float32 [4, 768, 40], replicated
- grad_lora_a_o: float32 [768, 40], replicated
- grad_lora_a_out: float32 [3072, 40], replicated
- grad_lora_b_qkv: float32 [3, 40, 768], P(None, None, 'tensor')
- grad_lora_b_o: float32 [40, 768], replicated
- grad_lora_b_in: float32 [40, 3072], P(None, 'tensor')
- grad_lora_b_out: float32 [40, 768], replicated
The draws below stay inside these ranges and needn't reach their ends.
Inputs may be any that keep to these rules, and one draw needn't show every extreme that they name: `lengths`: each device's first sequence has all 512 tokens.
All inputs are finite; a program needn't handle non-finite values.
Results may differ from the reference program's by a relative error of at most 0.018.
The reference program's roundings to bfloat16 on the way count: a program that leaves them out, or rounds other values in their place, can miss the bound.
Values may be sent and summed in bfloat16 or wider, within the bound.
A program may use at most 192 MiB of HBM per device.

```python
import jax
import jax.numpy as jnp
import numpy as np
from jax import lax

MODEL_WIDTH = 768
HEADS = 12
HD = 64
HIDDEN_UNITS = 3072
NB = 32
MAX_DIST = 128
EXPERTS = 10
EXPERT_RANK = 4
SEQ_LEN = 512
SEQ_DEV = 2
HEAD_FEATURES = 768
ADAPTER_COLUMNS = 40
SEQS = 64


def draw_lengths(key, part):
    drawn_lengths = jax.random.randint(key, (SEQS,), SEQ_LEN // 8, SEQ_LEN + 1)
    places = jnp.arange(SEQS)
    drawn_lengths = jnp.where(places == 1, SEQ_LEN // 8, drawn_lengths)
    return jnp.where(places % SEQ_DEV == 0, SEQ_LEN, drawn_lengths).astype(jnp.int32)


def block_levels(rng, extent, pieces, smallest, high):
    loudness = 1.0
    for position, shards_of in pieces:
        heights = jax.random.uniform(jax.random.fold_in(jax.random.fold_in(rng, 6), position), (shards_of,), jnp.float32, smallest / len(pieces), high / len(pieces))
        loudness = loudness * jnp.repeat(jnp.exp(heights), extent[position] // shards_of).reshape((-1,) + (1,) * (len(extent) - 1 - position))
    return loudness


def bell_draw(own_key, extent, scale, bound, shards=(), held_as=jnp.bfloat16):
    gain = block_levels(own_key, extent, shards, -0.22, 0.18) if shards else 1.0
    drawn = jax.random.normal(own_key, extent, jnp.float32) * scale * gain
    return jnp.minimum(jnp.maximum(drawn, -bound), bound).astype(held_as)


def setup_inputs(seed: int = 0) -> dict:
    splits = jax.random.split(jax.random.key(seed), 19)
    return {
        "layer_inputs": bell_draw(splits[0], (SEQS, SEQ_LEN, MODEL_WIDTH), 1.0, 6.0, ((0, 32),)),
        "lengths": draw_lengths(jax.random.fold_in(splits[18], 71), 0),
        "first_norm1_gain": jnp.clip(1.0 + 0.18 * jax.random.normal(splits[2], (MODEL_WIDTH,), jnp.float32), 0.1, 1.9),
        "second_norm2_gain": jnp.clip(1.0 + 0.18 * jax.random.normal(splits[3], (MODEL_WIDTH,), jnp.float32), 0.1, 1.9),
        "router": bell_draw(splits[4], (MODEL_WIDTH, EXPERTS), 0.018, 0.099609375),
        "query_key_value_weight": bell_draw(splits[5], (3, MODEL_WIDTH, HEAD_FEATURES), (8 * MODEL_WIDTH) ** -0.5, 0.078125, ((2, 4),)),
        "relative_position_bias": bell_draw(splits[6], (NB, HEADS), 1.0, 4.0, ((1, 4),)),
        "attention_output_weight": bell_draw(splits[7], (HEAD_FEATURES, MODEL_WIDTH), (max(HEAD_FEATURES // 64, 4)) ** -0.5, 1.75, ((0, 4),)),
        "input_weight": bell_draw(splits[8], (MODEL_WIDTH, HIDDEN_UNITS), MODEL_WIDTH ** -0.5, 0.21875, ((1, 4),)),
        "output_weight": bell_draw(splits[9], (HIDDEN_UNITS, MODEL_WIDTH), HIDDEN_UNITS ** -0.5, 0.109375, ((0, 4),)),
        "adapter_down_input": bell_draw(splits[10], (4, MODEL_WIDTH, ADAPTER_COLUMNS), MODEL_WIDTH ** -0.5, 0.21875),
        "adapter_down_attention": bell_draw(splits[11], (HEAD_FEATURES, ADAPTER_COLUMNS), (max(HEAD_FEATURES // 64, 4)) ** -0.5, 1.75),
        "adapter_down_output": bell_draw(splits[12], (HIDDEN_UNITS, ADAPTER_COLUMNS), HIDDEN_UNITS ** -0.5, 0.109375),
        "adapter_up_query_key_value": bell_draw(splits[13], (3, ADAPTER_COLUMNS, HEAD_FEATURES), EXPERT_RANK ** -0.5, 3.0, ((2, 4),)),
        "adapter_up_attention": bell_draw(splits[14], (ADAPTER_COLUMNS, MODEL_WIDTH), EXPERT_RANK ** -0.5, 3.0),
        "adapter_up_input": bell_draw(splits[15], (ADAPTER_COLUMNS, HIDDEN_UNITS), EXPERT_RANK ** -0.5, 3.0, ((1, 4),)),
        "adapter_up_output": bell_draw(splits[16], (ADAPTER_COLUMNS, MODEL_WIDTH), EXPERT_RANK ** -0.5, 3.0),
        "cotangent": bell_draw(splits[17], (SEQS, SEQ_LEN, MODEL_WIDTH), 1.0, 6.0, ((0, 32),)),
    }


EPSILON = 1e-06
NEGATIVE = -1000000000.0
HIGHEST = lax.Precision.HIGHEST

@jax.custom_vjp
def lowrank_rows(v):
    return lax.optimization_barrier(v.astype(jnp.bfloat16)).astype(jnp.float32)

@jax.custom_vjp
def lowrank_backward(v):
    return v

def low_keep(v):
    return (lowrank_rows(v), None)

def low_pass(kept, grad):
    return (grad,)

def back_keep(v):
    return (v, None)

def back_low(kept, grad):
    return (lowrank_rows(grad),)
lowrank_rows.defvjp(low_keep, low_pass)
lowrank_backward.defvjp(back_keep, back_low)

def bucket_table(seq_length):
    places = np.arange(seq_length)
    relative = places[None, :] - places[:, None]
    half_count = NB // 2
    exact_count = half_count // 2
    distance = np.abs(relative)
    scaled = np.log(np.maximum(distance, 1) / exact_count) / np.log(MAX_DIST / exact_count) * (half_count - exact_count)
    far_bucket = np.minimum(exact_count + scaled.astype(np.int32), half_count - 1)
    return ((relative > 0) * half_count + np.where(distance < exact_count, distance, far_bucket)).astype(np.int32)

def matmul_high(a, b):
    return jnp.matmul(a, b, precision=HIGHEST)

def rms_norm(values, gain_vec):
    return values * lax.rsqrt(lax.optimization_barrier(jnp.mean(values * values, axis=-1, keepdims=True)) + EPSILON) * gain_vec

def round_twice(v):
    return lowrank_rows(lowrank_backward(v))

def project_rows(inputs, weight, down_map, up_map, gate_repeated):
    lowrank = lowrank_backward(matmul_high(inputs, down_map))
    return matmul_high(inputs, weight) + matmul_high(lowrank_rows(lowrank * gate_repeated), up_map)

def forward(input_block, lengths_block, parameters, frozen):
    router, adapter_down_input, adapter_down_attention, adapter_down_output, adapter_up_query_key_value, adapter_up_attention, adapter_up_input, adapter_up_output = parameters
    first_norm1_gain, second_norm2_gain, query_key_value_weight, bias_table, attention_output_weight, input_weight, output_weight = frozen
    seq_count = input_block.shape[0]
    input_matrix = input_block.reshape(-1, MODEL_WIDTH)
    first_normed1 = lowrank_rows(rms_norm(input_matrix, first_norm1_gain))
    gate_probs = jax.nn.softmax(lowrank_backward(matmul_high(first_normed1, router)), axis=-1)
    gate_repeated = jnp.repeat(gate_probs, EXPERT_RANK, axis=1)
    head_layout = (seq_count, SEQ_LEN, HEADS, HD)
    query_matrix = round_twice(project_rows(first_normed1, query_key_value_weight[0], adapter_down_input[0], adapter_up_query_key_value[0], gate_repeated)).reshape(head_layout)
    key_matrix = round_twice(project_rows(first_normed1, query_key_value_weight[1], adapter_down_input[1], adapter_up_query_key_value[1], gate_repeated)).reshape(head_layout)
    value_matrix = round_twice(project_rows(first_normed1, query_key_value_weight[2], adapter_down_input[2], adapter_up_query_key_value[2], gate_repeated)).reshape(head_layout)
    key_valid = jnp.arange(SEQ_LEN)[None, :] < lengths_block[:, None]

    def attend(inputs):
        q_seq, k_seq, v_seq, valid_keys = inputs
        scores = lowrank_backward(jnp.einsum('qhd,khd->hqk', q_seq, k_seq, precision=HIGHEST) + bias_table)
        scores = jnp.where(valid_keys[None, None, :], scores, NEGATIVE)
        attn_probs = jax.nn.softmax(scores, axis=-1)
        return jnp.einsum('hqk,khd->qhd', lowrank_rows(attn_probs), v_seq, precision=HIGHEST).reshape(SEQ_LEN, HEAD_FEATURES)
    context_rows = lax.map(jax.checkpoint(attend), (query_matrix, key_matrix, value_matrix, key_valid))
    context_rows = round_twice(context_rows.reshape(-1, HEAD_FEATURES))
    hidden_first1 = input_matrix + lowrank_backward(project_rows(context_rows, attention_output_weight, adapter_down_attention, adapter_up_attention, gate_repeated))
    second_normed2 = lowrank_rows(rms_norm(hidden_first1, second_norm2_gain))
    active_flags = lowrank_rows(jax.nn.silu(lowrank_backward(project_rows(second_normed2, input_weight, adapter_down_input[3], adapter_up_input, gate_repeated))))
    block_output = hidden_first1 + lowrank_backward(project_rows(active_flags, output_weight, adapter_down_output, adapter_up_output, gate_repeated))
    return block_output.reshape(input_block.shape)

def reference(layer_inputs, lengths, first_norm1_gain, second_norm2_gain, router, query_key_value_weight, relative_position_bias, attention_output_weight, input_weight, output_weight, adapter_down_input, adapter_down_attention, adapter_down_output, adapter_up_query_key_value, adapter_up_attention, adapter_up_input, adapter_up_output, cotangent):
    single_float = jnp.float32
    bucket_ids = jnp.asarray(bucket_table(SEQ_LEN))
    bias_table = jnp.transpose(jnp.take(relative_position_bias.astype(single_float), bucket_ids, axis=0), (2, 0, 1))
    frozen = (first_norm1_gain.astype(single_float), second_norm2_gain.astype(single_float), query_key_value_weight.astype(single_float), bias_table, attention_output_weight.astype(single_float), input_weight.astype(single_float), output_weight.astype(single_float))
    parameters = (router.astype(single_float), adapter_down_input.astype(single_float), adapter_down_attention.astype(single_float), adapter_down_output.astype(single_float), adapter_up_query_key_value.astype(single_float), adapter_up_attention.astype(single_float), adapter_up_input.astype(single_float), adapter_up_output.astype(single_float))
    group_size = 8
    input_groups = layer_inputs.reshape(SEQS // group_size, group_size, SEQ_LEN, MODEL_WIDTH)
    length_groups = lengths.reshape(SEQS // group_size, group_size)
    cot_groups = cotangent.reshape(SEQS // group_size, group_size, SEQ_LEN, MODEL_WIDTH)

    def group_step(grad_total, group_item):
        input_group, length_group, cot_group = group_item

        def apply_layer(input_values, param_values):
            return forward(input_values, length_group, param_values, frozen)
        block_output, pull_back = jax.vjp(apply_layer, input_group.astype(single_float), parameters)
        grad_values, grad_params = pull_back(cot_group.astype(single_float))
        grad_total = jax.tree.map(jnp.add, grad_total, grad_params)
        return (grad_total, (block_output.astype(jnp.bfloat16), grad_values))
    start_total = jax.tree.map(jnp.zeros_like, parameters)
    grad_total, (outputs, grad_inputs) = lax.scan(group_step, start_total, (input_groups, length_groups, cot_groups))
    return (outputs.reshape(SEQS, SEQ_LEN, MODEL_WIDTH), grad_inputs.reshape(SEQS, SEQ_LEN, MODEL_WIDTH), grad_total[0], grad_total[1], grad_total[2], grad_total[3], grad_total[4], grad_total[5], grad_total[6], grad_total[7])
```

```python
import jax
import jax.numpy as jnp
import numpy as np
from jax import lax
from jax.experimental import pallas as pl
from jax.experimental.pallas import tpu as pltpu
from jax.sharding import PartitionSpec as P

NB = 32
MAX_DIST = 128
EPS = 1e-06
NEG = -1000000000.0
F32 = jnp.float32
BF16 = jnp.bfloat16
PAD = 64
VMEM_LIMIT = 60 * 1024 * 1024


def nn(a, b):
    return lax.dot_general(a, b, (((1,), (0,)), ((), ())), preferred_element_type=F32)


def nt(a, b):
    return lax.dot_general(a, b, (((1,), (1,)), ((), ())), preferred_element_type=F32)


def tn(a, b):
    return lax.dot_general(a, b, (((0,), (0,)), ((), ())), preferred_element_type=F32)


def bucket_of(relative):
    half = NB // 2
    exact = half // 2
    distance = np.abs(relative)
    scaled = np.log(np.maximum(distance, 1) / exact) / np.log(MAX_DIST / exact) * (half - exact)
    far = np.minimum(exact + scaled.astype(np.int32), half - 1)
    return ((relative > 0) * half + np.where(distance < exact, distance, far)).astype(np.int32)


def bucket_lines(seq):
    m = np.arange(2 * seq)
    rel = seq - 128 - m
    rel = np.where(rel < -seq, rel + 2 * seq, rel)
    rel = np.clip(rel, -(seq - 1), seq - 1)
    ids = bucket_of(rel)
    return (ids[None, :] == np.arange(NB)[:, None]).astype(np.float32)


def attention_forward(
    lens, x_ref, g1_ref, wsm_ref, wqkv_ref, bqkv_ref, rb_ref, oh_ref,
    n1_ref, low_ref, gate_ref, gate_t_ref, gated_ref, qkv_ref, e_ref, r_ref, ctx_ref,
    small, urow, brow,
):
    tokens = x_ref.shape[0]
    groups = wqkv_ref.shape[0]
    inner = wqkv_ref.shape[1] // 3
    seq = e_ref.shape[1]
    seqs = tokens // seq
    heads_here = e_ref.shape[0] // (groups * seqs)
    hd = inner // heads_here
    tb = 256
    experts_rep = 40

    def norm(i, c):
        rows = pl.ds(pl.multiple_of(i * tb, tb), tb)
        x = x_ref[rows, :].astype(F32)
        n1 = (x * lax.rsqrt(jnp.mean(x * x, axis=1, keepdims=True) + EPS) * g1_ref[...]).astype(BF16)
        n1_ref[rows, :] = n1
        small = nt(wsm_ref[...], n1)
        low = small[: 3 * PAD]
        logits = small[3 * PAD :]
        valid = lax.broadcasted_iota(jnp.int32, logits.shape, 0) < experts_rep
        logits = jnp.where(valid, logits, -jnp.inf)
        ex = jnp.exp(logits - jnp.max(logits, axis=0, keepdims=True))
        gate = ex / (jnp.sum(ex, axis=0, keepdims=True) * 0.25)
        low_ref[:, rows] = low
        gate_ref[:, rows] = gate
        gate_t_ref[rows, :] = jnp.concatenate([gate, gate], axis=0).T
        for p in range(3):
            gated_ref[p * PAD : (p + 1) * PAD, rows] = (low[p * PAD : (p + 1) * PAD] * gate).astype(BF16)
        return c

    lax.fori_loop(0, tokens // tb, norm, 0)
    u = nn(rb_ref[...], oh_ref[...])
    for h in range(groups * heads_here):
        urow[h] = u[h : h + 1]

    maskrow = jnp.where(
        lax.broadcasted_iota(jnp.int32, (16, seq), 1) < lens[seqs - 1], 0.0, NEG
    )
    maskrow = jnp.where(lax.broadcasted_iota(jnp.int32, (16, seq), 0) == 0, maskrow, 0.0).astype(BF16)
    onerow = (lax.broadcasted_iota(jnp.int32, (16, seq), 0) == 0).astype(F32).astype(BF16)

    def group(g, c):
        proj = nt(wqkv_ref[g], n1_ref[...])
        for p in range(3):
            up = tn(bqkv_ref[g, p], gated_ref[p * PAD : (p + 1) * PAD, :])
            qkv_ref[g, p] = (proj[p * inner : (p + 1) * inner] + up).astype(BF16)

        def head(h, c):
            gh = g * heads_here + h
            line = jnp.broadcast_to(urow[gh], (128, 2 * seq))
            brow[...] = pltpu.roll(line, 0, 1, stride=1, stride_axis=0)[:, : 2 * seq - 128]
            feats = pl.ds(pl.multiple_of(h * hd, hd), hd)
            for s in range(seqs):
                q = qkv_ref[g, 0, feats, s * seq : (s + 1) * seq]
                k = qkv_ref[g, 1, feats, s * seq : (s + 1) * seq]
                v = qkv_ref[g, 2, feats, s * seq : (s + 1) * seq]
                if s > 0:
                    q = jnp.concatenate([q, onerow], axis=0)
                    k = jnp.concatenate([k, maskrow], axis=0)
                qb = 256
                for b in range(seq // qb):
                    st = tn(k, q[:, b * qb : (b + 1) * qb])
                    bias = jnp.concatenate(
                        [
                            brow[:, seq - 128 - 128 * kb + b * qb : seq - 128 - 128 * kb + (b + 1) * qb]
                            for kb in range(seq // 128)
                        ],
                        axis=0,
                    )
                    st = st + bias
                    ex = jnp.exp(st - jnp.max(st, axis=0, keepdims=True))
                    recip = 1.0 / jnp.sum(ex, axis=0, keepdims=True)
                    eb = ex.astype(BF16)
                    e_ref[gh * seqs + s, :, b * qb : (b + 1) * qb] = eb
                    r_ref[gh, :, s * seq + b * qb : s * seq + (b + 1) * qb] = recip
                    ot = nn(v, eb) * recip
                    ctx_ref[
                        pl.ds(pl.multiple_of(gh * hd, hd), hd), s * seq + b * qb : s * seq + (b + 1) * qb
                    ] = ot.astype(BF16)
            return c

        lax.fori_loop(0, heads_here, head, 0)
        return c

    lax.fori_loop(0, groups, group, 0)


def feed_forward(
    x_ref, c_ref, g2_ref, ctx_ref, gate_ref, wo_ref, ao_ref, bo_ref, ain_ref, bin_ref, aout_ref, bout_ref,
    win_ref, wout_ref,
    y_ref, dh_ref, dctx_ref, z_ref, gao_ref, gaout_ref, gbo_ref, gbin_ref, gbout_ref, gain_ref,
    h1, n2, acc, dn2, low_o, low_in, low_out, d_low_in, gated_in, gated_in_t, dgo, dgo_t, d_low_out,
):
    tokens = x_ref.shape[0]
    groups = win_ref.shape[0]
    tb = 256
    blocks = tokens // tb

    def rows_of(i):
        return pl.ds(pl.multiple_of(i * tb, tb), tb)

    def first(i, c):
        rows = rows_of(i)
        gate = gate_ref[rows, :PAD]
        ctx = ctx_ref[:, rows].T
        lo = nt(ctx, ao_ref[...])
        low_o[rows, :] = lo
        gated_o = (lo * gate).astype(BF16)
        hidden = x_ref[rows, :].astype(F32) + nn(ctx, wo_ref[...]) + nn(gated_o, bo_ref[...])
        h1[rows, :] = hidden
        norm = (
            hidden * lax.rsqrt(jnp.mean(hidden * hidden, axis=1, keepdims=True) + EPS) * g2_ref[...]
        ).astype(BF16)
        n2[rows, :] = norm
        li = nt(norm, ain_ref[...])
        low_in[rows, :] = li
        gi = li * gate
        gated_in[rows, :] = gi.astype(BF16)
        dlo = nt(c_ref[rows, :], bout_ref[...])
        d_low_out[rows, :] = dlo
        dg = dlo * gate
        dgo[rows, :] = dg.astype(BF16)
        both = jnp.concatenate([gi, dg], axis=1).T.astype(BF16)
        gated_in_t[:, rows] = both[:PAD]
        dgo_t[:, rows] = both[PAD:]
        return c

    lax.fori_loop(0, blocks, first, 0)

    def chunk(step, c):
        k = step // blocks
        i = step % blocks
        rows = rows_of(i)
        pre = nn(n2[rows, :], win_ref[k]) + nn(gated_in[rows, :], bin_ref[k])
        da = nt(c_ref[rows, :], wout_ref[k]) + nn(dgo[rows, :], aout_ref[k])
        sig = 1.0 / (1.0 + jnp.exp(-pre))
        active = (pre * sig).astype(BF16)
        dpre = (da * sig * (1.0 + pre * (1.0 - sig))).astype(BF16)
        part = nn(active, wout_ref[k])
        lo = nt(active, aout_ref[k])
        dn = nt(dpre, win_ref[k])
        dl = nt(dpre, bin_ref[k])
        ga = nn(dgo_t[:, rows], active)
        gb = nn(gated_in_t[:, rows], dpre)

        @pl.when(k == 0)
        def _():
            acc[rows, :] = part
            low_out[rows, :] = lo
            dn2[rows, :] = dn
            d_low_in[rows, :] = dl

        @pl.when(k > 0)
        def _():
            acc[rows, :] += part
            low_out[rows, :] += lo
            dn2[rows, :] += dn
            d_low_in[rows, :] += dl

        @pl.when(i == 0)
        def _():
            gaout_ref[k] = ga
            gbin_ref[k] = gb

        @pl.when(i > 0)
        def _():
            gaout_ref[k] += ga
            gbin_ref[k] += gb

        return c

    lax.fori_loop(0, groups * blocks, chunk, 0)

    gbout_ref[...] = jnp.zeros_like(gbout_ref)
    gbo_ref[...] = jnp.zeros_like(gbo_ref)
    gao_ref[...] = jnp.zeros_like(gao_ref)
    gain_ref[...] = jnp.zeros_like(gain_ref)

    def last(i, c):
        rows = rows_of(i)
        gate = gate_ref[rows, :PAD]
        cot = c_ref[rows, :]
        hidden = h1[rows, :]
        go = low_out[rows, :] * gate
        y_ref[rows, :] = (hidden + acc[rows, :] + nn(go.astype(BF16), bout_ref[...])).astype(BF16)
        dli = d_low_in[rows, :]
        dgi = dli * gate
        dn = dn2[rows, :] + nn(dgi.astype(BF16), ain_ref[...])
        both = jnp.concatenate([go, dgi], axis=1).T.astype(BF16)
        gbout_ref[...] += nn(both[:PAD], cot)
        gain_ref[...] += nn(both[PAD:], n2[rows, :])
        inv = lax.rsqrt(jnp.mean(hidden * hidden, axis=1, keepdims=True) + EPS)
        up = dn * g2_ref[...]
        dh = (
            cot.astype(F32)
            + inv * up
            - hidden * (inv * inv * inv) * jnp.mean(hidden * up, axis=1, keepdims=True)
        )
        dh_ref[rows, :] = dh
        da = dh.astype(BF16)
        dlo = nt(da, bo_ref[...])
        lo = low_o[rows, :]
        dg = dlo * gate
        dgb = dg.astype(BF16)
        both = jnp.concatenate([lo * gate, dg], axis=1).T.astype(BF16)
        gbo_ref[...] += nn(both[:PAD], da)
        gao_ref[...] += nt(both[PAD:], ctx_ref[:, rows])
        dctx_ref[:, rows] = (nt(wo_ref[...], da) + tn(ao_ref[...], both[PAD:])).astype(BF16)
        z = dlo * lo + dli * low_in[rows, :] + d_low_out[rows, :] * low_out[rows, :]
        z_ref[:, rows] = jnp.concatenate([z, z], axis=1).T[:PAD]
        return c

    lax.fori_loop(0, blocks, last, 0)


def attention_backward(
    x_ref, g1_ref, wsm_ref, wqkv_ref, bqkv_ref, n1_ref, low_ref, gate_ref, gated_ref, qkv_ref, e_ref, r_ref,
    ctx_ref, dctx_ref, z_ref, dh_ref, sum_ref,
    gx_ref, gsm_ref, gbqkv_ref,
    dqkv, dlow, dn1, dsmall,
):
    tokens = x_ref.shape[0]
    groups = wqkv_ref.shape[0]
    inner = wqkv_ref.shape[1] // 3
    seq = e_ref.shape[1]
    seqs = tokens // seq
    heads_here = e_ref.shape[0] // (groups * seqs)
    hd = inner // heads_here
    qb = 256

    def group(g, c):
        def head(h, c):
            gh = g * heads_here + h
            feats = pl.ds(pl.multiple_of(h * hd, hd), hd)
            full = pl.ds(pl.multiple_of(gh * hd, hd), hd)
            for s in range(seqs):
                cols = slice(s * seq, (s + 1) * seq)
                q = qkv_ref[g, 0, feats, cols]
                k = qkv_ref[g, 1, feats, cols]
                v = qkv_ref[g, 2, feats, cols]
                dk = jnp.zeros((hd, seq), F32)
                dv = jnp.zeros((hd, seq), F32)
                for b in range(seq // qb):
                    part = slice(s * seq + b * qb, s * seq + (b + 1) * qb)
                    do = (dctx_ref[full, part].astype(F32) * r_ref[gh, :, part]).astype(BF16)
                    delta = jnp.sum(do.astype(F32) * ctx_ref[full, part].astype(F32), axis=0, keepdims=True)
                    eb = e_ref[gh * seqs + s, :, b * qb : (b + 1) * qb]
                    dp = tn(v, do)
                    ds = (eb.astype(F32) * (dp - delta)).astype(BF16)
                    dqkv[feats, part] = nn(k, ds).astype(BF16)
                    dk = dk + nt(q[:, b * qb : (b + 1) * qb], ds)
                    dv = dv + nt(do, eb)
                dqkv[pl.ds(pl.multiple_of(inner + h * hd, hd), hd), cols] = dk.astype(BF16)
                dqkv[pl.ds(pl.multiple_of(2 * inner + h * hd, hd), hd), cols] = dv.astype(BF16)
            return c

        lax.fori_loop(0, heads_here, head, 0)
        dn = tn(wqkv_ref[g], dqkv[...])

        @pl.when(g == 0)
        def _():
            dn1[...] = dn

        @pl.when(g > 0)
        def _():
            dn1[...] += dn

        for p in range(3):
            d = dqkv[p * inner : (p + 1) * inner, :]
            dl = nn(bqkv_ref[g, p], d)

            @pl.when(g == 0)
            def _():
                dlow[p * PAD : (p + 1) * PAD, :] = dl

            @pl.when(g > 0)
            def _():
                dlow[p * PAD : (p + 1) * PAD, :] += dl

            gbqkv_ref[g, p] = nt(gated_ref[p * PAD : (p + 1) * PAD, :], d)
        return c

    lax.fori_loop(0, groups, group, 0)
    gate = gate_ref[...]
    z = z_ref[...]
    for p in range(3):
        part = slice(p * PAD, (p + 1) * PAD)
        z = z + dlow[part, :] * low_ref[part, :]
        dsmall[part, :] = (dlow[part, :] * gate).astype(BF16)
    zh = z.astype(BF16)
    zl = (z - zh.astype(F32)).astype(BF16)
    dgate = nn(sum_ref[...], zh) + nn(sum_ref[...], zl)
    total = jnp.sum(gate * z, axis=0, keepdims=True)
    dlogit = gate * (dgate - total)
    row = lax.broadcasted_iota(jnp.int32, dlogit.shape, 0)
    keep = jnp.logical_and(row % 4 == 0, row < 40)
    dsmall[3 * PAD :, :] = jnp.where(keep, dlogit, 0.0).astype(BF16)
    gsm_ref[...] = nn(dsmall[...], n1_ref[...])

    tb = 256

    def finish(i, c):
        rows = pl.ds(pl.multiple_of(i * tb, tb), tb)
        dn = (dn1[:, rows] + tn(wsm_ref[...], dsmall[:, rows])).T
        x = x_ref[rows, :].astype(F32)
        inv = lax.rsqrt(jnp.mean(x * x, axis=1, keepdims=True) + EPS)
        up = dn * g1_ref[...]
        gx_ref[rows, :] = (
            dh_ref[rows, :] + inv * up - x * (inv * inv * inv) * jnp.mean(x * up, axis=1, keepdims=True)
        )
        return c

    lax.fori_loop(0, tokens // tb, finish, 0)


def call(body, name, outs, scratch, args, smem=0):
    specs = [pl.BlockSpec(memory_space=pltpu.SMEM)] * smem
    specs += [pl.BlockSpec(memory_space=pltpu.VMEM)] * (len(args) - smem)
    return pl.pallas_call(
        body,
        name=name,
        out_shape=[jax.ShapeDtypeStruct(s, d) for s, d in outs],
        in_specs=specs,
        out_specs=[pl.BlockSpec(memory_space=pltpu.VMEM)] * len(outs),
        scratch_shapes=[pltpu.VMEM(s, d) for s, d in scratch],
        compiler_params=pltpu.CompilerParams(vmem_limit_bytes=VMEM_LIMIT),
    )(*args)


def pad_rows(a):
    width = [(0, 0)] * (a.ndim - 2) + [(0, PAD - a.shape[-2]), (0, 0)]
    return jnp.pad(a, width)


def shards(
    layer_inputs, lengths, first_gain, second_gain, router, wqkv, bias_table, wo, win, wout,
    a_in, a_o, a_out, b_qkv, b_o, b_in, b_out, cotangent,
):
    groups = lax.axis_size("tensor")
    member = lax.axis_index("tensor")
    seqs, seq, width = layer_inputs.shape
    tokens = seqs * seq
    inner = wo.shape[0]
    heads_here = bias_table.shape[1]
    heads = heads_here * groups
    hd = inner // heads_here
    hidden = win.shape[1]
    experts = router.shape[1]
    cols = a_in.shape[2]
    rank = cols // experts

    def gather(v):
        return lax.all_gather(v, "tensor", axis=0)

    x = layer_inputs.reshape(tokens, width)
    cot = cotangent.reshape(tokens, width)
    g1 = first_gain.reshape(1, width)
    g2 = second_gain.reshape(1, width)
    at = jnp.swapaxes(a_in, 1, 2)
    rrep = jnp.repeat(router.T, rank, axis=0)
    wsm = pad_rows(jnp.concatenate([at[:3], rrep[None]], axis=0)).reshape(4 * PAD, width)
    wqkv_all = gather(jnp.swapaxes(wqkv, 1, 2).reshape(3 * inner, width))
    bqkv_all = pad_rows(gather(b_qkv))
    rb = gather(bias_table.T).reshape(heads, NB)
    rb = jnp.pad(rb, ((0, 16 - heads % 16), (0, 0)))
    wo_all = gather(wo).reshape(groups * inner, width)
    win_all = gather(win)
    wout_all = gather(wout)
    bin_all = pad_rows(gather(b_in))
    ao = pad_rows(a_o.T)
    ain = pad_rows(at[3])
    aout = pad_rows(jnp.swapaxes(a_out.T.reshape(cols, groups, hidden), 0, 1))
    bo = pad_rows(b_o)
    bout = pad_rows(b_out)
    onehot = jnp.asarray(bucket_lines(seq), BF16)

    n1, low, gate, gate_t, gated, qkv, e, r, ctx = call(
        attention_forward,
        "attention_forward",
        [
            ((tokens, width), BF16),
            ((3 * PAD, tokens), F32),
            ((PAD, tokens), F32),
            ((tokens, 2 * PAD), F32),
            ((3 * PAD, tokens), BF16),
            ((groups, 3, inner, tokens), BF16),
            ((heads * seqs, seq, seq), BF16),
            ((heads, 1, tokens), F32),
            ((groups * inner, tokens), BF16),
        ],
        [
            ((8, 128), F32),
            ((heads, 1, 2 * seq), F32),
            ((128, 2 * seq - 128), F32),
        ],
        (lengths, x, g1, wsm, wqkv_all, bqkv_all, rb, onehot),
        smem=1,
    )
    y, dh, dctx, z, gao, gaout, gbo, gbin, gbout, gain = call(
        feed_forward,
        "feed_forward",
        [
            ((tokens, width), BF16),
            ((tokens, width), F32),
            ((groups * inner, tokens), BF16),
            ((PAD, tokens), F32),
            ((PAD, groups * inner), F32),
            ((groups, PAD, hidden), F32),
            ((PAD, width), F32),
            ((groups, PAD, hidden), F32),
            ((PAD, width), F32),
            ((PAD, width), F32),
        ],
        [
            ((tokens, width), F32),
            ((tokens, width), BF16),
            ((tokens, width), F32),
            ((tokens, width), F32),
            ((tokens, PAD), F32),
            ((tokens, PAD), F32),
            ((tokens, PAD), F32),
            ((tokens, PAD), F32),
            ((tokens, PAD), BF16),
            ((PAD, tokens), BF16),
            ((tokens, PAD), BF16),
            ((PAD, tokens), BF16),
            ((tokens, PAD), F32),
        ],
        (x, cot, g2, ctx, gate_t, wo_all, ao, bo, ain, bin_all, aout, bout, win_all, wout_all),
    )
    c = np.arange(PAD)
    same = (c[:, None] // rank == c[None, :] // rank) & (c[None, :] < cols)
    gx, gsm, gbqkv = call(
        attention_backward,
        "attention_backward",
        [
            ((tokens, width), F32),
            ((4 * PAD, width), F32),
            ((groups, 3, PAD, inner), F32),
        ],
        [
            ((3 * inner, tokens), BF16),
            ((3 * PAD, tokens), F32),
            ((width, tokens), F32),
            ((4 * PAD, tokens), BF16),
        ],
        (x, g1, wsm, wqkv_all, bqkv_all, n1, low, gate, gated, qkv, e, r, ctx, dctx, z, dh, jnp.asarray(same, BF16)),
    )
    g_in = jnp.concatenate([gsm.reshape(4, PAD, width)[:3, :cols], gain[None, :cols]], axis=0)
    g_router = gsm.reshape(4, PAD, width)[3, :cols:rank]
    summed = lax.psum(
        (g_router, g_in, gao[:cols], gaout[:, :cols], gbqkv[:, :, :cols], gbo[:cols], gbin[:, :cols], gbout[:cols]),
        ("dp", "tensor"),
    )
    return (
        y.reshape(layer_inputs.shape),
        gx.reshape(layer_inputs.shape),
        summed[0].T,
        jnp.swapaxes(summed[1], 1, 2),
        summed[2].T,
        jnp.swapaxes(summed[3], 0, 1).reshape(cols, groups * hidden).T,
        lax.dynamic_index_in_dim(summed[4], member, 0, keepdims=False),
        summed[5],
        lax.dynamic_index_in_dim(summed[6], member, 0, keepdims=False),
        summed[7],
    )


def solution(mesh):
    rows = P(("dp", "tensor"), None, None)
    placed = (
        rows, P(("dp", "tensor")), P(), P(), P(), P(None, None, "tensor"), P(None, "tensor"), P("tensor", None),
        P(None, "tensor"), P("tensor", None), P(), P(), P(), P(None, None, "tensor"), P(), P(None, "tensor"), P(), rows,
    )
    return jax.shard_map(
        shards,
        mesh=mesh,
        in_specs=placed,
        out_specs=(rows, rows, P(), P(), P(), P(), P(None, None, "tensor"), P(), P(None, "tensor"), P()),
        check_vma=False,
    )
```

```python
import jax
import jax.numpy as jnp
import numpy as np
from jax import lax
from jax.experimental import pallas as pl
from jax.experimental.pallas import tpu as pltpu
from jax.sharding import PartitionSpec as P

NB = 32
MAX_DIST = 128
EPS = 1e-06
NEG = -1000000000.0
F32 = jnp.float32
BF16 = jnp.bfloat16
PAD = 64
VMEM_LIMIT = 60 * 1024 * 1024


def nn(a, b):
    return lax.dot_general(a, b, (((1,), (0,)), ((), ())), preferred_element_type=F32)


def nt(a, b):
    return lax.dot_general(a, b, (((1,), (1,)), ((), ())), preferred_element_type=F32)


def tn(a, b):
    return lax.dot_general(a, b, (((0,), (0,)), ((), ())), preferred_element_type=F32)


def flip(index, bit):
    return index + (1 - 2 * ((index // bit) % 2)) * bit


def group_at(member, step):
    high = (member // 2 + step // 2) % 2
    low = (member % 2 + step % 2) % 2
    return 2 * high + low


class Links:
    def __init__(self, send, recv):
        self.send, self.recv, self.count, self.waiting = send, recv, 0, []

    def __call__(self, src, dst, device):
        n = self.count
        self.count += 1
        return pltpu.make_async_remote_copy(
            src_ref=src, dst_ref=dst, send_sem=self.send.at[n], recv_sem=self.recv.at[n],
            device_id=device, device_id_type=pl.DeviceIdType.MESH,
        )


def greet(devices):
    barrier = pltpu.get_barrier_semaphore()
    for device in devices:
        pl.semaphore_signal(barrier, inc=1, device_id=device, device_id_type=pl.DeviceIdType.MESH)
    pl.semaphore_wait(barrier, len(devices))


class Places:
    def __init__(self):
        d, t = lax.axis_index("dp"), lax.axis_index("tensor")
        self.d, self.t = d, t
        self.half = d % 2
        self.core = (d, flip(t, 1))
        self.y = (d, flip(t, 2))
        self.across = (d, flip(flip(t, 1), 2))
        self.x = (flip(d, 1), t)
        self.y_group = flip(t, 2)


def spread(links, places, own, whole, chunks):
    g, g2 = places.t, places.y_group
    total = own.shape[0]
    rows = total // 2 // chunks
    out = {"core": links(own, whole.at[g], places.core), "y": [], "x": [], "near": [], "far": []}
    for j in range(chunks):
        mine = pl.ds(pl.multiple_of(places.half * (total // 2) + j * rows, 16), rows)
        other = pl.ds(pl.multiple_of((1 - places.half) * (total // 2) + j * rows, 16), rows)
        out["y"].append(links(own.at[mine], whole.at[g, mine], places.y))
        out["x"].append(links(whole.at[g2, mine], whole.at[g2, mine], places.x))
        out["near"].append(links(whole.at[g2, mine], whole.at[g2, mine], places.core))
        out["far"].append(links(whole.at[g2, other], whole.at[g2, other], places.core))
    return out


def relay(item, j):
    item["y"][j].wait_recv()
    item["x"][j].start()
    item["near"][j].start()


def close(item, j):
    item["x"][j].wait_recv()
    item["far"][j].start()


def bucket_of(relative):
    half = NB // 2
    exact = half // 2
    distance = np.abs(relative)
    scaled = np.log(np.maximum(distance, 1) / exact) / np.log(MAX_DIST / exact) * (half - exact)
    far = np.minimum(exact + scaled.astype(np.int32), half - 1)
    return ((relative > 0) * half + np.where(distance < exact, distance, far)).astype(np.int32)


def bucket_lines(seq):
    m = np.arange(2 * seq)
    rel = seq - 128 - m
    rel = np.where(rel < -seq, rel + 2 * seq, rel)
    rel = np.clip(rel, -(seq - 1), seq - 1)
    ids = bucket_of(rel)
    return (ids[None, :] == np.arange(NB)[:, None]).astype(np.float32)


def attention_forward(
    lens, x_ref, g1_ref, wsm_ref, oh_ref, wqkv_own, bqkv_own, rb_own, wo_own, win_own, bin_own,
    n1_ref, low_ref, gate_ref, gate_t_ref, gated_ref, qkv_ref, e_ref, r_ref, ctx_ref,
    wqkv_all, bqkv_all, wo_all, win_all, bin_all,
    wqkv_ref, bqkv_ref, rb_ref, urow, brow, send, recv, local,
):
    places = Places()
    t = places.t
    greet([places.core, places.y, places.across, places.x])
    links = Links(send, recv)
    moves = {
        "qkv": spread(links, places, wqkv_own, wqkv_ref, 2),
        "o": spread(links, places, wo_own, wo_all, 1),
        "in": spread(links, places, win_own, win_all, 2),
    }
    small = {
        who: [
            links(rb_own, rb_ref.at[t], device),
            links(bqkv_own, bqkv_ref.at[t], device),
            links(bin_own, bin_all.at[t], device),
        ]
        for who, device in (("core", places.core), ("y", places.y), ("across", places.across))
    }
    own = [
        pltpu.make_async_copy(a, b.at[t], local.at[i])
        for i, (a, b) in enumerate(
            (
                (wqkv_own, wqkv_ref), (bqkv_own, bqkv_ref), (rb_own, rb_ref),
                (wo_own, wo_all), (win_own, win_all), (bin_own, bin_all),
            )
        )
    ]
    for copy in own[:3]:
        copy.start()
    moves["qkv"]["y"][0].start()
    moves["qkv"]["core"].start()
    for who in ("core", "y", "across"):
        small[who][0].start()
        small[who][1].start()
    moves["qkv"]["y"][1].start()
    for copy in own[3:]:
        copy.start()

    def at_step(step):
        if step == 1:
            relay(moves["qkv"], 0)
            moves["o"]["y"][0].start()
            moves["o"]["core"].start()
        if step == 2:
            relay(moves["qkv"], 1)
            moves["in"]["y"][0].start()
            moves["in"]["core"].start()
        if step == 3:
            close(moves["qkv"], 0)
            moves["qkv"]["core"].wait_recv()
            small["core"][0].wait_recv()
            small["core"][1].wait_recv()
        if step == 4:
            relay(moves["o"], 0)
            close(moves["qkv"], 1)
            moves["in"]["y"][1].start()
            for who in ("core", "y", "across"):
                small[who][2].start()
        if step == 6:
            relay(moves["in"], 0)
            close(moves["o"], 0)
            small["y"][0].wait_recv()
            small["y"][1].wait_recv()
        if step == 9:
            relay(moves["in"], 1)
            close(moves["in"], 0)
            for j in range(2):
                moves["qkv"]["near"][j].wait_recv()
                moves["qkv"]["far"][j].wait_recv()
            small["across"][0].wait_recv()
            small["across"][1].wait_recv()
        if step == 11:
            close(moves["in"], 1)

    tokens = x_ref.shape[0]
    groups = wqkv_ref.shape[0]
    inner = wqkv_ref.shape[1] // 3
    seq = e_ref.shape[1]
    seqs = tokens // seq
    heads_here = e_ref.shape[0] // (groups * seqs)
    hd = inner // heads_here
    tb = 256
    experts_rep = 40

    def norm(i, c):
        rows = pl.ds(pl.multiple_of(i * tb, tb), tb)
        x = x_ref[rows, :].astype(F32)
        n1 = (x * lax.rsqrt(jnp.mean(x * x, axis=1, keepdims=True) + EPS) * g1_ref[...]).astype(BF16)
        n1_ref[rows, :] = n1
        small = nt(wsm_ref[...], n1)
        low = small[: 3 * PAD]
        logits = small[3 * PAD :]
        valid = lax.broadcasted_iota(jnp.int32, logits.shape, 0) < experts_rep
        logits = jnp.where(valid, logits, -jnp.inf)
        ex = jnp.exp(logits - jnp.max(logits, axis=0, keepdims=True))
        gate = ex / (jnp.sum(ex, axis=0, keepdims=True) * 0.25)
        low_ref[:, rows] = low
        gate_ref[:, rows] = gate
        gate_t_ref[rows, :] = jnp.concatenate([gate, gate], axis=0).T
        for p in range(3):
            gated_ref[p * PAD : (p + 1) * PAD, rows] = (low[p * PAD : (p + 1) * PAD] * gate).astype(BF16)
        return c

    lax.fori_loop(0, tokens // tb, norm, 0)
    for copy in own[:3]:
        copy.wait()

    def keep(k, g):
        return pltpu.make_async_copy(wqkv_ref.at[g], wqkv_all.at[g], local.at[6 + k])

    maskrow = jnp.where(
        lax.broadcasted_iota(jnp.int32, (16, seq), 1) < lens[seqs - 1], 0.0, NEG
    )
    maskrow = jnp.where(lax.broadcasted_iota(jnp.int32, (16, seq), 0) == 0, maskrow, 0.0).astype(BF16)
    onerow = (lax.broadcasted_iota(jnp.int32, (16, seq), 0) == 0).astype(F32).astype(BF16)

    def head(gh, c):
        for step in (1, 2, 3, 4, 6, 9, 11):
            pl.when(gh == step)(lambda step=step: at_step(step))
        k = gh // heads_here
        h = gh % heads_here
        g = group_at(t, k)

        @pl.when(h == 0)
        def _():
            keep(k, g).start()
            u = nn(rb_ref[g], oh_ref[...])
            for i in range(heads_here):
                urow[i] = u[i : i + 1]
            proj = nt(wqkv_ref[g], n1_ref[...])
            for p in range(3):
                up = tn(bqkv_ref[g, p * PAD : (p + 1) * PAD], gated_ref[p * PAD : (p + 1) * PAD, :])
                qkv_ref[k, p] = (proj[p * inner : (p + 1) * inner] + up).astype(BF16)

        line = jnp.broadcast_to(urow[h], (128, 2 * seq))
        brow[...] = pltpu.roll(line, 0, 1, stride=1, stride_axis=0)[:, : 2 * seq - 128]
        feats = pl.ds(pl.multiple_of(h * hd, hd), hd)
        full = pl.ds(pl.multiple_of(g * inner + h * hd, hd), hd)
        for s in range(seqs):
            q = qkv_ref[k, 0, feats, s * seq : (s + 1) * seq]
            key = qkv_ref[k, 1, feats, s * seq : (s + 1) * seq]
            v = qkv_ref[k, 2, feats, s * seq : (s + 1) * seq]
            if s > 0:
                q = jnp.concatenate([q, onerow], axis=0)
                key = jnp.concatenate([key, maskrow], axis=0)
            qb = 256
            for b in range(seq // qb):
                part = slice(s * seq + b * qb, s * seq + (b + 1) * qb)
                st = tn(key, q[:, b * qb : (b + 1) * qb])
                bias = jnp.concatenate(
                    [
                        brow[:, seq - 128 - 128 * kb + b * qb : seq - 128 - 128 * kb + (b + 1) * qb]
                        for kb in range(seq // 128)
                    ],
                    axis=0,
                )
                st = st + bias
                ex = jnp.exp(st - jnp.max(st, axis=0, keepdims=True))
                recip = 1.0 / jnp.sum(ex, axis=0, keepdims=True)
                eb = ex.astype(BF16)
                e_ref[gh * seqs + s, :, b * qb : (b + 1) * qb] = eb
                r_ref[gh, :, part] = recip
                ctx_ref[full, part] = (nn(v, eb) * recip).astype(BF16)
        return c

    lax.fori_loop(0, groups * heads_here, head, 0)
    for k in range(groups):
        keep(k, group_at(t, k)).wait()
    bqkv_all[...] = bqkv_ref[...]
    for copy in own[3:]:
        copy.wait()
    for j in range(1):
        moves["o"]["near"][j].wait_recv()
        moves["o"]["far"][j].wait_recv()
    for j in range(2):
        moves["in"]["near"][j].wait_recv()
        moves["in"]["far"][j].wait_recv()
    moves["o"]["core"].wait_recv()
    moves["in"]["core"].wait_recv()
    for who in small:
        small[who][2].wait_recv()
        for copy in small[who]:
            copy.wait_send()
    for item in moves.values():
        item["core"].wait_send()
        for kind in ("y", "x", "near", "far"):
            for copy in item[kind]:
                copy.wait_send()


def feed_forward(
    x_ref, c_ref, g2_ref, ctx_ref, gate_ref, wo_ref, ao_ref, bo_ref, ain_ref, bin_ref, aout_ref, bout_ref,
    win_all, wout_own,
    y_ref, dh_ref, dctx_ref, z_ref, gao_ref, gaout_ref, gbo_ref, gbin_ref, gbout_ref, gain_ref,
    h1, n2, acc, dn2, low_o, low_in, low_out, d_low_in, gated_in, gated_in_t, dgo, dgo_t, d_low_out,
    win_ref, wout_ref, send, recv, local,
):
    places = Places()
    t = places.t
    greet([places.core, places.y, places.x])
    out = spread(Links(send, recv), places, wout_own, wout_ref, 3)
    own = pltpu.make_async_copy(wout_own, wout_ref.at[t], local.at[0])
    for j in range(3):
        out["y"][j].start()
    out["core"].start()
    own.start()

    def win_copy(k, g):
        return pltpu.make_async_copy(win_all.at[g], win_ref.at[g], local.at[1 + k])

    for k in range(4):
        win_copy(k, group_at(t, k)).start()

    def at_step(step):
        if step == 0:
            own.wait()
            relay(out, 0)
        if step == 2:
            relay(out, 1)
        if step == 4:
            relay(out, 2)
            close(out, 0)
            out["core"].wait_recv()
        if step == 6:
            close(out, 1)
        if step == 8:
            close(out, 2)
        if step == 12:
            for j in range(3):
                out["near"][j].wait_recv()
                out["far"][j].wait_recv()

    tokens = x_ref.shape[0]
    groups = win_ref.shape[0]
    tb = 256
    blocks = tokens // tb

    def rows_of(i):
        return pl.ds(pl.multiple_of(i * tb, tb), tb)

    def first(i, c):
        rows = rows_of(i)
        gate = gate_ref[rows, :PAD]
        ctx = ctx_ref[:, rows].T
        lo = nt(ctx, ao_ref[...])
        low_o[rows, :] = lo
        gated_o = (lo * gate).astype(BF16)
        hidden = x_ref[rows, :].astype(F32) + nn(ctx, wo_ref[...]) + nn(gated_o, bo_ref[...])
        h1[rows, :] = hidden
        norm = (
            hidden * lax.rsqrt(jnp.mean(hidden * hidden, axis=1, keepdims=True) + EPS) * g2_ref[...]
        ).astype(BF16)
        n2[rows, :] = norm
        li = nt(norm, ain_ref[...])
        low_in[rows, :] = li
        gi = li * gate
        gated_in[rows, :] = gi.astype(BF16)
        dlo = nt(c_ref[rows, :], bout_ref[...])
        d_low_out[rows, :] = dlo
        dg = dlo * gate
        dgo[rows, :] = dg.astype(BF16)
        both = jnp.concatenate([gi, dg], axis=1).T.astype(BF16)
        gated_in_t[:, rows] = both[:PAD]
        dgo_t[:, rows] = both[PAD:]
        return c

    lax.fori_loop(0, blocks, first, 0)

    def chunk(step, c):
        for point in (0, 2, 4, 6, 8, 12):
            pl.when(step == point)(lambda point=point: at_step(point))
        n = step // blocks
        i = step % blocks
        rows = rows_of(i)
        k = group_at(t, n)

        @pl.when(i == 0)
        def _():
            win_copy(n, k).wait()

        pre = nn(n2[rows, :], win_ref[k]) + nn(gated_in[rows, :], bin_ref[k])
        da = nt(c_ref[rows, :], wout_ref[k]) + nn(dgo[rows, :], aout_ref[k])
        sig = 1.0 / (1.0 + jnp.exp(-pre))
        active = (pre * sig).astype(BF16)
        dpre = (da * sig * (1.0 + pre * (1.0 - sig))).astype(BF16)
        part = nn(active, wout_ref[k])
        lo = nt(active, aout_ref[k])
        dn = nt(dpre, win_ref[k])
        dl = nt(dpre, bin_ref[k])
        ga = nn(dgo_t[:, rows], active)
        gb = nn(gated_in_t[:, rows], dpre)

        @pl.when(n == 0)
        def _():
            acc[rows, :] = part
            low_out[rows, :] = lo
            dn2[rows, :] = dn
            d_low_in[rows, :] = dl

        @pl.when(n > 0)
        def _():
            acc[rows, :] += part
            low_out[rows, :] += lo
            dn2[rows, :] += dn
            d_low_in[rows, :] += dl

        @pl.when(i == 0)
        def _():
            gaout_ref[k] = ga
            gbin_ref[k] = gb

        @pl.when(i > 0)
        def _():
            gaout_ref[k] += ga
            gbin_ref[k] += gb

        return c

    lax.fori_loop(0, groups * blocks, chunk, 0)

    gbout_ref[...] = jnp.zeros_like(gbout_ref)
    gbo_ref[...] = jnp.zeros_like(gbo_ref)
    gao_ref[...] = jnp.zeros_like(gao_ref)
    gain_ref[...] = jnp.zeros_like(gain_ref)

    def last(i, c):
        rows = rows_of(i)
        gate = gate_ref[rows, :PAD]
        cot = c_ref[rows, :]
        hidden = h1[rows, :]
        go = low_out[rows, :] * gate
        y_ref[rows, :] = (hidden + acc[rows, :] + nn(go.astype(BF16), bout_ref[...])).astype(BF16)
        dli = d_low_in[rows, :]
        dgi = dli * gate
        dn = dn2[rows, :] + nn(dgi.astype(BF16), ain_ref[...])
        both = jnp.concatenate([go, dgi], axis=1).T.astype(BF16)
        gbout_ref[...] += nn(both[:PAD], cot)
        gain_ref[...] += nn(both[PAD:], n2[rows, :])
        inv = lax.rsqrt(jnp.mean(hidden * hidden, axis=1, keepdims=True) + EPS)
        up = dn * g2_ref[...]
        dh = (
            cot.astype(F32)
            + inv * up
            - hidden * (inv * inv * inv) * jnp.mean(hidden * up, axis=1, keepdims=True)
        )
        dh_ref[rows, :] = dh
        da = dh.astype(BF16)
        dlo = nt(da, bo_ref[...])
        lo = low_o[rows, :]
        dg = dlo * gate
        dgb = dg.astype(BF16)
        both = jnp.concatenate([lo * gate, dg], axis=1).T.astype(BF16)
        gbo_ref[...] += nn(both[:PAD], da)
        gao_ref[...] += nt(both[PAD:], ctx_ref[:, rows])
        dctx_ref[:, rows] = (nt(wo_ref[...], da) + tn(ao_ref[...], both[PAD:])).astype(BF16)
        z = dlo * lo + dli * low_in[rows, :] + d_low_out[rows, :] * low_out[rows, :]
        z_ref[:, rows] = jnp.concatenate([z, z], axis=1).T[:PAD]
        return c

    lax.fori_loop(0, blocks, last, 0)
    out["core"].wait_send()
    for kind in ("y", "x", "near", "far"):
        for copy in out[kind]:
            copy.wait_send()


def attention_backward(
    x_ref, g1_ref, wsm_ref, wqkv_ref, bqkv_ref, n1_ref, low_ref, gate_ref, gated_ref, qkv_ref, e_ref, r_ref,
    ctx_ref, dctx_ref, z_ref, dh_ref, sum_ref,
    gx_ref, gsm_ref, gbqkv_ref,
    dqkv, dlow, dn1, dsmall,
):
    tokens = x_ref.shape[0]
    groups = wqkv_ref.shape[0]
    inner = wqkv_ref.shape[1] // 3
    seq = e_ref.shape[1]
    seqs = tokens // seq
    heads_here = e_ref.shape[0] // (groups * seqs)
    hd = inner // heads_here
    qb = 256

    t = lax.axis_index("tensor")

    def group(n, c):
        g = group_at(t, n)

        def head(h, c):
            gh = n * heads_here + h
            feats = pl.ds(pl.multiple_of(h * hd, hd), hd)
            full = pl.ds(pl.multiple_of(g * inner + h * hd, hd), hd)
            for s in range(seqs):
                cols = slice(s * seq, (s + 1) * seq)
                q = qkv_ref[n, 0, feats, cols]
                k = qkv_ref[n, 1, feats, cols]
                v = qkv_ref[n, 2, feats, cols]
                dk = jnp.zeros((hd, seq), F32)
                dv = jnp.zeros((hd, seq), F32)
                for b in range(seq // qb):
                    part = slice(s * seq + b * qb, s * seq + (b + 1) * qb)
                    do = (dctx_ref[full, part].astype(F32) * r_ref[gh, :, part]).astype(BF16)
                    delta = jnp.sum(do.astype(F32) * ctx_ref[full, part].astype(F32), axis=0, keepdims=True)
                    eb = e_ref[gh * seqs + s, :, b * qb : (b + 1) * qb]
                    dp = tn(v, do)
                    ds = (eb.astype(F32) * (dp - delta)).astype(BF16)
                    dqkv[feats, part] = nn(k, ds).astype(BF16)
                    dk = dk + nt(q[:, b * qb : (b + 1) * qb], ds)
                    dv = dv + nt(do, eb)
                dqkv[pl.ds(pl.multiple_of(inner + h * hd, hd), hd), cols] = dk.astype(BF16)
                dqkv[pl.ds(pl.multiple_of(2 * inner + h * hd, hd), hd), cols] = dv.astype(BF16)
            return c

        lax.fori_loop(0, heads_here, head, 0)
        dn = tn(wqkv_ref[g], dqkv[...])

        @pl.when(n == 0)
        def _():
            dn1[...] = dn

        @pl.when(n > 0)
        def _():
            dn1[...] += dn

        for p in range(3):
            d = dqkv[p * inner : (p + 1) * inner, :]
            dl = nn(bqkv_ref[g, p * PAD : (p + 1) * PAD], d)

            @pl.when(n == 0)
            def _():
                dlow[p * PAD : (p + 1) * PAD, :] = dl

            @pl.when(n > 0)
            def _():
                dlow[p * PAD : (p + 1) * PAD, :] += dl

            gbqkv_ref[g, p] = nt(gated_ref[p * PAD : (p + 1) * PAD, :], d)
        return c

    lax.fori_loop(0, groups, group, 0)
    gate = gate_ref[...]
    z = z_ref[...]
    for p in range(3):
        part = slice(p * PAD, (p + 1) * PAD)
        z = z + dlow[part, :] * low_ref[part, :]
        dsmall[part, :] = (dlow[part, :] * gate).astype(BF16)
    zh = z.astype(BF16)
    zl = (z - zh.astype(F32)).astype(BF16)
    dgate = nn(sum_ref[...], zh) + nn(sum_ref[...], zl)
    total = jnp.sum(gate * z, axis=0, keepdims=True)
    dlogit = gate * (dgate - total)
    row = lax.broadcasted_iota(jnp.int32, dlogit.shape, 0)
    keep = jnp.logical_and(row % 4 == 0, row < 40)
    dsmall[3 * PAD :, :] = jnp.where(keep, dlogit, 0.0).astype(BF16)
    gsm_ref[...] = nn(dsmall[...], n1_ref[...])

    tb = 256

    def finish(i, c):
        rows = pl.ds(pl.multiple_of(i * tb, tb), tb)
        dn = (dn1[:, rows] + tn(wsm_ref[...], dsmall[:, rows])).T
        x = x_ref[rows, :].astype(F32)
        inv = lax.rsqrt(jnp.mean(x * x, axis=1, keepdims=True) + EPS)
        up = dn * g1_ref[...]
        gx_ref[rows, :] = (
            dh_ref[rows, :] + inv * up - x * (inv * inv * inv) * jnp.mean(x * up, axis=1, keepdims=True)
        )
        return c

    lax.fori_loop(0, tokens // tb, finish, 0)


ANY = "any"
SEM = "semaphores"


def call(body, name, outs, scratch, args, kinds, collective=None):
    def spec(kind):
        return pl.BlockSpec(memory_space={"s": pltpu.SMEM, "v": pltpu.VMEM, "a": pl.ANY}[kind])

    extra = {} if collective is None else {"collective_id": collective, "has_side_effects": True}
    return pl.pallas_call(
        body,
        name=name,
        out_shape=[jax.ShapeDtypeStruct(o[0], o[1]) for o in outs],
        in_specs=[spec(k) for k in kinds],
        out_specs=[spec("a" if len(o) > 2 else "v") for o in outs],
        scratch_shapes=[pltpu.SemaphoreType.DMA((n[1],)) if n[0] == SEM else pltpu.VMEM(*n) for n in scratch],
        compiler_params=pltpu.CompilerParams(vmem_limit_bytes=VMEM_LIMIT, **extra),
    )(*args)


def pad_rows(a):
    width = [(0, 0)] * (a.ndim - 2) + [(0, PAD - a.shape[-2]), (0, 0)]
    return jnp.pad(a, width)


def shards(
    layer_inputs, lengths, first_gain, second_gain, router, wqkv, bias_table, wo, win, wout,
    a_in, a_o, a_out, b_qkv, b_o, b_in, b_out, cotangent,
):
    groups = lax.axis_size("tensor")
    member = lax.axis_index("tensor")
    seqs, seq, width = layer_inputs.shape
    tokens = seqs * seq
    inner = wo.shape[0]
    heads_here = bias_table.shape[1]
    heads = heads_here * groups
    hd = inner // heads_here
    hidden = win.shape[1]
    experts = router.shape[1]
    cols = a_in.shape[2]
    rank = cols // experts

    x = layer_inputs.reshape(tokens, width)
    cot = cotangent.reshape(tokens, width)
    g1 = first_gain.reshape(1, width)
    g2 = second_gain.reshape(1, width)
    at = jnp.swapaxes(a_in, 1, 2)
    rrep = jnp.repeat(router.T, rank, axis=0)
    wsm = pad_rows(jnp.concatenate([at[:3], rrep[None]], axis=0)).reshape(4 * PAD, width)
    wqkv_own = jnp.swapaxes(wqkv, 1, 2).reshape(3 * inner, width)
    bqkv_own = pad_rows(b_qkv).reshape(3 * PAD, inner)
    rb_own = jnp.pad(bias_table.T, ((0, 16 - heads_here), (0, 0)))
    bin_own = pad_rows(b_in)
    ao = pad_rows(a_o.T)
    ain = pad_rows(at[3])
    aout = pad_rows(jnp.swapaxes(a_out.T.reshape(cols, groups, hidden), 0, 1))
    bo = pad_rows(b_o)
    bout = pad_rows(b_out)
    onehot = jnp.asarray(bucket_lines(seq), BF16)

    n1, low, gate, gate_t, gated, qkv, e, r, ctx, wqkv_all, bqkv_all, wo_all, win_all, bin_all = call(
        attention_forward,
        "attention_forward",
        [
            ((tokens, width), BF16),
            ((3 * PAD, tokens), F32),
            ((PAD, tokens), F32),
            ((tokens, 2 * PAD), F32),
            ((3 * PAD, tokens), BF16),
            ((groups, 3, inner, tokens), BF16),
            ((heads * seqs, seq, seq), BF16),
            ((heads, 1, tokens), F32),
            ((groups * inner, tokens), BF16),
            ((groups, 3 * inner, width), BF16, ANY),
            ((groups, 3 * PAD, inner), BF16),
            ((groups, inner, width), BF16, ANY),
            ((groups, width, hidden), BF16, ANY),
            ((groups, PAD, hidden), BF16, ANY),
        ],
        [
            ((groups, 3 * inner, width), BF16),
            ((groups, 3 * PAD, inner), BF16),
            ((groups, 16, NB), BF16),
            ((heads_here, 1, 2 * seq), F32),
            ((128, 2 * seq - 128), F32),
            (SEM, 32),
            (SEM, 32),
            (SEM, 10),
        ],
        (lengths, x, g1, wsm, onehot, wqkv_own, bqkv_own, rb_own, wo, win, bin_own),
        "svvvvaaaaaa",
        collective=0,
    )
    wo_all = wo_all.reshape(groups * inner, width)
    y, dh, dctx, z, gao, gaout, gbo, gbin, gbout, gain = call(
        feed_forward,
        "feed_forward",
        [
            ((tokens, width), BF16),
            ((tokens, width), F32),
            ((groups * inner, tokens), BF16),
            ((PAD, tokens), F32),
            ((PAD, groups * inner), F32),
            ((groups, PAD, hidden), F32),
            ((PAD, width), F32),
            ((groups, PAD, hidden), F32),
            ((PAD, width), F32),
            ((PAD, width), F32),
        ],
        [
            ((tokens, width), F32),
            ((tokens, width), BF16),
            ((tokens, width), F32),
            ((tokens, width), F32),
            ((tokens, PAD), F32),
            ((tokens, PAD), F32),
            ((tokens, PAD), F32),
            ((tokens, PAD), F32),
            ((tokens, PAD), BF16),
            ((PAD, tokens), BF16),
            ((tokens, PAD), BF16),
            ((PAD, tokens), BF16),
            ((tokens, PAD), F32),
            ((groups, width, hidden), BF16),
            ((groups, hidden, width), BF16),
            (SEM, 16),
            (SEM, 16),
            (SEM, 5),
        ],
        (x, cot, g2, ctx, gate_t, wo_all, ao, bo, ain, bin_all, aout, bout, win_all, wout),
        "v" * 12 + "aa",
        collective=1,
    )
    c = np.arange(PAD)
    same = (c[:, None] // rank == c[None, :] // rank) & (c[None, :] < cols)
    gx, gsm, gbqkv = call(
        attention_backward,
        "attention_backward",
        [
            ((tokens, width), F32),
            ((4 * PAD, width), F32),
            ((groups, 3, PAD, inner), F32),
        ],
        [
            ((3 * inner, tokens), BF16),
            ((3 * PAD, tokens), F32),
            ((width, tokens), F32),
            ((4 * PAD, tokens), BF16),
        ],
        (x, g1, wsm, wqkv_all, bqkv_all, n1, low, gate, gated, qkv, e, r, ctx, dctx, z, dh, jnp.asarray(same, BF16)),
        "v" * 17,
    )
    g_in = jnp.concatenate([gsm.reshape(4, PAD, width)[:3, :cols], gain[None, :cols]], axis=0)
    g_router = gsm.reshape(4, PAD, width)[3, :cols:rank]
    summed = lax.psum(
        (g_router, g_in, gao[:cols], gaout[:, :cols], gbqkv[:, :, :cols], gbo[:cols], gbin[:, :cols], gbout[:cols]),
        ("dp", "tensor"),
    )
    return (
        y.reshape(layer_inputs.shape),
        gx.reshape(layer_inputs.shape),
        summed[0].T,
        jnp.swapaxes(summed[1], 1, 2),
        summed[2].T,
        jnp.swapaxes(summed[3], 0, 1).reshape(cols, groups * hidden).T,
        lax.dynamic_index_in_dim(summed[4], member, 0, keepdims=False),
        summed[5],
        lax.dynamic_index_in_dim(summed[6], member, 0, keepdims=False),
        summed[7],
    )


def solution(mesh):
    rows = P(("dp", "tensor"), None, None)
    placed = (
        rows, P(("dp", "tensor")), P(), P(), P(), P(None, None, "tensor"), P(None, "tensor"), P("tensor", None),
        P(None, "tensor"), P("tensor", None), P(), P(), P(), P(None, None, "tensor"), P(), P(None, "tensor"), P(), rows,
    )
    return jax.shard_map(
        shards,
        mesh=mesh,
        in_specs=placed,
        out_specs=(rows, rows, P(), P(), P(), P(), P(None, None, "tensor"), P(), P(None, "tensor"), P()),
        check_vma=False,
    )
```

```python
import jax
import jax.numpy as jnp
import numpy as np
from jax import lax
from jax.experimental import pallas as pl
from jax.experimental.pallas import tpu as pltpu
from jax.sharding import PartitionSpec as P

NB = 32
MAX_DIST = 128
EPS = 1e-06
NEG = -1000000000.0
F32 = jnp.float32
BF16 = jnp.bfloat16
PAD = 64
VMEM_LIMIT = 60 * 1024 * 1024


def padded(a):
    wide = jnp.concatenate([a.astype(F32), jnp.zeros((PAD - a.shape[0], a.shape[1]), F32)], axis=0)
    return wide.astype(a.dtype)


def nn(a, b):
    return lax.dot_general(a, b, (((1,), (0,)), ((), ())), preferred_element_type=F32)


def nt(a, b):
    return lax.dot_general(a, b, (((1,), (1,)), ((), ())), preferred_element_type=F32)


def tn(a, b):
    return lax.dot_general(a, b, (((0,), (0,)), ((), ())), preferred_element_type=F32)


def flip(index, bit):
    return index + (1 - 2 * ((index // bit) % 2)) * bit


def group_at(member, step):
    high = (member // 2 + step // 2) % 2
    low = (member % 2 + step % 2) % 2
    return 2 * high + low


class Links:
    def __init__(self, send, recv):
        self.send, self.recv, self.count, self.waiting = send, recv, 0, []

    def __call__(self, src, dst, device):
        n = self.count
        self.count += 1
        return pltpu.make_async_remote_copy(
            src_ref=src, dst_ref=dst, send_sem=self.send.at[n], recv_sem=self.recv.at[n],
            device_id=device, device_id_type=pl.DeviceIdType.MESH,
        )


def greet(devices):
    barrier = pltpu.get_barrier_semaphore()
    for device in devices:
        pl.semaphore_signal(barrier, inc=1, device_id=device, device_id_type=pl.DeviceIdType.MESH)
    pl.semaphore_wait(barrier, len(devices))


class Places:
    def __init__(self):
        d, t = lax.axis_index("dp"), lax.axis_index("tensor")
        self.d, self.t = d, t
        self.half = d % 2
        self.core = (d, flip(t, 1))
        self.y = (d, flip(t, 2))
        self.across = (d, flip(flip(t, 1), 2))
        self.x = (flip(d, 1), t)
        self.y_group = flip(t, 2)


def spread(links, places, own, whole, chunks):
    g, g2 = places.t, places.y_group
    total = own.shape[0]
    rows = total // 2 // chunks
    out = {"core": links(own, whole.at[g], places.core), "y": [], "x": [], "near": [], "far": []}
    for j in range(chunks):
        mine = pl.ds(pl.multiple_of(places.half * (total // 2) + j * rows, 16), rows)
        other = pl.ds(pl.multiple_of((1 - places.half) * (total // 2) + j * rows, 16), rows)
        out["y"].append(links(own.at[mine], whole.at[g, mine], places.y))
        out["x"].append(links(whole.at[g2, mine], whole.at[g2, mine], places.x))
        out["near"].append(links(whole.at[g2, mine], whole.at[g2, mine], places.core))
        out["far"].append(links(whole.at[g2, other], whole.at[g2, other], places.core))
    return out


def relay(item, j):
    item["y"][j].wait_recv()
    item["x"][j].start()
    item["near"][j].start()


def close(item, j):
    item["x"][j].wait_recv()
    item["far"][j].start()


def bucket_of(relative):
    half = NB // 2
    exact = half // 2
    distance = np.abs(relative)
    scaled = np.log(np.maximum(distance, 1) / exact) / np.log(MAX_DIST / exact) * (half - exact)
    far = np.minimum(exact + scaled.astype(np.int32), half - 1)
    return ((relative > 0) * half + np.where(distance < exact, distance, far)).astype(np.int32)


def bucket_lines(seq):
    m = np.arange(2 * seq)
    rel = seq - 128 - m
    rel = np.where(rel < -seq, rel + 2 * seq, rel)
    rel = np.clip(rel, -(seq - 1), seq - 1)
    ids = bucket_of(rel)
    return (ids[None, :] == np.arange(NB)[:, None]).astype(np.float32)


def attention_forward(
    lens, x_ref, g1_ref, at_ref, router_ref, oh_ref, bqkv_own, rb_own, bin_own, wqkv_own, wo_own, win_own,
    n1_ref, low_ref, gate_ref, gate_t_ref, gated_ref, qkv_ref, e_ref, r_ref, ctx_ref,
    wqkv_all, bqkv_ref, wo_all, win_all, bin_ref, wsm_ref,
    wqkv_ref, rb_ref, urow, brow, send, recv, local,
):
    places = Places()
    t = places.t
    for p in range(3):
        bqkv_ref[t, p * PAD : (p + 1) * PAD] = padded(bqkv_own[p])
    pick = lax.broadcasted_iota(jnp.int32, (16, rb_own.shape[0]), 0)
    pick = pick == lax.broadcasted_iota(jnp.int32, (16, rb_own.shape[0]), 1)
    rb_ref[t] = nn(pick.astype(F32).astype(BF16), rb_own[...]).astype(BF16)
    bin_ref[t] = padded(bin_own[...])
    greet([places.core, places.y, places.across, places.x])
    links = Links(send, recv)
    moves = {
        "qkv": spread(links, places, wqkv_own, wqkv_ref, 2),
        "o": spread(links, places, wo_own, wo_all, 1),
        "in": spread(links, places, win_own, win_all, 2),
    }
    small = {
        who: [
            links(rb_ref.at[t], rb_ref.at[t], device),
            links(bqkv_ref.at[t], bqkv_ref.at[t], device),
            links(bin_ref.at[t], bin_ref.at[t], device),
        ]
        for who, device in (("core", places.core), ("y", places.y), ("across", places.across))
    }
    own = [
        pltpu.make_async_copy(a, b.at[t], local.at[i])
        for i, (a, b) in enumerate(
            ((wqkv_own, wqkv_ref), (wo_own, wo_all), (win_own, win_all))
        )
    ]
    own[0].start()
    moves["qkv"]["y"][0].start()
    moves["qkv"]["core"].start()
    for who in ("core", "y", "across"):
        small[who][0].start()
        small[who][1].start()
    moves["qkv"]["y"][1].start()
    own[1].start()
    own[2].start()
    for p in range(3):
        wsm_ref[p * PAD : (p + 1) * PAD, :] = padded(at_ref[p])
    experts = router_ref.shape[0]
    spots = lax.broadcasted_iota(jnp.int32, (PAD, experts), 0) // 4
    spots = spots == lax.broadcasted_iota(jnp.int32, (PAD, experts), 1)
    wsm_ref[3 * PAD :, :] = nn(spots.astype(F32).astype(BF16), router_ref[...]).astype(BF16)

    def at_step(step):
        if step == 1:
            relay(moves["qkv"], 0)
            moves["o"]["y"][0].start()
            moves["o"]["core"].start()
        if step == 2:
            relay(moves["qkv"], 1)
            moves["in"]["y"][0].start()
            moves["in"]["core"].start()
        if step == 3:
            close(moves["qkv"], 0)
            moves["qkv"]["core"].wait_recv()
            small["core"][0].wait_recv()
            small["core"][1].wait_recv()
        if step == 4:
            relay(moves["o"], 0)
            close(moves["qkv"], 1)
            moves["in"]["y"][1].start()
            for who in ("core", "y", "across"):
                small[who][2].start()
        if step == 6:
            relay(moves["in"], 0)
            close(moves["o"], 0)
            small["y"][0].wait_recv()
            small["y"][1].wait_recv()
        if step == 9:
            relay(moves["in"], 1)
            close(moves["in"], 0)
            for j in range(2):
                moves["qkv"]["near"][j].wait_recv()
                moves["qkv"]["far"][j].wait_recv()
            small["across"][0].wait_recv()
            small["across"][1].wait_recv()
        if step == 11:
            close(moves["in"], 1)

    tokens = x_ref.shape[0]
    groups = wqkv_ref.shape[0]
    inner = wqkv_ref.shape[1] // 3
    seq = e_ref.shape[1]
    seqs = tokens // seq
    heads_here = e_ref.shape[0] // (groups * seqs)
    hd = inner // heads_here
    tb = 256
    experts_rep = 40

    def norm(i, c):
        rows = pl.ds(pl.multiple_of(i * tb, tb), tb)
        x = x_ref[rows, :].astype(F32)
        n1 = (x * lax.rsqrt(jnp.mean(x * x, axis=1, keepdims=True) + EPS) * g1_ref[...].reshape(1, x_ref.shape[1])).astype(BF16)
        n1_ref[rows, :] = n1
        small = nt(wsm_ref[...], n1)
        low = small[: 3 * PAD]
        logits = small[3 * PAD :]
        valid = lax.broadcasted_iota(jnp.int32, logits.shape, 0) < experts_rep
        logits = jnp.where(valid, logits, -jnp.inf)
        ex = jnp.exp(logits - jnp.max(logits, axis=0, keepdims=True))
        gate = ex / (jnp.sum(ex, axis=0, keepdims=True) * 0.25)
        low_ref[:, rows] = low
        gate_ref[:, rows] = gate
        gate_t_ref[rows, :] = jnp.concatenate([gate, gate], axis=0).T
        for p in range(3):
            gated_ref[p * PAD : (p + 1) * PAD, rows] = (low[p * PAD : (p + 1) * PAD] * gate).astype(BF16)
        return c

    lax.fori_loop(0, tokens // tb, norm, 0)
    own[0].wait()

    def keep(k, g):
        return pltpu.make_async_copy(wqkv_ref.at[g], wqkv_all.at[g], local.at[3 + k])

    maskrow = jnp.where(
        lax.broadcasted_iota(jnp.int32, (16, seq), 1) < lens[seqs - 1], 0.0, NEG
    )
    maskrow = jnp.where(lax.broadcasted_iota(jnp.int32, (16, seq), 0) == 0, maskrow, 0.0).astype(BF16)
    onerow = (lax.broadcasted_iota(jnp.int32, (16, seq), 0) == 0).astype(F32).astype(BF16)

    def head(gh, c):
        for step in (1, 2, 3, 4, 6, 9, 11):
            pl.when(gh == step)(lambda step=step: at_step(step))
        k = gh // heads_here
        h = gh % heads_here
        g = group_at(t, k)

        @pl.when(h == 0)
        def _():
            keep(k, g).start()
            u = nn(rb_ref[g], oh_ref[...])
            for i in range(heads_here):
                urow[i] = u[i : i + 1]
            proj = nt(wqkv_ref[g], n1_ref[...])
            for p in range(3):
                up = tn(bqkv_ref[g, p * PAD : (p + 1) * PAD], gated_ref[p * PAD : (p + 1) * PAD, :])
                qkv_ref[k, p] = (proj[p * inner : (p + 1) * inner] + up).astype(BF16)

        line = jnp.broadcast_to(urow[h], (128, 2 * seq))
        brow[...] = pltpu.roll(line, 0, 1, stride=1, stride_axis=0)[:, : 2 * seq - 128]
        feats = pl.ds(pl.multiple_of(h * hd, hd), hd)
        full = pl.ds(pl.multiple_of(g * inner + h * hd, hd), hd)
        for s in range(seqs):
            q = qkv_ref[k, 0, feats, s * seq : (s + 1) * seq]
            key = qkv_ref[k, 1, feats, s * seq : (s + 1) * seq]
            v = qkv_ref[k, 2, feats, s * seq : (s + 1) * seq]
            if s > 0:
                q = jnp.concatenate([q, onerow], axis=0)
                key = jnp.concatenate([key, maskrow], axis=0)
            qb = 256
            for b in range(seq // qb):
                part = slice(s * seq + b * qb, s * seq + (b + 1) * qb)
                st = tn(key, q[:, b * qb : (b + 1) * qb])
                bias = jnp.concatenate(
                    [
                        brow[:, seq - 128 - 128 * kb + b * qb : seq - 128 - 128 * kb + (b + 1) * qb]
                        for kb in range(seq // 128)
                    ],
                    axis=0,
                )
                st = st + bias
                ex = jnp.exp(st - jnp.max(st, axis=0, keepdims=True))
                recip = 1.0 / jnp.sum(ex, axis=0, keepdims=True)
                eb = ex.astype(BF16)
                e_ref[gh * seqs + s, :, b * qb : (b + 1) * qb] = eb
                r_ref[gh, :, part] = recip
                ctx_ref[full, part] = (nn(v, eb) * recip).astype(BF16)
        return c

    lax.fori_loop(0, groups * heads_here, head, 0)
    for k in range(groups):
        keep(k, group_at(t, k)).wait()
    own[1].wait()
    own[2].wait()
    for j in range(1):
        moves["o"]["near"][j].wait_recv()
        moves["o"]["far"][j].wait_recv()
    for j in range(2):
        moves["in"]["near"][j].wait_recv()
        moves["in"]["far"][j].wait_recv()
    moves["o"]["core"].wait_recv()
    moves["in"]["core"].wait_recv()
    for who in small:
        small[who][2].wait_recv()
        for copy in small[who]:
            copy.wait_send()
    for item in moves.values():
        item["core"].wait_send()
        for kind in ("y", "x", "near", "far"):
            for copy in item[kind]:
                copy.wait_send()


def feed_forward(
    x_ref, c_ref, g2_ref, ctx_ref, gate_ref, wo_ref, ao_raw, bo_raw, at_raw, bin_ref, aout_raw, bout_raw,
    win_all, wout_own,
    y_ref, dh_ref, dctx_ref, z_ref, part_ref,
    h1, n2, acc, dn2, low_o, low_in, low_out, d_low_in, gated_in, gated_in_t, dgo, dgo_t, d_low_out,
    win_ref, wout_ref, ao_ref, bo_ref, ain_ref, aout_ref, bout_ref, send, recv, local,
):
    places = Places()
    t = places.t
    greet([places.core, places.y, places.x])
    out = spread(Links(send, recv), places, wout_own, wout_ref, 3)
    own = pltpu.make_async_copy(wout_own, wout_ref.at[t], local.at[0])
    for j in range(3):
        out["y"][j].start()
    out["core"].start()
    own.start()

    def win_copy(k, g):
        return pltpu.make_async_copy(win_all.at[g], win_ref.at[g], local.at[1 + k])

    for k in range(4):
        win_copy(k, group_at(t, k)).start()

    def at_step(step):
        if step == 0:
            own.wait()
            relay(out, 0)
        if step == 2:
            relay(out, 1)
        if step == 4:
            relay(out, 2)
            close(out, 0)
            out["core"].wait_recv()
        if step == 6:
            close(out, 1)
        if step == 8:
            close(out, 2)
        if step == 12:
            for j in range(3):
                out["near"][j].wait_recv()
                out["far"][j].wait_recv()

    tokens = x_ref.shape[0]
    groups = win_ref.shape[0]
    tb = 256
    blocks = tokens // tb

    hidden_here = aout_ref.shape[2]
    cols = ao_raw.shape[0]
    ao_ref[...] = padded(ao_raw[...])
    bo_ref[...] = padded(bo_raw[...])
    ain_ref[...] = padded(at_raw[3])
    bout_ref[...] = padded(bout_raw[...])
    for j in range(groups):
        aout_ref[j] = padded(aout_raw[:, j * hidden_here : (j + 1) * hidden_here])
    part_ref[...] = jnp.zeros_like(part_ref)

    def rows_of(i):
        return pl.ds(pl.multiple_of(i * tb, tb), tb)

    def first(i, c):
        rows = rows_of(i)
        gate = gate_ref[rows, :PAD]
        ctx = ctx_ref[:, rows].T
        lo = nt(ctx, ao_ref[...])
        low_o[rows, :] = lo
        gated_o = (lo * gate).astype(BF16)
        hidden = x_ref[rows, :].astype(F32) + nn(ctx, wo_ref[...]) + nn(gated_o, bo_ref[...])
        h1[rows, :] = hidden
        norm = (
            hidden * lax.rsqrt(jnp.mean(hidden * hidden, axis=1, keepdims=True) + EPS) * g2_ref[...].reshape(1, x_ref.shape[1])
        ).astype(BF16)
        n2[rows, :] = norm
        li = nt(norm, ain_ref[...])
        low_in[rows, :] = li
        gi = li * gate
        gated_in[rows, :] = gi.astype(BF16)
        dlo = nt(c_ref[rows, :], bout_ref[...])
        d_low_out[rows, :] = dlo
        dg = dlo * gate
        dgo[rows, :] = dg.astype(BF16)
        both = jnp.concatenate([gi, dg], axis=1).T.astype(BF16)
        gated_in_t[:, rows] = both[:PAD]
        dgo_t[:, rows] = both[PAD:]
        return c

    lax.fori_loop(0, blocks, first, 0)

    def chunk(step, c):
        for point in (0, 2, 4, 6, 8, 12):
            pl.when(step == point)(lambda point=point: at_step(point))
        n = step // blocks
        i = step % blocks
        rows = rows_of(i)
        k = group_at(t, n)

        @pl.when(i == 0)
        def _():
            win_copy(n, k).wait()

        pre = nn(n2[rows, :], win_ref[k]) + nn(gated_in[rows, :], bin_ref[k])
        da = nt(c_ref[rows, :], wout_ref[k]) + nn(dgo[rows, :], aout_ref[k])
        sig = 1.0 / (1.0 + jnp.exp(-pre))
        active = (pre * sig).astype(BF16)
        dpre = (da * sig * (1.0 + pre * (1.0 - sig))).astype(BF16)
        part = nn(active, wout_ref[k])
        lo = nt(active, aout_ref[k])
        dn = nt(dpre, win_ref[k])
        dl = nt(dpre, bin_ref[k])
        ga = nn(dgo_t[:, rows], active)
        gb = nn(gated_in_t[:, rows], dpre)

        @pl.when(n == 0)
        def _():
            acc[rows, :] = part
            low_out[rows, :] = lo
            dn2[rows, :] = dn
            d_low_in[rows, :] = dl

        @pl.when(n > 0)
        def _():
            acc[rows, :] += part
            low_out[rows, :] += lo
            dn2[rows, :] += dn
            d_low_in[rows, :] += dl

        part_ref[k, :cols] += ga[:cols]
        part_ref[k, 2 * cols : 3 * cols] += gb[:cols]
        return c

    lax.fori_loop(0, groups * blocks, chunk, 0)

    def last(i, c):
        rows = rows_of(i)
        gate = gate_ref[rows, :PAD]
        cot = c_ref[rows, :]
        hidden = h1[rows, :]
        go = low_out[rows, :] * gate
        y_ref[rows, :] = (hidden + acc[rows, :] + nn(go.astype(BF16), bout_ref[...])).astype(BF16)
        dli = d_low_in[rows, :]
        dgi = dli * gate
        dn = dn2[rows, :] + nn(dgi.astype(BF16), ain_ref[...])
        both = jnp.concatenate([go, dgi], axis=1).T.astype(BF16)
        part_ref[2, cols : 2 * cols] += nn(both[:PAD], cot)[:cols]
        part_ref[3, cols : 2 * cols] += nn(both[PAD:], n2[rows, :])[:cols]
        inv = lax.rsqrt(jnp.mean(hidden * hidden, axis=1, keepdims=True) + EPS)
        up = dn * g2_ref[...].reshape(1, x_ref.shape[1])
        dh = (
            cot.astype(F32)
            + inv * up
            - hidden * (inv * inv * inv) * jnp.mean(hidden * up, axis=1, keepdims=True)
        )
        dh_ref[rows, :] = dh
        da = dh.astype(BF16)
        dlo = nt(da, bo_ref[...])
        lo = low_o[rows, :]
        dg = dlo * gate
        dgb = dg.astype(BF16)
        both = jnp.concatenate([lo * gate, dg], axis=1).T.astype(BF16)
        part_ref[1, cols : 2 * cols] += nn(both[:PAD], da)[:cols]
        part_ref[0, cols : 2 * cols] += nt(both[PAD:], ctx_ref[:, rows])[:cols]
        dctx_ref[:, rows] = (nt(wo_ref[...], da) + tn(ao_ref[...], both[PAD:])).astype(BF16)
        z = dlo * lo + dli * low_in[rows, :] + d_low_out[rows, :] * low_out[rows, :]
        z_ref[:, rows] = jnp.concatenate([z, z], axis=1).T[:PAD]
        return c

    lax.fori_loop(0, blocks, last, 0)
    out["core"].wait_send()
    for kind in ("y", "x", "near", "far"):
        for copy in out[kind]:
            copy.wait_send()


def attention_backward(
    x_ref, g1_ref, wsm_ref, wqkv_ref, bqkv_ref, n1_ref, low_ref, gate_ref, gated_ref, qkv_ref, e_ref, r_ref,
    ctx_ref, dctx_ref, z_ref, dh_ref, part_ref,
    gx_ref, grouter_ref, gin_ref, gao_ref, gaout_ref, gbqkv_out, gbo_ref, gbin_ref, gbout_ref,
    dqkv, dlow, dn1, dsmall, gsm_ref, gbqkv_ref,
    core_out, core_in, y_out, y_in, x_out, x_in, held, z_all, full,
    small_out, small_in, small_z, small_full, b_out, b_in, b_z, b_full, send, recv,
):
    places = Places()
    t, d, half = places.t, places.d, places.half
    zs = z_all.shape[0]
    z = d // 2
    z_peers = [((z + i) % zs, ((z + i) % zs * 2 + half, t)) for i in range(1, zs)]
    tens = [(flip(t, 1), places.core), (places.y_group, places.y), (flip(places.y_group, 1), places.across)]
    block_peers = [(half * 4 + j, dev) for j, dev in tens]
    block_peers += [((1 - half) * 4 + j, (flip(d, 1), dev[1])) for j, dev in tens]
    block_peers += [((1 - half) * 4 + t, places.x)]
    me = half * 4 + t
    greet([dev for _, dev in block_peers] + [dev for _, dev in z_peers])
    links = Links(send, recv)
    partner, y_group, far_group = flip(t, 1), places.y_group, flip(places.y_group, 1)
    rows_half = x_out.shape[0]
    mine = pl.ds(pl.multiple_of(half * rows_half, rows_half), rows_half)
    other = pl.ds(pl.multiple_of((1 - half) * rows_half, rows_half), rows_half)
    shared = 2 * gao_ref.shape[0]
    cols = gao_ref.shape[0]
    to_core = links(core_out, core_in, places.core)
    to_y = links(y_out, y_in, places.y)
    to_x = links(x_out, x_in, places.x)
    to_z = [links(z_all.at[z], z_all.at[z], dev) for _, dev in z_peers]
    all_x = links(full.at[t, mine], full.at[t, mine], places.x)
    all_y = links(full.at[t, :shared], full.at[t, :shared], places.y)
    all_core = [
        links(full.at[t, :shared], full.at[t, :shared], places.core),
        links(full.at[y_group, :shared], full.at[y_group, :shared], places.core),
    ]
    share = small_in.shape[1]
    b_share = b_in.shape[1]
    give = []
    for j, dev in block_peers:
        there = pl.ds(pl.multiple_of(j * share, 16), share)
        there_b = pl.ds(pl.multiple_of((j // 4) * b_share, 16), b_share)
        give.append(links(small_out.at[there], small_in.at[me], dev))
        give.append(links(b_out.at[j % 4, there_b], b_in.at[me], dev))
    cross = []
    for _, dev in z_peers:
        cross.append(links(small_z.at[z], small_z.at[z], dev))
        cross.append(links(b_z.at[z], b_z.at[z], dev))
    back = [links(small_full.at[me], small_full.at[me], dev) for _, dev in block_peers]
    back.append(links(b_full.at[half], b_full.at[half], places.x))

    def at_step(step):
        if step == 0:
            core_out[0] = part_ref[partner].astype(BF16)
            core_out[1] = part_ref[far_group].astype(BF16)
            to_core.start()
        if step == 1:
            to_core.wait_recv()
            y_out[...] = (part_ref[y_group] + core_in[1].astype(F32)).astype(BF16)
            to_y.start()
            held[...] = part_ref[t] + core_in[0].astype(F32)
        if step == 3:
            to_y.wait_recv()
            held[...] += y_in[...].astype(F32)
            x_out[...] = held[other, :].astype(BF16)
            to_x.start()
        if step == 5:
            to_x.wait_recv()
            z_all[z] = (held[mine, :] + x_in[...].astype(F32)).astype(BF16)
            for copy in to_z:
                copy.start()
        if step == 8:
            for copy in to_z:
                copy.wait_recv()
            total = z_all[0].astype(F32)
            for i in range(1, zs):
                total = total + z_all[i].astype(F32)
            full[t, mine] = total.astype(BF16)
            all_x.start()
        if step == 9:
            all_x.wait_recv()
            all_y.start()
            all_core[0].start()
        if step == 11:
            all_y.wait_recv()
            all_core[1].start()

    tokens = x_ref.shape[0]
    groups = wqkv_ref.shape[0]
    inner = wqkv_ref.shape[1] // 3
    seq = e_ref.shape[1]
    seqs = tokens // seq
    heads_here = e_ref.shape[0] // (groups * seqs)
    hd = inner // heads_here
    qb = 256

    def group(n, c):
        g = group_at(t, n)

        def head(h, c):
            gh = n * heads_here + h
            for point in (0, 1, 3, 5, 8, 9, 11):
                pl.when(gh == point)(lambda point=point: at_step(point))
            feats = pl.ds(pl.multiple_of(h * hd, hd), hd)
            full = pl.ds(pl.multiple_of(g * inner + h * hd, hd), hd)
            for s in range(seqs):
                cols = slice(s * seq, (s + 1) * seq)
                q = qkv_ref[n, 0, feats, cols]
                k = qkv_ref[n, 1, feats, cols]
                v = qkv_ref[n, 2, feats, cols]
                dk = jnp.zeros((hd, seq), F32)
                dv = jnp.zeros((hd, seq), F32)
                for b in range(seq // qb):
                    part = slice(s * seq + b * qb, s * seq + (b + 1) * qb)
                    do = (dctx_ref[full, part].astype(F32) * r_ref[gh, :, part]).astype(BF16)
                    delta = jnp.sum(do.astype(F32) * ctx_ref[full, part].astype(F32), axis=0, keepdims=True)
                    eb = e_ref[gh * seqs + s, :, b * qb : (b + 1) * qb]
                    dp = tn(v, do)
                    ds = (eb.astype(F32) * (dp - delta)).astype(BF16)
                    dqkv[feats, part] = nn(k, ds).astype(BF16)
                    dk = dk + nt(q[:, b * qb : (b + 1) * qb], ds)
                    dv = dv + nt(do, eb)
                dqkv[pl.ds(pl.multiple_of(inner + h * hd, hd), hd), cols] = dk.astype(BF16)
                dqkv[pl.ds(pl.multiple_of(2 * inner + h * hd, hd), hd), cols] = dv.astype(BF16)
            return c

        lax.fori_loop(0, heads_here, head, 0)
        dn = tn(wqkv_ref[g], dqkv[...])

        @pl.when(n == 0)
        def _():
            dn1[...] = dn

        @pl.when(n > 0)
        def _():
            dn1[...] += dn

        for p in range(3):
            d = dqkv[p * inner : (p + 1) * inner, :]
            dl = nn(bqkv_ref[g, p * PAD : (p + 1) * PAD], d)

            @pl.when(n == 0)
            def _():
                dlow[p * PAD : (p + 1) * PAD, :] = dl

            @pl.when(n > 0)
            def _():
                dlow[p * PAD : (p + 1) * PAD, :] += dl

            gbqkv_ref[g, p] = nt(gated_ref[p * PAD : (p + 1) * PAD, :], d)
        return c

    lax.fori_loop(0, groups, group, 0)
    gate = gate_ref[...]
    prod = z_ref[...]
    for p in range(3):
        part = slice(p * PAD, (p + 1) * PAD)
        prod = prod + dlow[part, :] * low_ref[part, :]
        dsmall[part, :] = (dlow[part, :] * gate).astype(BF16)
    high = prod.astype(BF16)
    low = (prod - high.astype(F32)).astype(BF16)
    same = lax.broadcasted_iota(jnp.int32, (PAD, PAD), 0) // 4 == lax.broadcasted_iota(jnp.int32, (PAD, PAD), 1) // 4
    same = jnp.logical_and(same, lax.broadcasted_iota(jnp.int32, (PAD, PAD), 1) < cols).astype(F32).astype(BF16)
    dgate = nn(same, high) + nn(same, low)
    total = jnp.sum(gate * prod, axis=0, keepdims=True)
    dlogit = gate * (dgate - total)
    row = lax.broadcasted_iota(jnp.int32, dlogit.shape, 0)
    keep = jnp.logical_and(row % 4 == 0, row < 40)
    dsmall[3 * PAD :, :] = jnp.where(keep, dlogit, 0.0).astype(BF16)
    gsm_ref[...] = nn(dsmall[...], n1_ref[...])
    lines = [gsm_ref[p * PAD : p * PAD + cols, :] for p in range(3)]
    lines.append(jnp.concatenate([gsm_ref[3 * PAD + 4 * e : 3 * PAD + 4 * e + 1, :] for e in range(16)], axis=0))
    count = 3 * cols + 16
    tall = -(-count // 16) * 16
    lines.append(jnp.zeros((tall - count, gsm_ref.shape[1]), F32))
    lines = jnp.concatenate(lines, axis=0).astype(BF16)
    wide = gsm_ref.shape[1] // 128
    for i in range(wide):
        small_out[i * tall : (i + 1) * tall, :] = lines[:, i * 128 : (i + 1) * 128]
    small_out[wide * tall :, :] = jnp.zeros((small_out.shape[0] - wide * tall, 128), BF16)
    for j in range(groups):
        block = [gbqkv_ref[j, p, :cols] for p in range(3)]
        block.append(jnp.zeros((b_out.shape[1] - 3 * cols, inner), F32))
        b_out[j] = jnp.concatenate(block, axis=0).astype(BF16)
    for copy in give:
        copy.start()

    tb = 256

    def finish(i, c):
        rows = pl.ds(pl.multiple_of(i * tb, tb), tb)
        dn = (dn1[:, rows] + tn(wsm_ref[...], dsmall[:, rows])).T
        x = x_ref[rows, :].astype(F32)
        inv = lax.rsqrt(jnp.mean(x * x, axis=1, keepdims=True) + EPS)
        up = dn * g1_ref[...].reshape(1, x_ref.shape[1])
        gx_ref[rows, :] = (
            dh_ref[rows, :] + inv * up - x * (inv * inv * inv) * jnp.mean(x * up, axis=1, keepdims=True)
        )
        return c

    lax.fori_loop(0, tokens // tb // 2, finish, 0)
    for copy in give:
        copy.wait_recv()
    small_in[me] = small_out[pl.ds(pl.multiple_of(me * share, 16), share), :]
    b_in[me] = b_out[t, pl.ds(pl.multiple_of(half * b_share, 16), b_share), :]
    total = small_in[0].astype(F32)
    total_b = b_in[0].astype(F32)
    for i in range(1, 8):
        total = total + small_in[i].astype(F32)
        total_b = total_b + b_in[i].astype(F32)
    small_z[z] = total.astype(BF16)
    b_z[z] = total_b.astype(BF16)
    for copy in cross:
        copy.start()
    lax.fori_loop(tokens // tb // 2, tokens // tb, finish, 0)
    for copy in cross:
        copy.wait_recv()
    total = small_z[0].astype(F32)
    total_b = b_z[0].astype(F32)
    for i in range(1, zs):
        total = total + small_z[i].astype(F32)
        total_b = total_b + b_z[i].astype(F32)
    small_full[me] = total.astype(BF16)
    b_full[half] = total_b.astype(BF16)
    for copy in back:
        copy.start()
    for copy in all_core:
        copy.wait_recv()
    gbin_ref[...] = full[t].astype(F32)[2 * cols : 3 * cols]
    hidden = gaout_ref.shape[1] // groups
    for j in range(groups):
        block = full[j].astype(F32)
        gaout_ref[:, j * hidden : (j + 1) * hidden] = block[:cols]
        target = (gao_ref, gbo_ref, gbout_ref, gin_ref.at[3])[j]
        target[...] = block[cols : 2 * cols]
    for copy in back:
        copy.wait_recv()
    flat = small_full[...].reshape(8 * share, 128)
    for i in range(wide):
        block = flat[i * tall : (i + 1) * tall].astype(F32)
        for p in range(3):
            gin_ref[p, :, i * 128 : (i + 1) * 128] = block[p * cols : (p + 1) * cols]
        grouter_ref[:, i * 128 : (i + 1) * 128] = block[3 * cols : 3 * cols + grouter_ref.shape[0]]
    block = b_full[...].reshape(2 * b_share, inner).astype(F32)
    for p in range(3):
        gbqkv_out[p] = block[p * cols : (p + 1) * cols]
    for copy in [to_core, to_y, to_x, *to_z, all_x, all_y, *all_core, *give, *cross, *back]:
        copy.wait_send()


ANY = "any"
SEM = "semaphores"


def call(body, name, outs, scratch, args, kinds, collective=None):
    def spec(kind):
        return pl.BlockSpec(memory_space={"s": pltpu.SMEM, "v": pltpu.VMEM, "a": pl.ANY}[kind])

    extra = {} if collective is None else {"collective_id": collective, "has_side_effects": True}
    return pl.pallas_call(
        body,
        name=name,
        out_shape=[jax.ShapeDtypeStruct(o[0], o[1]) for o in outs],
        in_specs=[spec(k) for k in kinds],
        out_specs=[spec("a" if len(o) > 2 else "v") for o in outs],
        scratch_shapes=[pltpu.SemaphoreType.DMA((n[1],)) if n[0] == SEM else pltpu.VMEM(*n) for n in scratch],
        compiler_params=pltpu.CompilerParams(vmem_limit_bytes=VMEM_LIMIT, **extra),
    )(*args)


def shards(
    layer_inputs, lengths, first_gain, second_gain, router, wqkv, bias_table, wo, win, wout,
    a_in, a_o, a_out, b_qkv, b_o, b_in, b_out, cotangent,
):
    groups = lax.axis_size("tensor")
    seqs, seq, width = layer_inputs.shape
    tokens = seqs * seq
    inner = wo.shape[0]
    heads_here = bias_table.shape[1]
    heads = heads_here * groups
    hd = inner // heads_here
    hidden = win.shape[1]
    experts = router.shape[1]
    cols = a_in.shape[2]

    x = layer_inputs.reshape(tokens, width)
    cot = cotangent.reshape(tokens, width)
    at = jnp.swapaxes(a_in, 1, 2)
    wqkv_own = jnp.swapaxes(wqkv, 1, 2).reshape(3 * inner, width)
    onehot = jnp.asarray(bucket_lines(seq), BF16)
    zs = lax.axis_size("dp") // 2

    n1, low, gate, gate_t, gated, qkv, e, r, ctx, wqkv_all, bqkv_all, wo_all, win_all, bin_all, wsm = call(
        attention_forward,
        "attention_forward",
        [
            ((tokens, width), BF16),
            ((3 * PAD, tokens), F32),
            ((PAD, tokens), F32),
            ((tokens, 2 * PAD), F32),
            ((3 * PAD, tokens), BF16),
            ((groups, 3, inner, tokens), BF16),
            ((heads * seqs, seq, seq), BF16),
            ((heads, 1, tokens), F32),
            ((groups * inner, tokens), BF16),
            ((groups, 3 * inner, width), BF16, ANY),
            ((groups, 3 * PAD, inner), BF16),
            ((groups, inner, width), BF16, ANY),
            ((groups, width, hidden), BF16, ANY),
            ((groups, PAD, hidden), BF16),
            ((4 * PAD, width), BF16),
        ],
        [
            ((groups, 3 * inner, width), BF16),
            ((groups, 16, NB), BF16),
            ((heads_here, 1, 2 * seq), F32),
            ((128, 2 * seq - 128), F32),
            (SEM, 32),
            (SEM, 32),
            (SEM, 7),
        ],
        (lengths, x, first_gain, at, router.T, onehot, b_qkv, bias_table.T, b_in, wqkv_own, wo, win),
        "s" + "v" * 8 + "aaa",
        collective=0,
    )
    wo_all = wo_all.reshape(groups * inner, width)
    y, dh, dctx, z, part = call(
        feed_forward,
        "feed_forward",
        [
            ((tokens, width), BF16),
            ((tokens, width), F32),
            ((groups * inner, tokens), BF16),
            ((PAD, tokens), F32),
            ((groups, 128, width), F32),
        ],
        [
            ((tokens, width), F32),
            ((tokens, width), BF16),
            ((tokens, width), F32),
            ((tokens, width), F32),
            ((tokens, PAD), F32),
            ((tokens, PAD), F32),
            ((tokens, PAD), F32),
            ((tokens, PAD), F32),
            ((tokens, PAD), BF16),
            ((PAD, tokens), BF16),
            ((tokens, PAD), BF16),
            ((PAD, tokens), BF16),
            ((tokens, PAD), F32),
            ((groups, width, hidden), BF16),
            ((groups, hidden, width), BF16),
            ((PAD, width), BF16),
            ((PAD, width), BF16),
            ((PAD, width), BF16),
            ((groups, PAD, hidden), BF16),
            ((PAD, width), BF16),
            (SEM, 16),
            (SEM, 16),
            (SEM, 5),
        ],
        (x, cot, second_gain, ctx, gate_t, wo_all, a_o.T, b_o, at, bin_all, a_out.T, b_out, win_all, wout),
        "v" * 12 + "aa",
        collective=1,
    )
    copies = 7 + 3 * (zs - 1) + 22
    outs = call(
        attention_backward,
        "attention_backward",
        [
            ((tokens, width), F32),
            ((experts, width), F32),
            ((4, cols, width), F32),
            ((cols, width), F32),
            ((cols, groups * hidden), F32),
            ((3, cols, inner), F32),
            ((cols, width), F32),
            ((cols, hidden), F32),
            ((cols, width), F32),
        ],
        [
            ((3 * inner, tokens), BF16),
            ((3 * PAD, tokens), F32),
            ((width, tokens), F32),
            ((4 * PAD, tokens), BF16),
            ((4 * PAD, width), F32),
            ((groups, 3, PAD, inner), F32),
            ((2, 128, width), BF16),
            ((2, 128, width), BF16),
            ((128, width), BF16),
            ((128, width), BF16),
            ((64, width), BF16),
            ((64, width), BF16),
            ((128, width), F32),
            ((zs, 64, width), BF16),
            ((groups, 128, width), BF16),
            ((896, 128), BF16),
            ((8, 112, 128), BF16),
            ((zs, 112, 128), BF16),
            ((8, 112, 128), BF16),
            ((groups, 128, inner), BF16),
            ((8, 64, inner), BF16),
            ((zs, 64, inner), BF16),
            ((2, 64, inner), BF16),
            (SEM, copies),
            (SEM, copies),
        ],
        (x, first_gain, wsm, wqkv_all, bqkv_all, n1, low, gate, gated, qkv, e, r, ctx, dctx, z, dh, part),
        "v" * 17,
        collective=2,
    )
    gx, g_router, g_in, g_ao, g_aout, g_bqkv, g_bo, g_bin, g_bout = outs
    return (
        y.reshape(layer_inputs.shape),
        gx.reshape(layer_inputs.shape),
        g_router.T,
        jnp.swapaxes(g_in, 1, 2),
        g_ao.T,
        g_aout.T,
        g_bqkv,
        g_bo,
        g_bin,
        g_bout,
    )


def solution(mesh):
    rows = P(("dp", "tensor"), None, None)
    placed = (
        rows, P(("dp", "tensor")), P(), P(), P(), P(None, None, "tensor"), P(None, "tensor"), P("tensor", None),
        P(None, "tensor"), P("tensor", None), P(), P(), P(), P(None, None, "tensor"), P(), P(None, "tensor"), P(), rows,
    )
    return jax.shard_map(
        shards,
        mesh=mesh,
        in_specs=placed,
        out_specs=(rows, rows, P(), P(), P(), P(), P(None, None, "tensor"), P(), P(None, "tensor"), P()),
        check_vma=False,
    )
```

```python
import jax
import jax.numpy as jnp
import numpy as np
from jax import lax
from jax.experimental import pallas as pl
from jax.experimental.pallas import tpu as pltpu
from jax.sharding import PartitionSpec as P

NB = 32
MAX_DIST = 128
EPS = 1e-06
NEG = -1000000000.0
LOG2E = 1.4426950408889634
F32 = jnp.float32
BF16 = jnp.bfloat16
PAD = 64
RANK_PAD = 48
VMEM_LIMIT = 63 * 1024 * 1024
MESH = pl.DeviceIdType.MESH


def filled(a, rows):
    wide = jnp.concatenate([a.astype(F32), jnp.zeros((rows - a.shape[0], a.shape[1]), F32)], axis=0)
    return wide.astype(a.dtype)


def nn(a, b):
    return lax.dot_general(a, b, (((1,), (0,)), ((), ())), preferred_element_type=F32)


def nt(a, b):
    return lax.dot_general(a, b, (((1,), (1,)), ((), ())), preferred_element_type=F32)


def tn(a, b):
    return lax.dot_general(a, b, (((0,), (0,)), ((), ())), preferred_element_type=F32)


def ds(start, size):
    return pl.ds(pl.multiple_of(start, 16), size)


def flip(index, bit):
    return index + (1 - 2 * ((index // bit) % 2)) * bit


def group_at(member, step):
    high = (member // 2 + step // 2) % 2
    low = (member % 2 + step % 2) % 2
    return 2 * high + low


class Links:
    def __init__(self, send, recv):
        self.send, self.recv, self.made = send, recv, []

    def __call__(self, src, dst, device):
        n = len(self.made)
        copy = pltpu.make_async_remote_copy(
            src_ref=src, dst_ref=dst, send_sem=self.send.at[n], recv_sem=self.recv.at[n],
            device_id=device, device_id_type=MESH,
        )
        self.made.append(copy)
        return copy


class Places:
    def __init__(self):
        d, t = lax.axis_index("dp"), lax.axis_index("tensor")
        self.d, self.t = d, t
        self.half = d % 2
        self.quarter = d % 4
        self.core_t, self.y_t = flip(t, 1), flip(t, 2)
        self.far_t = flip(self.core_t, 2)
        self.core = (d, self.core_t)
        self.y = (d, self.y_t)
        self.across = (d, self.far_t)
        self.x = (flip(d, 1), t)
        self.z = (flip(d, 2), t)


class Chunk:
    def __init__(self, links, places, own, whole, first, base, rows, over_x):
        part = rows // 4
        q = places.quarter
        qx, qz = flip(q, 1), flip(q, 2)
        qd = flip(qx, 2)
        g, g2 = places.t, places.y_t

        def at(group, quarter):
            return whole.at[ds(first(group) + base + quarter * part, part)]

        def pass_on(quarter, device):
            return links(at(g2, quarter), at(g2, quarter), device)

        self.y = links(own.at[ds(base + q * part, part)], at(g, q), places.y)
        self.one = [pass_on(q, places.x), pass_on(q, places.z), pass_on(q, places.core)]
        self.two = [pass_on(qz, places.x) if over_x else pass_on(qx, places.z)]
        self.two += [pass_on(qx, places.core), pass_on(qz, places.core)]
        self.three = pass_on(qd, places.core)

    def start(self):
        self.y.start()

    def relay(self):
        self.y.wait_recv()
        for copy in self.one:
            copy.start()

    def forward(self):
        self.one[0].wait_recv()
        self.one[1].wait_recv()
        for copy in self.two:
            copy.start()

    def close(self):
        self.two[0].wait_recv()
        self.three.start()

    def whole_here(self):
        for copy in (self.one[2], self.two[1], self.two[2], self.three):
            copy.wait_recv()


def bucket_of(relative):
    half = NB // 2
    exact = half // 2
    distance = np.abs(relative)
    scaled = np.log(np.maximum(distance, 1) / exact) / np.log(MAX_DIST / exact) * (half - exact)
    far = np.minimum(exact + scaled.astype(np.int32), half - 1)
    return ((relative > 0) * half + np.where(distance < exact, distance, far)).astype(np.int32)


def bucket_lines(seq):
    m = np.arange(2 * seq)
    rel = seq - 128 - m
    rel = np.where(rel < -seq, rel + 2 * seq, rel)
    rel = np.clip(rel, -(seq - 1), seq - 1)
    ids = bucket_of(rel)
    return (ids[None, :] == np.arange(NB)[:, None]).astype(np.float32)


class Names:
    def __init__(self, **refs):
        self.__dict__.update(refs)


def layer(names, sizes, *refs):
    r = Names(**dict(zip(names, refs)))
    tokens, width, seq, seqs, groups, inner, heads_here, hd, hidden, cols, experts, zs = sizes
    heads = groups * heads_here
    span = 3 * hd
    rank = cols // experts
    places = Places()
    t, d, half = places.t, places.d, places.half
    z = d // 2
    links = Links(r.send, r.recv)

    def gb_rows(g, p):
        return ds(4 * PAD + (g * 3 + p) * PAD, PAD)

    r.zed = r.low_in
    r.dsmall = r.dctx.at[: 4 * PAD]
    r.d_low = [r.low_out, r.d_low_in, r.d_low_out]
    r.core_out = [r.cot.at[:128], r.cot.at[128:256]]
    r.y_out, r.x_out, r.z_out = r.cot.at[256:384], r.cot.at[384:448], r.cot.at[448:512]
    batch = min(zs, 4)
    r.z_in = r.cot.at[512 : 512 + 64 * batch]

    local = [0]

    def here(src, dst):
        local[0] += 1
        return pltpu.make_async_copy(src, dst, r.local.at[local[0] - 1])

    get_x = here(r.x, r.xy)
    get_c = here(r.c, r.cot)
    get_qkv = [
        here(
            r.wqkv_own.at[p, h * hd : (h + 1) * hd],
            r.wqkv.at[ds(t * heads_here * span + h * span + p * hd, hd)],
        )
        for h in range(heads_here)
        for p in range(3)
    ]
    get_x.start()
    for copy in get_qkv:
        copy.start()

    z_peers = [((z + i) % zs * 2 + half, t) for i in range(1, zs)]
    same_x = [(half * 4 + j, (d, j)) for j in (places.core_t, places.y_t, places.far_t)]
    other_x = [((1 - half) * 4 + j, (flip(d, 1), j)) for j in (places.core_t, places.y_t, places.far_t, t)]
    block_peers = same_x + other_x
    barrier = pltpu.get_barrier_semaphore()
    known = [dev for _, dev in block_peers] + z_peers
    for dev in known:
        pl.semaphore_signal(barrier, inc=1, device_id=dev, device_id_type=MESH)

    def quarter_of(ref, g, rows):
        return ref.at[ds(g * rows, rows)]

    def qkv_row(g):
        return g * heads_here * span

    qkv_chunks = [
        Chunk(links, places, quarter_of(r.wqkv, t, heads_here * span), r.wqkv, qkv_row, h * span, span, h % 2 == 0)
        for h in range(heads_here)
    ]
    o_chunk = Chunk(links, places, r.wo_own, r.wo, lambda g: g * inner, 0, inner, False)
    in_chunks = [
        Chunk(links, places, r.win_own, r.win_all, lambda g: g * width, j * width // 2, width // 2, j == 0)
        for j in range(2)
    ]
    out_chunks = [
        Chunk(links, places, r.wout_own, r.wout, lambda g: g * hidden, j * hidden // 2, hidden // 2, j == 1)
        for j in range(2)
    ]

    own_qkv = quarter_of(r.wqkv, t, heads_here * span)
    core_qkv = links(own_qkv, own_qkv, places.core)
    core_o = links(r.wo_own, quarter_of(r.wo, t, inner), places.core)
    core_in = links(r.win_own, quarter_of(r.win_all, t, width), places.core)
    core_out = links(r.wout_own, quarter_of(r.wout, t, hidden), places.core)
    small = [r.bq, r.rb, r.bin]
    small_y = [links(a.at[t], a.at[t], places.y) for a in small]
    small_core = [links(a.at[t], a.at[t], places.core) for a in small]
    small_far = [links(a.at[places.y_t], a.at[places.y_t], places.core) for a in small]
    keep = [
        here(r.wo_own, quarter_of(r.wo, t, inner)),
        here(r.win_own, quarter_of(r.win_all, t, width)),
        here(r.wout_own, quarter_of(r.wout, t, hidden)),
    ]

    for p in range(3):
        r.bq[t, p * RANK_PAD : (p + 1) * RANK_PAD] = filled(r.b_qkv[p], RANK_PAD)
    pick = lax.broadcasted_iota(jnp.int32, (16, heads_here), 0)
    pick = pick == lax.broadcasted_iota(jnp.int32, (16, heads_here), 1)
    r.rb[t] = nn(pick.astype(F32).astype(BF16), r.table[...]).astype(BF16)
    r.bin[t] = filled(r.b_in[...], PAD)
    for copy in get_qkv:
        copy.wait()
    pl.semaphore_wait(barrier, len(known))
    qkv_chunks[0].start()
    core_qkv.start()
    small_core[0].start()
    small_core[1].start()
    qkv_chunks[1].start()
    small_y[0].start()
    small_y[1].start()
    qkv_chunks[2].start()
    get_c.start()
    keep[0].start()
    keep[1].start()
    for p in range(3):
        r.wsm[p * PAD : (p + 1) * PAD, :] = filled(r.at[p], PAD)
    spots = lax.broadcasted_iota(jnp.int32, (PAD, experts), 0) // rank
    spots = spots == lax.broadcasted_iota(jnp.int32, (PAD, experts), 1)
    r.wsm[3 * PAD :, :] = nn(spots.astype(F32).astype(BF16), r.router[...]).astype(BF16)
    r.ao[...] = filled(r.a_o[...], PAD)
    r.bo[...] = filled(r.b_o[...], PAD)
    r.ain[...] = filled(r.at[3], PAD)
    r.bout[...] = filled(r.b_out[...], PAD)
    for j in range(groups):
        r.aout[j] = filled(r.a_out[:, j * hidden : (j + 1) * hidden], PAD)
    g1 = r.g1[...].reshape(1, width)
    g2 = r.g2[...].reshape(1, width)

    tb = 256
    get_x.wait()

    def norm(i, c):
        rows = ds(i * tb, tb)
        x = r.xy[rows, :].astype(F32)
        n1 = (x * lax.rsqrt(jnp.mean(x * x, axis=1, keepdims=True) + EPS) * g1).astype(BF16)
        r.n1[rows, :] = n1
        lines = nt(r.wsm[...], n1)
        low = lines[: 3 * PAD]
        logits = lines[3 * PAD :]
        valid = lax.broadcasted_iota(jnp.int32, logits.shape, 0) < cols
        logits = jnp.where(valid, logits, -jnp.inf)
        ex = jnp.exp(logits - jnp.max(logits, axis=0, keepdims=True))
        gate = ex / (jnp.sum(ex, axis=0, keepdims=True) * (1.0 / rank))
        r.low[:, rows] = low
        r.gate[:, rows] = gate
        for p in range(3):
            r.gated[p * PAD : (p + 1) * PAD, rows] = (low[p * PAD : (p + 1) * PAD] * gate).astype(BF16)
        return c

    lax.fori_loop(0, tokens // tb, norm, 0)

    maskrow = jnp.where(lax.broadcasted_iota(jnp.int32, (16, seq), 1) < r.lens[seqs - 1], 0.0, NEG)
    maskrow = jnp.where(lax.broadcasted_iota(jnp.int32, (16, seq), 0) == 0, maskrow, 0.0).astype(BF16)
    onerow = (lax.broadcasted_iota(jnp.int32, (16, seq), 0) == 0).astype(F32).astype(BF16)

    def head_row(n):
        return (group_at(t, n // heads_here) * heads_here + n % heads_here) * span

    def next_group(k):
        g = group_at(t, k)
        u = nn(r.rb[g], r.onehot[...]) * LOG2E
        for h in range(heads_here):
            r.urow[k * heads_here + h] = u[h : h + 1]
            for p in range(3):
                block = r.bq[g, p * RANK_PAD : (p + 1) * RANK_PAD, h * hd : (h + 1) * hd]
                r.bh[h, p * PAD : p * PAD + RANK_PAD, :] = block

    def project(n):
        row = head_row(n)
        h = n % heads_here
        out = nt(r.wqkv[ds(row, span), :], r.n1[...])
        for p in range(3):
            up = tn(r.bh[h, p * PAD : p * PAD + RANK_PAD, :], r.gated[p * PAD : p * PAD + RANK_PAD, :])
            r.qkv[ds(row + p * hd, hd), :] = (out[p * hd : (p + 1) * hd] + up).astype(BF16)

    def spread_bias(n):
        line = jnp.broadcast_to(r.urow[n], (128, 2 * seq))
        r.brow[n % 2] = pltpu.roll(line, 0, 1, stride=1, stride_axis=0)[:, : 2 * seq - 128]

    qb = 256
    parts = seq // qb

    def score_place(i):
        return slice((i % 2) * seq, (i % 2 + 1) * seq), slice((i // 2 % 3) * qb, (i // 2 % 3 + 1) * qb)

    def attend(n):
        row = head_row(n)
        full = ds(row // 3, hd)
        blocks = [(s, b) for s in range(seqs) for b in range(parts)]
        made, tops = {}, {}

        def score(i):
            s, b = blocks[i]
            token = slice(s * seq, (s + 1) * seq)
            if b == 0:
                q = r.qkv[ds(row, hd), token]
                k = r.qkv[ds(row + hd, hd), token].astype(F32) * LOG2E
                high = k.astype(BF16)
                keys = [high, (k - high.astype(F32)).astype(BF16)]
                queries = [q, q]
                if s > 0:
                    keys.append(maskrow)
                    queries.append(onerow)
                v = jnp.concatenate([r.qkv[ds(row + 2 * hd, hd), token], onerow], axis=0)
                made[s] = jnp.concatenate(keys, axis=0), jnp.concatenate(queries, axis=0), v
            keys, queries, v = made[s]
            top = None
            rows, lanes = score_place(i)
            for kc in range(seq // 256):
                st = tn(keys[:, kc * 256 : (kc + 1) * 256], queries[:, b * qb : (b + 1) * qb])
                for kk in range(2):
                    kb = kc * 2 + kk
                    shift = seq - 128 - 128 * kb + b * qb
                    st_b = st[kk * 128 : (kk + 1) * 128] + r.brow[n % 2, :, shift : shift + qb]
                    r.acc[rows.start + kb * 128 : rows.start + (kb + 1) * 128, lanes] = st_b
                    peak = jnp.max(st_b, axis=0, keepdims=True)
                    top = peak if top is None else jnp.maximum(top, peak)
            tops[i] = top

        def soft(i):
            s, b = blocks[i]
            v = made[s][2]
            rows, lanes = score_place(i)
            token = slice(s * seq + b * qb, s * seq + (b + 1) * qb)
            for kb in range(seq // 128):
                st = r.acc[rows.start + kb * 128 : rows.start + (kb + 1) * 128, lanes]
                r.e[n * seqs + s, kb * 128 : (kb + 1) * 128, b * qb : (b + 1) * qb] = jnp.exp2(st - tops[i]).astype(
                    BF16
                )
            o = nn(v, r.e[n * seqs + s, :, b * qb : (b + 1) * qb])
            recip = 1.0 / o[hd : hd + 1]
            r.recip[n, :, token] = recip
            r.ctx[full, token] = (o[:hd] * recip).astype(BF16)

        ahead = 3
        for i in range(ahead):
            score(i)
        for i in range(len(blocks)):
            if i + ahead < len(blocks):
                score(i + ahead)
            soft(i)

    def forward_step(step):
        if step == 1:
            qkv_chunks[0].relay()
        if step == 2:
            core_qkv.wait_recv()
            small_core[0].wait_recv()
            small_core[1].wait_recv()
            o_chunk.start()
            core_o.start()
        if step == 3:
            qkv_chunks[0].forward()
            qkv_chunks[1].relay()
            small_y[0].wait_recv()
            small_y[1].wait_recv()
            small_far[0].start()
            small_far[1].start()
        if step == 4:
            in_chunks[0].start()
            core_in.start()
            qkv_chunks[2].relay()
        if step == 5:
            qkv_chunks[0].close()
            qkv_chunks[1].forward()
        if step == 6:
            qkv_chunks[1].close()
            qkv_chunks[2].forward()
        if step == 7:
            qkv_chunks[2].close()
            o_chunk.relay()
            in_chunks[1].start()
        if step == 8:
            small_far[0].wait_recv()
            small_far[1].wait_recv()
            for chunk in qkv_chunks:
                chunk.whole_here()
        if step == 9:
            in_chunks[0].relay()
            o_chunk.forward()
            out_chunks[0].start()
            core_out.start()
            keep[2].start()
            small_y[2].start()
            small_core[2].start()
        if step == 11:
            in_chunks[1].relay()
            o_chunk.close()
            out_chunks[1].start()

    next_group(0)
    project(0)
    spread_bias(0)

    def forward_head(n, c):
        for step in (1, 2, 3, 4, 5, 6, 7, 8, 9, 11):
            pl.when(n == step)(lambda step=step: forward_step(step))
        last = heads - 1
        follow = jnp.minimum(n + 1, last)

        @pl.when(jnp.logical_and((n + 1) % heads_here == 0, n < last))
        def _():
            next_group((n + 1) // heads_here)

        attend(n)
        project(follow)
        spread_bias(follow)
        return c

    lax.fori_loop(0, heads, forward_head, 0)

    core_o.wait_recv()
    keep[0].wait()
    o_chunk.whole_here()
    get_c.wait()
    keep[1].wait()
    win_first = here(quarter_of(r.win_all, t, width), r.win.at[0])
    win_first.start()

    def first(i, c):
        for j in range(2):
            rows = ds((2 * i + j) * tb, tb)
            gate = r.gate[:, rows]
            ctx = r.ctx[:, rows]
            low = nn(r.ao[...], ctx)
            r.low_o[:, rows] = low
            gated = (low * gate).astype(BF16)
            h1 = r.xy[rows, :].astype(F32) + tn(ctx, r.wo[...]) + tn(gated, r.bo[...])
            r.h1[rows, :] = h1
            n2 = (h1 * lax.rsqrt(jnp.mean(h1 * h1, axis=1, keepdims=True) + EPS) * g2).astype(BF16)
            r.n2[rows, :] = n2
            low = nt(r.ain[...], n2)
            r.low_in[:, rows] = low
            r.gin[:, rows] = (low * gate).astype(BF16)
            low = nt(r.bout[...], r.cot[rows, :])
            r.d_low_out[:, rows] = low
            r.dgo[:, rows] = (low * gate).astype(BF16)
        return c

    lax.fori_loop(0, tokens // tb // 2, first, 0)
    r.acc[...] = jnp.zeros_like(r.acc)
    r.dn2[...] = jnp.zeros_like(r.dn2)
    r.low_out[...] = jnp.zeros_like(r.low_out)
    r.d_low_in[...] = jnp.zeros_like(r.d_low_in)
    r.part[...] = jnp.zeros_like(r.part)

    wide = 512
    blocks = tokens // wide
    win_next = [here(quarter_of(r.win_all, group_at(t, k), width), r.win.at[k % 2]) for k in range(1, groups)]

    def feed_step(step):
        if step == 0:
            keep[2].wait()
            out_chunks[0].relay()
            in_chunks[0].forward()
            win_first.wait()
        if step == 1:
            in_chunks[1].forward()
            out_chunks[1].relay()
            small_y[2].wait_recv()
            small_far[2].start()
            core_in.wait_recv()
            win_next[0].start()
        if step == 2:
            in_chunks[0].close()
            out_chunks[0].forward()
            core_out.wait_recv()
            small_core[2].wait_recv()
            win_next[0].wait()
        if step == 3:
            in_chunks[1].close()
            out_chunks[1].forward()
            win_next[1].start()
        if step == 4:
            out_chunks[0].close()
            out_chunks[1].close()
            win_next[1].wait()
        if step == 5:
            for chunk in in_chunks:
                chunk.whole_here()
            small_far[2].wait_recv()
            win_next[2].start()
        if step == 6:
            for chunk in out_chunks:
                chunk.whole_here()
            win_next[2].wait()

    active, d_pre = r.xy.at[:wide], r.xy.at[wide : 2 * wide]
    third = hidden // 3

    def chunk(step, c):
        for point in range(7):
            pl.when(step == point)(lambda point=point: feed_step(point))
        n = step // blocks
        rows = ds((step % blocks) * wide, wide)
        g = group_at(t, n)
        slot = n % 2
        gin, dgo = r.gin[:, rows], r.dgo[:, rows]
        for j in range(3):
            cs = slice(j * third, (j + 1) * third)
            pre = nn(r.n2[rows, :], r.win[slot, :, cs]) + tn(gin, r.bin[g, :, cs])
            da = nt(r.cot[rows, :], r.wout[ds(g * hidden + j * third, third), :]) + tn(dgo, r.aout[g, :, cs])
            sig = 1.0 / (1.0 + jnp.exp(-pre))
            act = pre * sig
            active[:, cs] = act.astype(BF16)
            d_pre[:, cs] = (da * (sig + act * (1.0 - sig))).astype(BF16)
        r.acc[rows, :] += nn(active[...], r.wout[ds(g * hidden, hidden), :])
        r.dn2[rows, :] += nt(d_pre[...], r.win[slot])
        r.low_out[:, rows] += nt(r.aout[g], active[...])
        r.d_low_in[:, rows] += nt(r.bin[g], d_pre[...])
        r.part[g, :cols] += nn(dgo, active[...])[:cols]
        r.part[g, 2 * cols : 3 * cols] += nn(gin, d_pre[...])[:cols]
        return c

    lax.fori_loop(0, groups * blocks, chunk, 0)

    def last(i, c):
        for j in range(2):
            rows = ds((2 * i + j) * tb, tb)
            gate = r.gate[:, rows]
            cot, n2, ctx, h1 = r.cot[rows, :], r.n2[rows, :], r.ctx[:, rows], r.h1[rows, :]
            low_out, d_low_in = r.low_out[:, rows], r.d_low_in[:, rows]
            go = (low_out * gate).astype(BF16)
            r.xy[rows, :] = (h1 + r.acc[rows, :] + tn(go, r.bout[...])).astype(BF16)
            dgi = (d_low_in * gate).astype(BF16)
            up = (r.dn2[rows, :] + tn(dgi, r.ain[...])) * g2
            r.part[2, cols : 2 * cols] += nn(go, cot)[:cols]
            r.part[3, cols : 2 * cols] += nn(dgi, n2)[:cols]
            inv = lax.rsqrt(jnp.mean(h1 * h1, axis=1, keepdims=True) + EPS)
            dh = cot.astype(F32) + inv * up - h1 * (inv * inv * inv * jnp.mean(h1 * up, axis=1, keepdims=True))
            r.h1[rows, :] = dh
            da = dh.astype(BF16)
            d_low = nt(r.bo[...], da)
            low = r.low_o[:, rows]
            dgo = (d_low * gate).astype(BF16)
            r.part[1, cols : 2 * cols] += nn((low * gate).astype(BF16), da)[:cols]
            r.part[0, cols : 2 * cols] += nt(dgo, ctx)[:cols]
            r.dctx[:, rows] = (nt(r.wo[...], da) + tn(r.ao[...], dgo)).astype(BF16)
            r.zed[:, rows] = d_low * low + d_low_in * r.low_in[:, rows] + r.d_low_out[:, rows] * low_out
        return c

    lax.fori_loop(0, tokens // tb // 2, last, 0)
    put_y = here(r.xy, r.y)
    put_y.start()

    rows_half = 64
    mine, other = ds(half * rows_half, rows_half), ds((1 - half) * rows_half, rows_half)
    shared = 2 * cols
    to_core = links(r.cot.at[:256], r.core_in, places.core)
    to_y = links(r.y_out, r.y_in, places.y)
    to_x = links(r.x_out, r.x_in, places.x)
    to_z = [links(r.z_out, r.z_all.at[ds(z * 64, 64)], dev) for dev in z_peers]
    keep_z = here(r.z_out, r.z_all.at[ds(z * 64, 64)])
    get_z = [here(r.z_all.at[i * 64 : (i + batch) * 64], r.z_in) for i in range(0, zs, batch)]
    all_x = links(r.full.at[t, mine], r.full.at[t, mine], places.x)
    all_y = links(r.full.at[t, :shared], r.full.at[t, :shared], places.y)
    all_core = [
        links(r.full.at[j, :shared], r.full.at[j, :shared], places.core) for j in (t, places.y_t)
    ]
    share = r.small_in.shape[1]
    b_share = r.b_in_sum.shape[1]
    me = half * 4 + t
    give = []
    for j, dev in block_peers:
        give.append(links(r.small_out.at[ds(j * share, share)], r.small_in.at[me], dev))
        give.append(links(r.b_all.at[j % 4, ds(j // 4 * b_share, b_share)], r.b_in_sum.at[me], dev))
    cross = []
    for dev in z_peers:
        cross.append(links(r.small_z.at[z], r.small_z.at[z], dev))
        cross.append(links(r.b_z.at[z], r.b_z.at[z], dev))
    back = [links(r.small_full.at[me], r.small_full.at[me], dev) for _, dev in block_peers]
    back.append(links(r.b_full.at[half], r.b_full.at[half], places.x))

    def sum_step(step):
        if step == 0:
            r.core_out[0][...] = r.part[places.core_t].astype(BF16)
            r.core_out[1][...] = r.part[places.far_t].astype(BF16)
            to_core.start()
        if step == 2:
            to_core.wait_recv()
            r.y_out[...] = (r.part[places.y_t] + r.core_in[128:].astype(F32)).astype(BF16)
            to_y.start()
            r.part[t] += r.core_in[:128].astype(F32)
            put_y.wait()
            get_x_again.start()
        if step == 5:
            to_y.wait_recv()
            r.part[t] += r.y_in[...].astype(F32)
            r.x_out[...] = r.part[t, other, :].astype(BF16)
            to_x.start()
        if step == 7:
            to_x.wait_recv()
            r.z_out[...] = (r.part[t, mine, :] + r.x_in[...].astype(F32)).astype(BF16)
            keep_z.start()
            for copy in to_z:
                copy.start()

    def sum_z():
        for copy in to_z:
            copy.wait_recv()
        keep_z.wait()
        total = None
        for copy in get_z:
            copy.start()
            copy.wait()
            for i in range(batch):
                term = r.z_in[i * 64 : (i + 1) * 64].astype(F32)
                total = term if total is None else total + term
        r.full[t, mine] = total.astype(BF16)
        all_x.start()

    get_x_again = here(r.x, r.xy)

    def attend_back(n):
        row = head_row(n)
        full = ds(row // 3, hd)
        blocks = [(s, b) for s in range(seqs) for b in range(parts)]
        sent, sums = {}, {}

        def ds_place(i):
            return slice((i % 2) * seq, (i % 2 + 1) * seq), slice((i // 2 % 3) * qb, (i // 2 % 3 + 1) * qb)

        def score(i):
            s, b = blocks[i]
            token = slice(s * seq + b * qb, s * seq + (b + 1) * qb)
            do = (r.dctx[full, token].astype(F32) * r.recip[n, :, token]).astype(BF16)
            delta = jnp.sum(do.astype(F32) * r.ctx[full, token].astype(F32), axis=0, keepdims=True)
            sent[i] = do
            v = r.qkv[ds(row + 2 * hd, hd), s * seq : (s + 1) * seq]
            rows, lanes = ds_place(i)
            for kc in range(seq // 256):
                keys = slice(kc * 256, (kc + 1) * 256)
                dp = tn(v[:, keys], do)
                e = r.e[n * seqs + s, keys, b * qb : (b + 1) * qb].astype(F32)
                r.n2[rows.start + kc * 256 : rows.start + (kc + 1) * 256, lanes] = (e * (dp - delta)).astype(BF16)

        def grads(i):
            s, b = blocks[i]
            token = slice(s * seq + b * qb, s * seq + (b + 1) * qb)
            whole = slice(s * seq, (s + 1) * seq)
            k = r.qkv[ds(row + hd, hd), whole]
            q = r.qkv[ds(row, hd), token]
            rows, lanes = ds_place(i)
            dsc = r.n2[rows, lanes]
            dk = nt(q, dsc)
            dv = nt(sent[i], r.e[n * seqs + s, :, b * qb : (b + 1) * qb])
            r.qkv[ds(row, hd), token] = nn(k, dsc).astype(BF16)
            if b > 0:
                dk, dv = sums[s][0] + dk, sums[s][1] + dv
            sums[s] = dk, dv
            if b == parts - 1:
                r.qkv[ds(row + hd, hd), whole] = dk.astype(BF16)
                r.qkv[ds(row + 2 * hd, hd), whole] = dv.astype(BF16)

        ahead = 2
        for i in range(ahead):
            score(i)
        for i in range(len(blocks)):
            if i + ahead < len(blocks):
                score(i + ahead)
            grads(i)

    def backward_head(n, c):
        for step in (0, 2, 5, 7):
            pl.when(n == step)(lambda step=step: sum_step(step))
        attend_back(n)
        return c

    lax.fori_loop(0, heads, backward_head, 0)
    sum_z()

    gsm = r.acc.at[: 4 * PAD]

    def adapters(g, c):
        for p in range(3):
            dp = [
                r.qkv[ds((g * heads_here + h) * span + p * hd, hd), :] for h in range(heads_here)
            ]
            dp = jnp.concatenate(dp, axis=0)
            low = nn(r.bq[g, p * RANK_PAD : (p + 1) * RANK_PAD], dp)
            r.d_low[p][:RANK_PAD, :] += low
            r.acc[gb_rows(g, p), :inner] = nt(r.gated[p * PAD : (p + 1) * PAD, :], dp)
        return c

    for p in range(3):
        r.d_low[p][...] = jnp.zeros(r.d_low[p].shape, F32)
    lax.fori_loop(0, groups, adapters, 0)
    gate = r.gate[...]
    prod = r.zed[...]
    for p in range(3):
        part = slice(p * PAD, (p + 1) * PAD)
        prod = prod + r.d_low[p][...] * r.low[part, :]
        r.dsmall[part, :] = (r.d_low[p][...] * gate).astype(BF16)
    high = prod.astype(BF16)
    low = (prod - high.astype(F32)).astype(BF16)
    same = lax.broadcasted_iota(jnp.int32, (PAD, PAD), 0) // rank
    same = same == lax.broadcasted_iota(jnp.int32, (PAD, PAD), 1) // rank
    same = jnp.logical_and(same, lax.broadcasted_iota(jnp.int32, (PAD, PAD), 1) < cols).astype(F32).astype(BF16)
    d_gate = nn(same, high) + nn(same, low)
    d_logit = gate * (d_gate - jnp.sum(gate * prod, axis=0, keepdims=True))
    row = lax.broadcasted_iota(jnp.int32, d_logit.shape, 0)
    chosen = jnp.logical_and(row % rank == 0, row < cols)
    r.dsmall[3 * PAD :, :] = jnp.where(chosen, d_logit, 0.0).astype(BF16)
    gsm[...] = nn(r.dsmall[...], r.n1[...])
    lines = [gsm[p * PAD : p * PAD + cols, :] for p in range(3)]
    lines.append(jnp.concatenate([gsm[3 * PAD + rank * e : 3 * PAD + rank * e + 1, :] for e in range(16)], axis=0))
    count = 3 * cols + 16
    tall = -(-count // 16) * 16
    lines.append(jnp.zeros((tall - count, width), F32))
    lines = jnp.concatenate(lines, axis=0).astype(BF16)
    strips = width // 128
    for i in range(strips):
        r.small_out[i * tall : (i + 1) * tall, :] = lines[:, i * 128 : (i + 1) * 128]
    r.small_out[strips * tall :, :] = jnp.zeros((r.small_out.shape[0] - strips * tall, 128), BF16)
    for j in range(groups):
        block = [r.acc[gb_rows(j, p), :inner][:cols] for p in range(3)]
        block.append(jnp.zeros((r.b_all.shape[1] - 3 * cols, inner), F32))
        r.b_all[j] = jnp.concatenate(block, axis=0).astype(BF16)
    for copy in give:
        copy.start()
    all_x.wait_recv()
    all_y.start()
    all_core[0].start()
    get_x_again.wait()

    def finish(i, c):
        rows = ds(i * tb, tb)
        dn = tn(r.qkv[:, rows], r.wqkv[...]) + tn(r.dsmall[:, rows], r.wsm[...])
        x = r.xy[rows, :].astype(F32)
        inv = lax.rsqrt(jnp.mean(x * x, axis=1, keepdims=True) + EPS)
        up = dn * g1
        r.h1[rows, :] += inv * up - x * (inv * inv * inv * jnp.mean(x * up, axis=1, keepdims=True))
        return c

    part_rows = tokens // 2
    put_x = [here(r.h1.at[i * part_rows : (i + 1) * part_rows], r.gx.at[i * part_rows : (i + 1) * part_rows]) for i in range(2)]
    lax.fori_loop(0, tokens // tb // 2, finish, 0)
    put_x[0].start()
    all_y.wait_recv()
    all_core[1].start()
    for copy in give:
        copy.wait_recv()
    r.small_in[me] = r.small_out[ds(me * share, share), :]
    r.b_in_sum[me] = r.b_all[t, ds(half * b_share, b_share), :]
    total = r.small_in[0].astype(F32)
    total_b = r.b_in_sum[0].astype(F32)
    for i in range(1, 8):
        total = total + r.small_in[i].astype(F32)
        total_b = total_b + r.b_in_sum[i].astype(F32)
    r.small_z[z] = total.astype(BF16)
    r.b_z[z] = total_b.astype(BF16)
    for copy in cross:
        copy.start()
    lax.fori_loop(tokens // tb // 2, tokens // tb, finish, 0)
    put_x[1].start()
    for copy in cross:
        copy.wait_recv()
    total = r.small_z[0].astype(F32)
    total_b = r.b_z[0].astype(F32)
    for i in range(1, zs):
        total = total + r.small_z[i].astype(F32)
        total_b = total_b + r.b_z[i].astype(F32)
    r.small_full[me] = total.astype(BF16)
    r.b_full[half] = total_b.astype(BF16)
    for copy in back:
        copy.start()
    for copy in all_core:
        copy.wait_recv()
    r.g_b_in[...] = r.full[t].astype(F32)[2 * cols : 3 * cols]
    for j in range(groups):
        block = r.full[j].astype(F32)
        r.g_a_out[:, j * hidden : (j + 1) * hidden] = block[:cols]
        target = (r.g_a_o, r.g_b_o, r.g_b_out, r.g_a_in.at[3])[j]
        target[...] = block[cols : 2 * cols]
    for copy in back:
        copy.wait_recv()
    flat = r.small_full[...].reshape(8 * share, 128)
    for i in range(strips):
        block = flat[i * tall : (i + 1) * tall].astype(F32)
        lanes = slice(i * 128, (i + 1) * 128)
        for p in range(3):
            r.g_a_in[p, :, lanes] = block[p * cols : (p + 1) * cols]
        r.g_router[:, lanes] = block[3 * cols : 3 * cols + experts]
    block = r.b_full[...].reshape(2 * b_share, inner).astype(F32)
    for p in range(3):
        r.g_b_qkv[p] = block[p * cols : (p + 1) * cols]
    for copy in put_x:
        copy.wait()
    for copy in links.made:
        copy.wait_send()


def shards(
    layer_inputs, lengths, first_gain, second_gain, router, wqkv, bias_table, wo, win, wout,
    a_in, a_o, a_out, b_qkv, b_o, b_in, b_out, cotangent,
):
    groups = lax.axis_size("tensor")
    zs = lax.axis_size("dp") // 2
    seqs, seq, width = layer_inputs.shape
    tokens = seqs * seq
    inner = wo.shape[0]
    heads_here = bias_table.shape[1]
    heads = heads_here * groups
    hd = inner // heads_here
    hidden = win.shape[1]
    experts = router.shape[1]
    cols = a_in.shape[2]
    sizes = (tokens, width, seq, seqs, groups, inner, heads_here, hd, hidden, cols, experts, zs)
    ins = {
        "lens": (lengths, pltpu.SMEM),
        "g1": (first_gain, pltpu.VMEM),
        "g2": (second_gain, pltpu.VMEM),
        "at": (jnp.swapaxes(a_in, 1, 2), pltpu.VMEM),
        "router": (router.T, pltpu.VMEM),
        "onehot": (jnp.asarray(bucket_lines(seq), BF16), pltpu.VMEM),
        "b_qkv": (b_qkv, pltpu.VMEM),
        "table": (bias_table.T, pltpu.VMEM),
        "b_in": (b_in, pltpu.VMEM),
        "a_o": (a_o.T, pltpu.VMEM),
        "b_o": (b_o, pltpu.VMEM),
        "a_out": (a_out.T, pltpu.VMEM),
        "b_out": (b_out, pltpu.VMEM),
        "x": (layer_inputs.reshape(tokens, width), pl.ANY),
        "c": (cotangent.reshape(tokens, width), pl.ANY),
        "wqkv_own": (jnp.swapaxes(wqkv, 1, 2), pl.ANY),
        "wo_own": (wo, pl.ANY),
        "win_own": (win, pl.ANY),
        "wout_own": (wout, pl.ANY),
    }
    outs = {
        "y": ((tokens, width), BF16, pl.ANY),
        "gx": ((tokens, width), F32, pl.ANY),
        "g_router": ((experts, width), F32, pltpu.VMEM),
        "g_a_in": ((4, cols, width), F32, pltpu.VMEM),
        "g_a_o": ((cols, width), F32, pltpu.VMEM),
        "g_a_out": ((cols, groups * hidden), F32, pltpu.VMEM),
        "g_b_qkv": ((3, cols, inner), F32, pltpu.VMEM),
        "g_b_o": ((cols, width), F32, pltpu.VMEM),
        "g_b_in": ((cols, hidden), F32, pltpu.VMEM),
        "g_b_out": ((cols, width), F32, pltpu.VMEM),
        "win_all": ((groups * width, hidden), BF16, pl.ANY),
        "z_all": ((zs * 64, width), BF16, pl.ANY),
    }
    line = (PAD, tokens)
    scratch = {
        "xy": ((tokens, width), BF16),
        "cot": ((tokens, width), BF16),
        "n1": ((tokens, width), BF16),
        "low": ((3 * PAD, tokens), F32),
        "gate": (line, F32),
        "gated": ((3 * PAD, tokens), BF16),
        "wqkv": ((3 * groups * inner, width), BF16),
        "qkv": ((3 * groups * inner, tokens), BF16),
        "e": ((heads * seqs, seq, seq), BF16),
        "recip": ((heads, 1, tokens), F32),
        "ctx": ((groups * inner, tokens), BF16),
        "wsm": ((4 * PAD, width), BF16),
        "bq": ((groups, 3 * RANK_PAD, inner), BF16),
        "bh": ((heads_here, 3 * PAD, hd), BF16),
        "rb": ((groups, 16, NB), BF16),
        "bin": ((groups, PAD, hidden), BF16),
        "urow": ((heads, 1, 2 * seq), F32),
        "brow": ((2, 128, 2 * seq - 128), F32),
        "wo": ((groups * inner, width), BF16),
        "win": ((2, width, hidden), BF16),
        "wout": ((groups * hidden, width), BF16),
        "h1": ((tokens, width), F32),
        "n2": ((tokens, width), BF16),
        "acc": ((tokens, width), F32),
        "dn2": ((tokens, width), F32),
        "gin": (line, BF16),
        "dgo": (line, BF16),
        "low_o": (line, F32),
        "low_in": (line, F32),
        "low_out": (line, F32),
        "d_low_in": (line, F32),
        "d_low_out": (line, F32),
        "dctx": ((groups * inner, tokens), BF16),
        "part": ((groups, 128, width), F32),
        "ao": ((PAD, width), BF16),
        "bo": ((PAD, width), BF16),
        "ain": ((PAD, width), BF16),
        "bout": ((PAD, width), BF16),
        "aout": ((groups, PAD, hidden), BF16),
        "core_in": ((256, width), BF16),
        "y_in": ((128, width), BF16),
        "x_in": ((64, width), BF16),
        "full": ((groups, 128, width), BF16),
        "small_out": ((896, 128), BF16),
        "small_in": ((8, 112, 128), BF16),
        "small_z": ((zs, 112, 128), BF16),
        "small_full": ((8, 112, 128), BF16),
        "b_all": ((groups, 128, inner), BF16),
        "b_in_sum": ((8, 64, inner), BF16),
        "b_z": ((zs, 64, inner), BF16),
        "b_full": ((2, 64, inner), BF16),
    }
    copies = 9 * 8 + 40 + 3 * zs
    shapes = [pltpu.VMEM(*v) for v in scratch.values()]
    shapes += [pltpu.SemaphoreType.DMA((copies,)), pltpu.SemaphoreType.DMA((copies,)), pltpu.SemaphoreType.DMA((40,))]
    names = list(ins) + list(outs) + list(scratch) + ["send", "recv", "local"]
    flops = 2 * tokens * (8 * width * hidden * groups + 24 * width * width)
    results = pl.pallas_call(
        lambda *refs: layer(names, sizes, *refs),
        name="encoder_layer",
        out_shape=[jax.ShapeDtypeStruct(o[0], o[1]) for o in outs.values()],
        in_specs=[pl.BlockSpec(memory_space=i[1]) for i in ins.values()],
        out_specs=[pl.BlockSpec(memory_space=o[2]) for o in outs.values()],
        scratch_shapes=shapes,
        cost_estimate=pl.CostEstimate(flops=flops, bytes_accessed=30 * 2**20, transcendentals=0),
        compiler_params=pltpu.CompilerParams(
            vmem_limit_bytes=VMEM_LIMIT, collective_id=0, has_side_effects=True
        ),
    )(*[i[0] for i in ins.values()])
    y, gx, g_router, g_in, g_ao, g_aout, g_bqkv, g_bo, g_bin, g_bout = results[:10]
    return (
        y.reshape(layer_inputs.shape),
        gx.reshape(layer_inputs.shape),
        g_router.T,
        jnp.swapaxes(g_in, 1, 2),
        g_ao.T,
        g_aout.T,
        g_bqkv,
        g_bo,
        g_bin,
        g_bout,
    )


def solution(mesh):
    rows = P(("dp", "tensor"), None, None)
    placed = (
        rows, P(("dp", "tensor")), P(), P(), P(), P(None, None, "tensor"), P(None, "tensor"), P("tensor", None),
        P(None, "tensor"), P("tensor", None), P(), P(), P(), P(None, None, "tensor"), P(), P(None, "tensor"), P(), rows,
    )
    return jax.shard_map(
        shards,
        mesh=mesh,
        in_specs=placed,
        out_specs=(rows, rows, P(), P(), P(), P(), P(None, None, "tensor"), P(), P(None, "tensor"), P()),
        check_vma=False,
    )
```

```python
import jax
import jax.numpy as jnp
import numpy as np
from jax import lax
from jax.experimental import pallas as pl
from jax.experimental.pallas import tpu as pltpu
from jax.sharding import PartitionSpec as P

NB = 32
MAX_DIST = 128
EPS = 1e-06
NEG = -1000000000.0
LOG2E = 1.4426950408889634
F32 = jnp.float32
BF16 = jnp.bfloat16
PAD = 64
RANK_PAD = 48
VMEM_LIMIT = 63 * 1024 * 1024
MESH = pl.DeviceIdType.MESH


def filled(a, rows):
    wide = jnp.concatenate([a.astype(F32), jnp.zeros((rows - a.shape[0], a.shape[1]), F32)], axis=0)
    return wide.astype(a.dtype)


def nn(a, b):
    return lax.dot_general(a, b, (((1,), (0,)), ((), ())), preferred_element_type=F32)


def nt(a, b):
    return lax.dot_general(a, b, (((1,), (1,)), ((), ())), preferred_element_type=F32)


def tn(a, b):
    return lax.dot_general(a, b, (((0,), (0,)), ((), ())), preferred_element_type=F32)


def ds(start, size):
    return pl.ds(pl.multiple_of(start, 16), size)


def flip(index, bit):
    return index + (1 - 2 * ((index // bit) % 2)) * bit


def group_at(member, step):
    high = (member // 2 + step // 2) % 2
    low = (member % 2 + step % 2) % 2
    return 2 * high + low


class Links:
    def __init__(self, send, recv):
        self.send, self.recv, self.made = send, recv, []

    def __call__(self, src, dst, device):
        n = len(self.made)
        copy = pltpu.make_async_remote_copy(
            src_ref=src, dst_ref=dst, send_sem=self.send.at[n], recv_sem=self.recv.at[n],
            device_id=device, device_id_type=MESH,
        )
        self.made.append(copy)
        return copy


class Places:
    def __init__(self):
        d, t = lax.axis_index("dp"), lax.axis_index("tensor")
        self.d, self.t = d, t
        self.half = d % 2
        self.quarter = d % 4
        self.core_t, self.y_t = flip(t, 1), flip(t, 2)
        self.far_t = flip(self.core_t, 2)
        self.core = (d, self.core_t)
        self.y = (d, self.y_t)
        self.across = (d, self.far_t)
        self.x = (flip(d, 1), t)
        self.z = (flip(d, 2), t)


class Chunk:
    def __init__(self, links, places, own, whole, first, base, rows, over_x):
        part = rows // 4
        q = places.quarter
        qx, qz = flip(q, 1), flip(q, 2)
        qd = flip(qx, 2)
        g, g2 = places.t, places.y_t

        def at(group, quarter):
            return whole.at[ds(first(group) + base + quarter * part, part)]

        def pass_on(quarter, device):
            return links(at(g2, quarter), at(g2, quarter), device)

        self.y = links(own.at[ds(base + q * part, part)], at(g, q), places.y)
        self.one = [pass_on(q, places.x), pass_on(q, places.z), pass_on(q, places.core)]
        self.two = [pass_on(qz, places.x) if over_x else pass_on(qx, places.z)]
        self.two += [pass_on(qx, places.core), pass_on(qz, places.core)]
        self.three = pass_on(qd, places.core)

    def start(self):
        self.y.start()

    def relay(self):
        self.y.wait_recv()
        for copy in self.one:
            copy.start()

    def forward(self):
        self.one[0].wait_recv()
        self.one[1].wait_recv()
        for copy in self.two:
            copy.start()

    def close(self):
        self.two[0].wait_recv()
        self.three.start()

    def whole_here(self):
        for copy in (self.one[2], self.two[1], self.two[2], self.three):
            copy.wait_recv()


def bucket_of(relative):
    half = NB // 2
    exact = half // 2
    distance = np.abs(relative)
    scaled = np.log(np.maximum(distance, 1) / exact) / np.log(MAX_DIST / exact) * (half - exact)
    far = np.minimum(exact + scaled.astype(np.int32), half - 1)
    return ((relative > 0) * half + np.where(distance < exact, distance, far)).astype(np.int32)


def bucket_lines(seq):
    m = np.arange(2 * seq)
    rel = seq - 128 - m
    rel = np.where(rel < -seq, rel + 2 * seq, rel)
    rel = np.clip(rel, -(seq - 1), seq - 1)
    ids = bucket_of(rel)
    return (ids[None, :] == np.arange(NB)[:, None]).astype(np.float32)


class Names:
    def __init__(self, **refs):
        self.__dict__.update(refs)


def layer(names, sizes, *refs):
    r = Names(**dict(zip(names, refs)))
    tokens, width, seq, seqs, groups, inner, heads_here, hd, hidden, cols, experts, zs = sizes
    heads = groups * heads_here
    span = 3 * hd
    rank = cols // experts
    places = Places()
    t, d, half = places.t, places.d, places.half
    z = d // 2
    links = Links(r.send, r.recv)

    def gb_rows(g, p):
        return ds(4 * PAD + (g * 3 + p) * PAD, PAD)

    r.zed = r.low_in
    r.dsmall = r.dctx.at[: 4 * PAD]
    r.d_low = [r.low_out, r.d_low_in, r.d_low_out]
    r.core_out = [r.cot.at[:128], r.cot.at[128:256]]
    r.y_out, r.x_out, r.z_out = r.cot.at[256:384], r.cot.at[384:448], r.cot.at[448:512]
    batch = min(zs, 4)
    r.z_in = r.cot.at[512 : 512 + 64 * batch]

    local = [0]

    def here(src, dst):
        local[0] += 1
        return pltpu.make_async_copy(src, dst, r.local.at[local[0] - 1])

    get_x = here(r.x, r.xy)
    get_c = here(r.c, r.cot)
    get_qkv = [
        here(
            r.wqkv_own.at[p, h * hd : (h + 1) * hd],
            r.wqkv.at[ds(t * heads_here * span + h * span + p * hd, hd)],
        )
        for h in range(heads_here)
        for p in range(3)
    ]
    get_x.start()
    for copy in get_qkv:
        copy.start()

    z_peers = [((z + i) % zs * 2 + half, t) for i in range(1, zs)]
    same_x = [(half * 4 + j, (d, j)) for j in (places.core_t, places.y_t, places.far_t)]
    other_x = [((1 - half) * 4 + j, (flip(d, 1), j)) for j in (places.core_t, places.y_t, places.far_t, t)]
    block_peers = same_x + other_x
    barrier = pltpu.get_barrier_semaphore()
    known = [dev for _, dev in block_peers] + z_peers
    for dev in known:
        pl.semaphore_signal(barrier, inc=1, device_id=dev, device_id_type=MESH)

    def quarter_of(ref, g, rows):
        return ref.at[ds(g * rows, rows)]

    def qkv_row(g):
        return g * heads_here * span

    qkv_chunks = [
        Chunk(links, places, quarter_of(r.wqkv, t, heads_here * span), r.wqkv, qkv_row, h * span, span, h % 2 == 0)
        for h in range(heads_here)
    ]
    o_chunk = Chunk(links, places, r.wo_own, r.wo, lambda g: g * inner, 0, inner, False)
    in_chunks = [
        Chunk(links, places, r.win_own, r.win_all, lambda g: g * width, j * width // 2, width // 2, j == 0)
        for j in range(2)
    ]
    out_chunks = [
        Chunk(links, places, r.wout_own, r.wout, lambda g: g * hidden, j * hidden // 2, hidden // 2, j == 1)
        for j in range(2)
    ]

    own_qkv = quarter_of(r.wqkv, t, heads_here * span)
    core_qkv = links(own_qkv, own_qkv, places.core)
    core_o = links(r.wo_own, quarter_of(r.wo, t, inner), places.core)
    core_in = links(r.win_own, quarter_of(r.win_all, t, width), places.core)
    core_out = links(r.wout_own, quarter_of(r.wout, t, hidden), places.core)
    small = [r.bq, r.rb, r.bin]
    small_y = [links(a.at[t], a.at[t], places.y) for a in small]
    small_core = [links(a.at[t], a.at[t], places.core) for a in small]
    small_far = [links(a.at[places.y_t], a.at[places.y_t], places.core) for a in small]
    keep = [
        here(r.wo_own, quarter_of(r.wo, t, inner)),
        here(r.wout_own, quarter_of(r.wout, t, hidden)),
    ]

    for p in range(3):
        r.bq[t, p * RANK_PAD : (p + 1) * RANK_PAD] = filled(r.b_qkv[p], RANK_PAD)
    pick = lax.broadcasted_iota(jnp.int32, (16, heads_here), 0)
    pick = pick == lax.broadcasted_iota(jnp.int32, (16, heads_here), 1)
    r.rb[t] = nn(pick.astype(F32).astype(BF16), r.table[...]).astype(BF16)
    r.bin[t] = filled(r.b_in[...], PAD)
    for copy in get_qkv:
        copy.wait()
    pl.semaphore_wait(barrier, len(known))
    qkv_chunks[0].start()
    core_qkv.start()
    small_core[0].start()
    small_core[1].start()
    qkv_chunks[1].start()
    qkv_chunks[2].start()
    o_chunk.start()
    small_y[0].start()
    small_y[1].start()
    get_c.start()
    keep[0].start()
    for p in range(3):
        r.wsm[p * PAD : (p + 1) * PAD, :] = filled(r.at[p], PAD)
    spots = lax.broadcasted_iota(jnp.int32, (PAD, experts), 0) // rank
    spots = spots == lax.broadcasted_iota(jnp.int32, (PAD, experts), 1)
    r.wsm[3 * PAD :, :] = nn(spots.astype(F32).astype(BF16), r.router[...]).astype(BF16)
    r.ao[...] = filled(r.a_o[...], PAD)
    r.bo[...] = filled(r.b_o[...], PAD)
    r.ain[...] = filled(r.at[3], PAD)
    r.bout[...] = filled(r.b_out[...], PAD)
    for j in range(groups):
        r.aout[j] = filled(r.a_out[:, j * hidden : (j + 1) * hidden], PAD)
    g1 = r.g1[...].reshape(1, width)
    g2 = r.g2[...].reshape(1, width)

    tb = 256
    get_x.wait()

    def norm(i, c):
        rows = ds(i * tb, tb)
        x = r.xy[rows, :].astype(F32)
        n1 = (x * lax.rsqrt(jnp.mean(x * x, axis=1, keepdims=True) + EPS) * g1).astype(BF16)
        r.n1[rows, :] = n1
        lines = nt(r.wsm[...], n1)
        low = lines[: 3 * PAD]
        logits = lines[3 * PAD :]
        valid = lax.broadcasted_iota(jnp.int32, logits.shape, 0) < cols
        logits = jnp.where(valid, logits, -jnp.inf)
        ex = jnp.exp(logits - jnp.max(logits, axis=0, keepdims=True))
        gate = ex / (jnp.sum(ex, axis=0, keepdims=True) * (1.0 / rank))
        r.low[:, rows] = low
        r.gate[:, rows] = gate
        for p in range(3):
            r.gated[p * PAD : (p + 1) * PAD, rows] = (low[p * PAD : (p + 1) * PAD] * gate).astype(BF16)
        return c

    lax.fori_loop(0, tokens // tb, norm, 0)

    maskrow = jnp.where(lax.broadcasted_iota(jnp.int32, (16, seq), 1) < r.lens[seqs - 1], 0.0, NEG)
    maskrow = jnp.where(lax.broadcasted_iota(jnp.int32, (16, seq), 0) == 0, maskrow, 0.0).astype(BF16)
    onerow = (lax.broadcasted_iota(jnp.int32, (16, seq), 0) == 0).astype(F32).astype(BF16)

    def head_row(n):
        return (group_at(t, n // heads_here) * heads_here + n % heads_here) * span

    def next_group(k):
        g = group_at(t, k)
        u = nn(r.rb[g], r.onehot[...]) * LOG2E
        for h in range(heads_here):
            r.urow[k * heads_here + h] = u[h : h + 1]
            for p in range(3):
                block = r.bq[g, p * RANK_PAD : (p + 1) * RANK_PAD, h * hd : (h + 1) * hd]
                r.bh[h, p * PAD : p * PAD + RANK_PAD, :] = block

    def project(n):
        row = head_row(n)
        h = n % heads_here
        out = nt(r.wqkv[ds(row, span), :], r.n1[...])
        for p in range(3):
            up = tn(r.bh[h, p * PAD : p * PAD + RANK_PAD, :], r.gated[p * PAD : p * PAD + RANK_PAD, :])
            r.qkv[ds(row + p * hd, hd), :] = (out[p * hd : (p + 1) * hd] + up).astype(BF16)

    def spread_bias(n):
        line = jnp.broadcast_to(r.urow[n], (128, 2 * seq))
        r.brow[n % 2] = pltpu.roll(line, 0, 1, stride=1, stride_axis=0)[:, : 2 * seq - 128]

    qb = 256
    parts = seq // qb

    def score_place(i):
        return slice((i % 2) * seq, (i % 2 + 1) * seq), slice((i // 2 % 3) * qb, (i // 2 % 3 + 1) * qb)

    blocks = [(s, b) for s in range(seqs) for b in range(parts)]

    def keys_of(n, s):
        row = head_row(n)
        token = slice(s * seq, (s + 1) * seq)
        q = r.qkv[ds(row, hd), token]
        k = r.qkv[ds(row + hd, hd), token].astype(F32) * LOG2E
        high = k.astype(BF16)
        keys = [high, (k - high.astype(F32)).astype(BF16)]
        queries = [q, q]
        if s > 0:
            keys.append(maskrow)
            queries.append(onerow)
        return jnp.concatenate(keys, axis=0), jnp.concatenate(queries, axis=0)

    def values_of(n):
        row = head_row(n)
        return [
            jnp.concatenate([r.qkv[ds(row + 2 * hd, hd), s * seq : (s + 1) * seq], onerow], axis=0)
            for s in range(seqs)
        ]

    def score(n, i, made):
        s, b = blocks[i]
        if b == 0:
            made[s] = keys_of(n, s)
        keys, queries = made[s]
        top = None
        rows, lanes = score_place(i)
        for kc in range(seq // 256):
            st = tn(keys[:, kc * 256 : (kc + 1) * 256], queries[:, b * qb : (b + 1) * qb])
            for kk in range(2):
                kb = kc * 2 + kk
                shift = seq - 128 - 128 * kb + b * qb
                st_b = st[kk * 128 : (kk + 1) * 128] + r.brow[n % 2, :, shift : shift + qb]
                r.acc[rows.start + kb * 128 : rows.start + (kb + 1) * 128, lanes] = st_b
                peak = jnp.max(st_b, axis=0, keepdims=True)
                top = peak if top is None else jnp.maximum(top, peak)
        return top

    def soft(n, i, top, values):
        s, b = blocks[i]
        rows, lanes = score_place(i)
        token = slice(s * seq + b * qb, s * seq + (b + 1) * qb)
        for kb in range(seq // 128):
            st = r.acc[rows.start + kb * 128 : rows.start + (kb + 1) * 128, lanes]
            r.e[n * seqs + s, kb * 128 : (kb + 1) * 128, b * qb : (b + 1) * qb] = jnp.exp2(st - top).astype(BF16)
        o = nn(values[s], r.e[n * seqs + s, :, b * qb : (b + 1) * qb])
        recip = 1.0 / o[hd : hd + 1]
        r.recip[n, :, token] = recip
        r.ctx[ds(head_row(n) // 3, hd), token] = (o[:hd] * recip).astype(BF16)

    def forward_step(step):
        if step == 0:
            qkv_chunks[0].relay()
        if step == 1:
            in_chunks[0].start()
        if step == 2:
            qkv_chunks[1].relay()
            core_qkv.wait_recv()
            small_core[0].wait_recv()
            small_core[1].wait_recv()
            core_o.start()
        if step == 3:
            qkv_chunks[2].relay()
            qkv_chunks[0].forward()
            in_chunks[1].start()
        if step == 4:
            qkv_chunks[1].forward()
        if step == 5:
            qkv_chunks[0].close()
            qkv_chunks[2].forward()
            small_y[0].wait_recv()
            small_y[1].wait_recv()
            small_far[0].start()
            small_far[1].start()
            o_chunk.relay()
        if step == 6:
            qkv_chunks[1].close()
            out_chunks[0].start()
        if step == 7:
            qkv_chunks[2].close()
            o_chunk.forward()
            in_chunks[0].relay()
            core_in.start()
            small_y[2].start()
            small_core[2].start()
        if step == 8:
            small_far[0].wait_recv()
            small_far[1].wait_recv()
            qkv_chunks[0].whole_here()
            out_chunks[1].start()
        if step == 9:
            qkv_chunks[1].whole_here()
            o_chunk.close()
            in_chunks[1].relay()
        if step == 10:
            qkv_chunks[2].whole_here()
            core_out.start()
            keep[1].start()
        if step == 11:
            in_chunks[0].forward()
            out_chunks[0].relay()

    def first_step(step):
        if step == 1:
            in_chunks[1].forward()
            out_chunks[1].relay()

    def forward_head(n, tops):
        for step in range(12):
            pl.when(n == step)(lambda step=step: forward_step(step))
        follow = jnp.minimum(n + 1, heads - 1)

        @pl.when(jnp.logical_and(follow % heads_here == 0, n < heads - 1))
        def _():
            next_group(follow // heads_here)

        values = values_of(n)
        project(follow)
        spread_bias(follow)
        made, fresh = {}, []
        behind = 2
        for i in range(len(blocks)):
            soft(n, i, tops[i], values)
            if i + 1 >= behind:
                fresh.append(score(follow, i + 1 - behind, made))
        for i in range(len(fresh), len(blocks)):
            fresh.append(score(follow, i, made))
        return tuple(fresh)

    next_group(0)
    project(0)
    spread_bias(0)
    made = {}
    lax.fori_loop(0, heads, forward_head, tuple(score(0, i, made) for i in range(len(blocks))))

    core_o.wait_recv()
    keep[0].wait()
    o_chunk.whole_here()
    get_c.wait()
    win_first = here(r.win_own, r.win.at[0])
    win_first.start()

    def first(i, c):
        pl.when(i == 1)(lambda: first_step(1))
        for j in range(2):
            rows = ds((2 * i + j) * tb, tb)
            gate = r.gate[:, rows]
            ctx = r.ctx[:, rows]
            low = nn(r.ao[...], ctx)
            r.low_o[:, rows] = low
            gated = (low * gate).astype(BF16)
            h1 = r.xy[rows, :].astype(F32) + tn(ctx, r.wo[...]) + tn(gated, r.bo[...])
            r.h1[rows, :] = h1
            n2 = (h1 * lax.rsqrt(jnp.mean(h1 * h1, axis=1, keepdims=True) + EPS) * g2).astype(BF16)
            r.n2[rows, :] = n2
            low = nt(r.ain[...], n2)
            r.low_in[:, rows] = low
            r.gin[:, rows] = (low * gate).astype(BF16)
            low = nt(r.bout[...], r.cot[rows, :])
            r.d_low_out[:, rows] = low
            r.dgo[:, rows] = (low * gate).astype(BF16)
        return c

    lax.fori_loop(0, tokens // tb // 2, first, 0)
    r.acc[...] = jnp.zeros_like(r.acc)
    r.dn2[...] = jnp.zeros_like(r.dn2)
    r.low_out[...] = jnp.zeros_like(r.low_out)
    r.d_low_in[...] = jnp.zeros_like(r.d_low_in)
    r.part[...] = jnp.zeros_like(r.part)

    wide = 512
    steps = tokens // wide
    win_next = [here(quarter_of(r.win_all, group_at(t, k), width), r.win.at[k % 2]) for k in range(1, groups)]

    def feed_step(step):
        if step == 0:
            keep[1].wait()
            win_first.wait()
            in_chunks[0].close()
            out_chunks[0].forward()
            core_in.wait_recv()
            win_next[0].start()
            small_y[2].wait_recv()
            small_far[2].start()
        if step == 1:
            in_chunks[1].close()
            out_chunks[1].forward()
        if step == 2:
            out_chunks[0].close()
            core_out.wait_recv()
            small_core[2].wait_recv()
            win_next[0].wait()
            win_next[1].start()
        if step == 3:
            out_chunks[1].close()
        if step == 4:
            for chunk in in_chunks:
                chunk.whole_here()
            win_next[1].wait()
            win_next[2].start()
        if step == 6:
            small_far[2].wait_recv()
            for chunk in out_chunks:
                chunk.whole_here()
            win_next[2].wait()

    active, d_pre = r.xy.at[:wide], r.xy.at[wide : 2 * wide]
    third = hidden // 3

    def chunk(step, c):
        for point in range(7):
            pl.when(step == point)(lambda point=point: feed_step(point))
        n = step // steps
        rows = ds((step % steps) * wide, wide)
        g = group_at(t, n)
        slot = n % 2
        gin, dgo = r.gin[:, rows], r.dgo[:, rows]
        for j in range(3):
            cs = slice(j * third, (j + 1) * third)
            pre = nn(r.n2[rows, :], r.win[slot, :, cs]) + tn(gin, r.bin[g, :, cs])
            da = nt(r.cot[rows, :], r.wout[ds(g * hidden + j * third, third), :]) + tn(dgo, r.aout[g, :, cs])
            sig = 1.0 / (1.0 + jnp.exp(-pre))
            act = pre * sig
            active[:, cs] = act.astype(BF16)
            d_pre[:, cs] = (da * (sig + act * (1.0 - sig))).astype(BF16)
        r.acc[rows, :] += nn(active[...], r.wout[ds(g * hidden, hidden), :])
        r.dn2[rows, :] += nt(d_pre[...], r.win[slot])
        r.low_out[:, rows] += nt(r.aout[g], active[...])
        r.d_low_in[:, rows] += nt(r.bin[g], d_pre[...])
        r.part[g, :cols] += nn(dgo, active[...])[:cols]
        r.part[g, 2 * cols : 3 * cols] += nn(gin, d_pre[...])[:cols]
        return c

    lax.fori_loop(0, groups * steps, chunk, 0)

    def last(i, c):
        for j in range(2):
            rows = ds((2 * i + j) * tb, tb)
            gate = r.gate[:, rows]
            cot, n2, ctx, h1 = r.cot[rows, :], r.n2[rows, :], r.ctx[:, rows], r.h1[rows, :]
            low_out, d_low_in = r.low_out[:, rows], r.d_low_in[:, rows]
            go = (low_out * gate).astype(BF16)
            r.xy[rows, :] = (h1 + r.acc[rows, :] + tn(go, r.bout[...])).astype(BF16)
            dgi = (d_low_in * gate).astype(BF16)
            up = (r.dn2[rows, :] + tn(dgi, r.ain[...])) * g2
            r.part[2, cols : 2 * cols] += nn(go, cot)[:cols]
            r.part[3, cols : 2 * cols] += nn(dgi, n2)[:cols]
            inv = lax.rsqrt(jnp.mean(h1 * h1, axis=1, keepdims=True) + EPS)
            dh = cot.astype(F32) + inv * up - h1 * (inv * inv * inv * jnp.mean(h1 * up, axis=1, keepdims=True))
            r.h1[rows, :] = dh
            da = dh.astype(BF16)
            d_low = nt(r.bo[...], da)
            low = r.low_o[:, rows]
            dgo = (d_low * gate).astype(BF16)
            r.part[1, cols : 2 * cols] += nn((low * gate).astype(BF16), da)[:cols]
            r.part[0, cols : 2 * cols] += nt(dgo, ctx)[:cols]
            r.dctx[:, rows] = (nt(r.wo[...], da) + tn(r.ao[...], dgo)).astype(BF16)
            r.zed[:, rows] = d_low * low + d_low_in * r.low_in[:, rows] + r.d_low_out[:, rows] * low_out
        return c

    lax.fori_loop(0, tokens // tb // 2, last, 0)
    put_y = here(r.xy, r.y)
    put_y.start()

    rows_half = 64
    mine, other = ds(half * rows_half, rows_half), ds((1 - half) * rows_half, rows_half)
    shared = 2 * cols
    to_core = links(r.cot.at[:256], r.core_in, places.core)
    to_y = links(r.y_out, r.y_in, places.y)
    to_x = links(r.x_out, r.x_in, places.x)
    to_z = [links(r.z_out, r.z_all.at[ds(z * 64, 64)], dev) for dev in z_peers]
    keep_z = here(r.z_out, r.z_all.at[ds(z * 64, 64)])
    get_z = [here(r.z_all.at[i * 64 : (i + batch) * 64], r.z_in) for i in range(0, zs, batch)]
    all_x = links(r.full.at[t, mine], r.full.at[t, mine], places.x)
    all_y = links(r.full.at[t, :shared], r.full.at[t, :shared], places.y)
    all_core = [
        links(r.full.at[j, :shared], r.full.at[j, :shared], places.core) for j in (t, places.y_t)
    ]
    share = r.small_in.shape[1]
    b_share = r.b_in_sum.shape[1]
    me = half * 4 + t
    give = []
    for j, dev in block_peers:
        give.append(links(r.small_out.at[ds(j * share, share)], r.small_in.at[me], dev))
        give.append(links(r.b_all.at[j % 4, ds(j // 4 * b_share, b_share)], r.b_in_sum.at[me], dev))
    cross = []
    for dev in z_peers:
        cross.append(links(r.small_z.at[z], r.small_z.at[z], dev))
        cross.append(links(r.b_z.at[z], r.b_z.at[z], dev))
    back = [links(r.small_full.at[me], r.small_full.at[me], dev) for _, dev in block_peers]
    back.append(links(r.b_full.at[half], r.b_full.at[half], places.x))

    def sum_step(step):
        if step == 0:
            r.core_out[0][...] = r.part[places.core_t].astype(BF16)
            r.core_out[1][...] = r.part[places.far_t].astype(BF16)
            to_core.start()
        if step == 2:
            to_core.wait_recv()
            r.y_out[...] = (r.part[places.y_t] + r.core_in[128:].astype(F32)).astype(BF16)
            to_y.start()
            r.part[t] += r.core_in[:128].astype(F32)
            put_y.wait()
            get_x_again.start()
        if step == 5:
            to_y.wait_recv()
            r.part[t] += r.y_in[...].astype(F32)
            r.x_out[...] = r.part[t, other, :].astype(BF16)
            to_x.start()
        if step == 7:
            to_x.wait_recv()
            r.z_out[...] = (r.part[t, mine, :] + r.x_in[...].astype(F32)).astype(BF16)
            keep_z.start()
            for copy in to_z:
                copy.start()

    def sum_z():
        for copy in to_z:
            copy.wait_recv()
        keep_z.wait()
        total = None
        for copy in get_z:
            copy.start()
            copy.wait()
            for i in range(batch):
                term = r.z_in[i * 64 : (i + 1) * 64].astype(F32)
                total = term if total is None else total + term
        r.full[t, mine] = total.astype(BF16)
        all_x.start()

    get_x_again = here(r.x, r.xy)

    def attend_back(n):
        row = head_row(n)
        full = ds(row // 3, hd)
        blocks = [(s, b) for s in range(seqs) for b in range(parts)]
        sent, sums = {}, {}

        def ds_place(i):
            return slice((i % 2) * seq, (i % 2 + 1) * seq), slice((i // 2 % 3) * qb, (i // 2 % 3 + 1) * qb)

        def score(i):
            s, b = blocks[i]
            token = slice(s * seq + b * qb, s * seq + (b + 1) * qb)
            do = (r.dctx[full, token].astype(F32) * r.recip[n, :, token]).astype(BF16)
            delta = jnp.sum(do.astype(F32) * r.ctx[full, token].astype(F32), axis=0, keepdims=True)
            sent[i] = do
            v = r.qkv[ds(row + 2 * hd, hd), s * seq : (s + 1) * seq]
            rows, lanes = ds_place(i)
            for kc in range(seq // 256):
                keys = slice(kc * 256, (kc + 1) * 256)
                dp = tn(v[:, keys], do)
                e = r.e[n * seqs + s, keys, b * qb : (b + 1) * qb].astype(F32)
                r.n2[rows.start + kc * 256 : rows.start + (kc + 1) * 256, lanes] = (e * (dp - delta)).astype(BF16)

        def grads(i):
            s, b = blocks[i]
            token = slice(s * seq + b * qb, s * seq + (b + 1) * qb)
            whole = slice(s * seq, (s + 1) * seq)
            k = r.qkv[ds(row + hd, hd), whole]
            q = r.qkv[ds(row, hd), token]
            rows, lanes = ds_place(i)
            dsc = r.n2[rows, lanes]
            dk = nt(q, dsc)
            dv = nt(sent[i], r.e[n * seqs + s, :, b * qb : (b + 1) * qb])
            r.qkv[ds(row, hd), token] = nn(k, dsc).astype(BF16)
            if b > 0:
                dk, dv = sums[s][0] + dk, sums[s][1] + dv
            sums[s] = dk, dv
            if b == parts - 1:
                r.qkv[ds(row + hd, hd), whole] = dk.astype(BF16)
                r.qkv[ds(row + 2 * hd, hd), whole] = dv.astype(BF16)

        ahead = 2
        for i in range(ahead):
            score(i)
        for i in range(len(blocks)):
            if i + ahead < len(blocks):
                score(i + ahead)
            grads(i)

    def backward_head(n, c):
        for step in (0, 2, 5, 7):
            pl.when(n == step)(lambda step=step: sum_step(step))
        attend_back(n)
        return c

    lax.fori_loop(0, heads, backward_head, 0)
    sum_z()

    gsm = r.acc.at[: 4 * PAD]

    def adapters(g, c):
        for p in range(3):
            dp = [
                r.qkv[ds((g * heads_here + h) * span + p * hd, hd), :] for h in range(heads_here)
            ]
            dp = jnp.concatenate(dp, axis=0)
            low = nn(r.bq[g, p * RANK_PAD : (p + 1) * RANK_PAD], dp)
            r.d_low[p][:RANK_PAD, :] += low
            r.acc[gb_rows(g, p), :inner] = nt(r.gated[p * PAD : (p + 1) * PAD, :], dp)
        return c

    for p in range(3):
        r.d_low[p][...] = jnp.zeros(r.d_low[p].shape, F32)
    lax.fori_loop(0, groups, adapters, 0)
    gate = r.gate[...]
    prod = r.zed[...]
    for p in range(3):
        part = slice(p * PAD, (p + 1) * PAD)
        prod = prod + r.d_low[p][...] * r.low[part, :]
        r.dsmall[part, :] = (r.d_low[p][...] * gate).astype(BF16)
    high = prod.astype(BF16)
    low = (prod - high.astype(F32)).astype(BF16)
    same = lax.broadcasted_iota(jnp.int32, (PAD, PAD), 0) // rank
    same = same == lax.broadcasted_iota(jnp.int32, (PAD, PAD), 1) // rank
    same = jnp.logical_and(same, lax.broadcasted_iota(jnp.int32, (PAD, PAD), 1) < cols).astype(F32).astype(BF16)
    d_gate = nn(same, high) + nn(same, low)
    d_logit = gate * (d_gate - jnp.sum(gate * prod, axis=0, keepdims=True))
    row = lax.broadcasted_iota(jnp.int32, d_logit.shape, 0)
    chosen = jnp.logical_and(row % rank == 0, row < cols)
    r.dsmall[3 * PAD :, :] = jnp.where(chosen, d_logit, 0.0).astype(BF16)
    gsm[...] = nn(r.dsmall[...], r.n1[...])
    lines = [gsm[p * PAD : p * PAD + cols, :] for p in range(3)]
    lines.append(jnp.concatenate([gsm[3 * PAD + rank * e : 3 * PAD + rank * e + 1, :] for e in range(16)], axis=0))
    count = 3 * cols + 16
    tall = -(-count // 16) * 16
    lines.append(jnp.zeros((tall - count, width), F32))
    lines = jnp.concatenate(lines, axis=0).astype(BF16)
    strips = width // 128
    for i in range(strips):
        r.small_out[i * tall : (i + 1) * tall, :] = lines[:, i * 128 : (i + 1) * 128]
    r.small_out[strips * tall :, :] = jnp.zeros((r.small_out.shape[0] - strips * tall, 128), BF16)
    for j in range(groups):
        block = [r.acc[gb_rows(j, p), :inner][:cols] for p in range(3)]
        block.append(jnp.zeros((r.b_all.shape[1] - 3 * cols, inner), F32))
        r.b_all[j] = jnp.concatenate(block, axis=0).astype(BF16)
    for copy in give:
        copy.start()
    all_x.wait_recv()
    all_y.start()
    all_core[0].start()
    get_x_again.wait()

    def finish(i, c):
        rows = ds(i * tb, tb)
        dn = tn(r.qkv[:, rows], r.wqkv[...]) + tn(r.dsmall[:, rows], r.wsm[...])
        x = r.xy[rows, :].astype(F32)
        inv = lax.rsqrt(jnp.mean(x * x, axis=1, keepdims=True) + EPS)
        up = dn * g1
        r.h1[rows, :] += inv * up - x * (inv * inv * inv * jnp.mean(x * up, axis=1, keepdims=True))
        return c

    part_rows = tokens // 2
    put_x = [here(r.h1.at[i * part_rows : (i + 1) * part_rows], r.gx.at[i * part_rows : (i + 1) * part_rows]) for i in range(2)]
    lax.fori_loop(0, tokens // tb // 2, finish, 0)
    put_x[0].start()
    all_y.wait_recv()
    all_core[1].start()
    for copy in give:
        copy.wait_recv()
    r.small_in[me] = r.small_out[ds(me * share, share), :]
    r.b_in_sum[me] = r.b_all[t, ds(half * b_share, b_share), :]
    total = r.small_in[0].astype(F32)
    total_b = r.b_in_sum[0].astype(F32)
    for i in range(1, 8):
        total = total + r.small_in[i].astype(F32)
        total_b = total_b + r.b_in_sum[i].astype(F32)
    r.small_z[z] = total.astype(BF16)
    r.b_z[z] = total_b.astype(BF16)
    for copy in cross:
        copy.start()
    lax.fori_loop(tokens // tb // 2, tokens // tb, finish, 0)
    put_x[1].start()
    for copy in cross:
        copy.wait_recv()
    total = r.small_z[0].astype(F32)
    total_b = r.b_z[0].astype(F32)
    for i in range(1, zs):
        total = total + r.small_z[i].astype(F32)
        total_b = total_b + r.b_z[i].astype(F32)
    r.small_full[me] = total.astype(BF16)
    r.b_full[half] = total_b.astype(BF16)
    for copy in back:
        copy.start()
    for copy in all_core:
        copy.wait_recv()
    results = [here(r.full, r.full_out), here(r.full.at[t, 2 * cols :], r.own_out)]
    for copy in results:
        copy.start()
    for copy in back:
        copy.wait_recv()
    late = [here(r.small_full, r.small_res), here(r.b_full, r.b_res)]
    for copy in late:
        copy.start()
    for copy in results + late:
        copy.wait()
    for copy in put_x:
        copy.wait()
    for copy in links.made:
        copy.wait_send()


def hand_out(cols, experts, *refs):
    y, gx, full, own, small, b_full = refs[:6]
    y_out, gx_out, g_router, g_a_in, g_a_o, g_a_out, g_b_qkv, g_b_o, g_b_in, g_b_out = refs[6:16]
    y_buf, x_buf, sems = refs[16:]
    pieces = [(y, y_buf, y_out, 0, y.shape[0])]
    part = gx.shape[0] // 4
    pieces += [(gx, x_buf, gx_out, i * part, (i + 1) * part) for i in range(4)]
    get = [
        pltpu.make_async_copy(a.at[lo:hi], b.at[lo:hi], sems.at[i]) for i, (a, b, _, lo, hi) in enumerate(pieces)
    ]
    put = [
        pltpu.make_async_copy(b.at[lo:hi], c.at[lo:hi], sems.at[5 + i]) for i, (_, b, c, lo, hi) in enumerate(pieces)
    ]
    for copy in get:
        copy.start()
    for one, two in zip(get, put):
        one.wait()
        two.start()
    groups = full.shape[0]
    hidden = g_a_out.shape[1] // groups
    g_b_in[...] = own[...].astype(F32)[:cols]
    for j in range(groups):
        block = full[j].astype(F32)
        g_a_out[:, j * hidden : (j + 1) * hidden] = block[:cols]
        target = (g_a_o, g_b_o, g_b_out, g_a_in.at[3])[j]
        target[...] = block[cols : 2 * cols]
    count = 3 * cols + 16
    tall = -(-count // 16) * 16
    flat = small[...].reshape(small.shape[0] * small.shape[1], 128)
    for i in range(g_router.shape[1] // 128):
        block = flat[i * tall : (i + 1) * tall].astype(F32)
        lanes = slice(i * 128, (i + 1) * 128)
        for p in range(3):
            g_a_in[p, :, lanes] = block[p * cols : (p + 1) * cols]
        g_router[:, lanes] = block[3 * cols : 3 * cols + experts]
    block = b_full[...].reshape(b_full.shape[0] * b_full.shape[1], b_full.shape[2]).astype(F32)
    for p in range(3):
        g_b_qkv[p] = block[p * cols : (p + 1) * cols]
    for copy in put:
        copy.wait()


def shards(
    layer_inputs, lengths, first_gain, second_gain, router, wqkv, bias_table, wo, win, wout,
    a_in, a_o, a_out, b_qkv, b_o, b_in, b_out, cotangent,
):
    groups = lax.axis_size("tensor")
    zs = lax.axis_size("dp") // 2
    seqs, seq, width = layer_inputs.shape
    tokens = seqs * seq
    inner = wo.shape[0]
    heads_here = bias_table.shape[1]
    heads = heads_here * groups
    hd = inner // heads_here
    hidden = win.shape[1]
    experts = router.shape[1]
    cols = a_in.shape[2]
    sizes = (tokens, width, seq, seqs, groups, inner, heads_here, hd, hidden, cols, experts, zs)
    ins = {
        "lens": (lengths, pltpu.SMEM),
        "g1": (first_gain, pltpu.VMEM),
        "g2": (second_gain, pltpu.VMEM),
        "at": (jnp.swapaxes(a_in, 1, 2), pltpu.VMEM),
        "router": (router.T, pltpu.VMEM),
        "onehot": (jnp.asarray(bucket_lines(seq), BF16), pltpu.VMEM),
        "b_qkv": (b_qkv, pltpu.VMEM),
        "table": (bias_table.T, pltpu.VMEM),
        "b_in": (b_in, pltpu.VMEM),
        "a_o": (a_o.T, pltpu.VMEM),
        "b_o": (b_o, pltpu.VMEM),
        "a_out": (a_out.T, pltpu.VMEM),
        "b_out": (b_out, pltpu.VMEM),
        "x": (layer_inputs.reshape(tokens, width), pl.ANY),
        "c": (cotangent.reshape(tokens, width), pl.ANY),
        "wqkv_own": (jnp.swapaxes(wqkv, 1, 2), pl.ANY),
        "wo_own": (wo, pl.ANY),
        "win_own": (win, pl.ANY),
        "wout_own": (wout, pl.ANY),
    }
    outs = {
        "y": ((tokens, width), BF16, pl.ANY),
        "gx": ((tokens, width), F32, pl.ANY),
        "full_out": ((groups, 128, width), BF16, pl.ANY),
        "own_out": ((128 - 2 * cols, width), BF16, pl.ANY),
        "small_res": ((8, 112, 128), BF16, pl.ANY),
        "b_res": ((2, 64, inner), BF16, pl.ANY),
        "win_all": ((groups * width, hidden), BF16, pl.ANY),
        "z_all": ((zs * 64, width), BF16, pl.ANY),
    }
    given = [
        ((tokens, width), BF16, pl.ANY),
        ((tokens, width), F32, pl.ANY),
        ((experts, width), F32, pltpu.VMEM),
        ((4, cols, width), F32, pltpu.VMEM),
        ((cols, width), F32, pltpu.VMEM),
        ((cols, groups * hidden), F32, pltpu.VMEM),
        ((3, cols, inner), F32, pltpu.VMEM),
        ((cols, width), F32, pltpu.VMEM),
        ((cols, hidden), F32, pltpu.VMEM),
        ((cols, width), F32, pltpu.VMEM),
    ]
    line = (PAD, tokens)
    scratch = {
        "xy": ((tokens, width), BF16),
        "cot": ((tokens, width), BF16),
        "n1": ((tokens, width), BF16),
        "low": ((3 * PAD, tokens), F32),
        "gate": (line, F32),
        "gated": ((3 * PAD, tokens), BF16),
        "wqkv": ((3 * groups * inner, width), BF16),
        "qkv": ((3 * groups * inner, tokens), BF16),
        "e": ((heads * seqs, seq, seq), BF16),
        "recip": ((heads, 1, tokens), F32),
        "ctx": ((groups * inner, tokens), BF16),
        "wsm": ((4 * PAD, width), BF16),
        "bq": ((groups, 3 * RANK_PAD, inner), BF16),
        "bh": ((heads_here, 3 * PAD, hd), BF16),
        "rb": ((groups, 16, NB), BF16),
        "bin": ((groups, PAD, hidden), BF16),
        "urow": ((heads, 1, 2 * seq), F32),
        "brow": ((2, 128, 2 * seq - 128), F32),
        "wo": ((groups * inner, width), BF16),
        "win": ((2, width, hidden), BF16),
        "wout": ((groups * hidden, width), BF16),
        "h1": ((tokens, width), F32),
        "n2": ((tokens, width), BF16),
        "acc": ((tokens, width), F32),
        "dn2": ((tokens, width), F32),
        "gin": (line, BF16),
        "dgo": (line, BF16),
        "low_o": (line, F32),
        "low_in": (line, F32),
        "low_out": (line, F32),
        "d_low_in": (line, F32),
        "d_low_out": (line, F32),
        "dctx": ((groups * inner, tokens), BF16),
        "part": ((groups, 128, width), F32),
        "ao": ((PAD, width), BF16),
        "bo": ((PAD, width), BF16),
        "ain": ((PAD, width), BF16),
        "bout": ((PAD, width), BF16),
        "aout": ((groups, PAD, hidden), BF16),
        "core_in": ((256, width), BF16),
        "y_in": ((128, width), BF16),
        "x_in": ((64, width), BF16),
        "full": ((groups, 128, width), BF16),
        "small_out": ((896, 128), BF16),
        "small_in": ((8, 112, 128), BF16),
        "small_z": ((zs, 112, 128), BF16),
        "small_full": ((8, 112, 128), BF16),
        "b_all": ((groups, 128, inner), BF16),
        "b_in_sum": ((8, 64, inner), BF16),
        "b_z": ((zs, 64, inner), BF16),
        "b_full": ((2, 64, inner), BF16),
    }
    copies = 9 * 8 + 40 + 3 * zs
    shapes = [pltpu.VMEM(*v) for v in scratch.values()]
    shapes += [pltpu.SemaphoreType.DMA((copies,)), pltpu.SemaphoreType.DMA((copies,)), pltpu.SemaphoreType.DMA((40,))]
    names = list(ins) + list(outs) + list(scratch) + ["send", "recv", "local"]
    flops = 2 * tokens * (8 * width * hidden * groups + 24 * width * width)
    results = pl.pallas_call(
        lambda *refs: layer(names, sizes, *refs),
        name="encoder_layer",
        out_shape=[jax.ShapeDtypeStruct(o[0], o[1]) for o in outs.values()],
        in_specs=[pl.BlockSpec(memory_space=i[1]) for i in ins.values()],
        out_specs=[pl.BlockSpec(memory_space=o[2]) for o in outs.values()],
        scratch_shapes=shapes,
        cost_estimate=pl.CostEstimate(flops=flops, bytes_accessed=30 * 2**20, transcendentals=0),
        compiler_params=pltpu.CompilerParams(
            vmem_limit_bytes=VMEM_LIMIT, collective_id=0, has_side_effects=True
        ),
    )(*[i[0] for i in ins.values()])
    y, gx, g_router, g_in, g_ao, g_aout, g_bqkv, g_bo, g_bin, g_bout = pl.pallas_call(
        lambda *refs: hand_out(cols, experts, *refs),
        name="hand_out",
        out_shape=[jax.ShapeDtypeStruct(o[0], o[1]) for o in given],
        in_specs=[pl.BlockSpec(memory_space=pl.ANY)] * 2 + [pl.BlockSpec(memory_space=pltpu.VMEM)] * 4,
        out_specs=[pl.BlockSpec(memory_space=o[2]) for o in given],
        scratch_shapes=[
            pltpu.VMEM((tokens, width), BF16),
            pltpu.VMEM((tokens, width), F32),
            pltpu.SemaphoreType.DMA((10,)),
        ],
        compiler_params=pltpu.CompilerParams(vmem_limit_bytes=VMEM_LIMIT),
    )(*results[:6])
    return (
        y.reshape(layer_inputs.shape),
        gx.reshape(layer_inputs.shape),
        g_router.T,
        jnp.swapaxes(g_in, 1, 2),
        g_ao.T,
        g_aout.T,
        g_bqkv,
        g_bo,
        g_bin,
        g_bout,
    )


def solution(mesh):
    rows = P(("dp", "tensor"), None, None)
    placed = (
        rows, P(("dp", "tensor")), P(), P(), P(), P(None, None, "tensor"), P(None, "tensor"), P("tensor", None),
        P(None, "tensor"), P("tensor", None), P(), P(), P(), P(None, None, "tensor"), P(), P(None, "tensor"), P(), rows,
    )
    return jax.shard_map(
        shards,
        mesh=mesh,
        in_specs=placed,
        out_specs=(rows, rows, P(), P(), P(), P(), P(None, None, "tensor"), P(), P(None, "tensor"), P()),
        check_vma=False,
    )
```

```python
import jax
import jax.numpy as jnp
import numpy as np
from jax import lax
from jax.experimental import pallas as pl
from jax.experimental.pallas import tpu as pltpu
from jax.sharding import PartitionSpec as P

NB = 32
MAX_DIST = 128
EPS = 1e-06
NEG = -1000000000.0
LOG2E = 1.4426950408889634
F32 = jnp.float32
BF16 = jnp.bfloat16
PAD = 64
RANK_PAD = 48
VMEM_LIMIT = 63 * 1024 * 1024
MESH = pl.DeviceIdType.MESH


def filled(a, rows):
    wide = jnp.concatenate([a.astype(F32), jnp.zeros((rows - a.shape[0], a.shape[1]), F32)], axis=0)
    return wide.astype(a.dtype)


def nn(a, b):
    return lax.dot_general(a, b, (((1,), (0,)), ((), ())), preferred_element_type=F32)


def nt(a, b):
    return lax.dot_general(a, b, (((1,), (1,)), ((), ())), preferred_element_type=F32)


def tn(a, b):
    return lax.dot_general(a, b, (((0,), (0,)), ((), ())), preferred_element_type=F32)


def ds(start, size):
    return pl.ds(pl.multiple_of(start, 16), size)


def flip(index, bit):
    return index + (1 - 2 * ((index // bit) % 2)) * bit


def group_at(member, step):
    high = (member // 2 + step // 2) % 2
    low = (member % 2 + step % 2) % 2
    return 2 * high + low


class Links:
    def __init__(self, send, recv):
        self.send, self.recv, self.made = send, recv, []

    def __call__(self, src, dst, device):
        n = len(self.made)
        copy = pltpu.make_async_remote_copy(
            src_ref=src, dst_ref=dst, send_sem=self.send.at[n], recv_sem=self.recv.at[n],
            device_id=device, device_id_type=MESH,
        )
        self.made.append(copy)
        return copy


class Places:
    def __init__(self):
        d, t = lax.axis_index("dp"), lax.axis_index("tensor")
        self.d, self.t = d, t
        self.half = d % 2
        self.quarter = d % 4
        self.core_t, self.y_t = flip(t, 1), flip(t, 2)
        self.far_t = flip(self.core_t, 2)
        self.core = (d, self.core_t)
        self.y = (d, self.y_t)
        self.across = (d, self.far_t)
        self.x = (flip(d, 1), t)
        self.z = (flip(d, 2), t)


class Chunk:
    def __init__(self, links, places, own, whole, first, base, rows, over_x):
        part = rows // 4
        q = places.quarter
        qx, qz = flip(q, 1), flip(q, 2)
        qd = flip(qx, 2)
        g, g2 = places.t, places.y_t

        def at(group, quarter):
            return whole.at[ds(first(group) + base + quarter * part, part)]

        def pass_on(quarter, device):
            return links(at(g2, quarter), at(g2, quarter), device)

        self.y = links(own.at[ds(base + q * part, part)], at(g, q), places.y)
        self.one = [pass_on(q, places.x), pass_on(q, places.z), pass_on(q, places.core)]
        self.two = [pass_on(qz, places.x) if over_x else pass_on(qx, places.z)]
        self.two += [pass_on(qx, places.core), pass_on(qz, places.core)]
        self.three = pass_on(qd, places.core)

    def start(self):
        self.y.start()

    def relay(self):
        self.y.wait_recv()
        for copy in self.one:
            copy.start()

    def forward(self):
        self.one[0].wait_recv()
        self.one[1].wait_recv()
        for copy in self.two:
            copy.start()

    def close(self):
        self.two[0].wait_recv()
        self.three.start()

    def whole_here(self):
        for copy in (self.one[2], self.two[1], self.two[2], self.three):
            copy.wait_recv()


def bucket_of(relative):
    half = NB // 2
    exact = half // 2
    distance = np.abs(relative)
    scaled = np.log(np.maximum(distance, 1) / exact) / np.log(MAX_DIST / exact) * (half - exact)
    far = np.minimum(exact + scaled.astype(np.int32), half - 1)
    return ((relative > 0) * half + np.where(distance < exact, distance, far)).astype(np.int32)


def bucket_lines(seq):
    m = np.arange(2 * seq)
    rel = seq - 128 - m
    rel = np.where(rel < -seq, rel + 2 * seq, rel)
    rel = np.clip(rel, -(seq - 1), seq - 1)
    ids = bucket_of(rel)
    return (ids[None, :] == np.arange(NB)[:, None]).astype(np.float32)


SMALL = ("b_qkv", "table", "b_in", "g1", "g2", "at", "router", "onehot", "a_o", "b_o", "a_out", "b_out")


class Names:
    def __init__(self, **refs):
        self.__dict__.update(refs)


def layer(names, sizes, *refs):
    r = Names(**dict(zip(names, refs)))
    tokens, width, seq, seqs, groups, inner, heads_here, hd, hidden, cols, experts, zs = sizes
    heads = groups * heads_here
    span = 3 * hd
    rank = cols // experts
    places = Places()
    t, d, half = places.t, places.d, places.half
    z = d // 2
    links = Links(r.send, r.recv)

    r.zed = r.low_in
    r.dsmall = r.dctx.at[: 4 * PAD]
    r.d_low = [r.low_out, r.d_low_in, r.d_low_out]
    r.core_out = [r.cot.at[:128], r.cot.at[128:256]]
    r.y_out, r.x_out, r.z_out = r.cot.at[256:384], r.cot.at[384:448], r.cot.at[448:512]
    batch = min(zs, 4)
    r.z_in = r.cot.at[512 : 512 + 64 * batch]

    local = [0]

    def here(src, dst):
        local[0] += 1
        return pltpu.make_async_copy(src, dst, r.local.at[local[0] - 1])

    get_small = [here(getattr(r, n + "_far"), getattr(r, n)) for n in SMALL]
    get_x = here(r.x, r.xy)
    get_c = here(r.c, r.cot)
    get_qkv = [
        here(
            r.wqkv_own.at[p, h * hd : (h + 1) * hd],
            r.wqkv.at[ds(t * heads_here * span + h * span + p * hd, hd)],
        )
        for h in range(heads_here)
        for p in range(3)
    ]
    for copy in get_qkv:
        copy.start()
    for copy in get_small:
        copy.start()
    get_x.start()

    z_peers = [((z + i) % zs * 2 + half, t) for i in range(1, zs)]
    same_x = [(half * 4 + j, (d, j)) for j in (places.core_t, places.y_t, places.far_t)]
    other_x = [((1 - half) * 4 + j, (flip(d, 1), j)) for j in (places.core_t, places.y_t, places.far_t, t)]
    block_peers = same_x + other_x
    barrier = pltpu.get_barrier_semaphore()
    known = [dev for _, dev in block_peers] + z_peers
    for dev in known:
        pl.semaphore_signal(barrier, inc=1, device_id=dev, device_id_type=MESH)

    def quarter_of(ref, g, rows):
        return ref.at[ds(g * rows, rows)]

    def qkv_row(g):
        return g * heads_here * span

    qkv_chunks = [
        Chunk(links, places, quarter_of(r.wqkv, t, heads_here * span), r.wqkv, qkv_row, h * span, span, h % 2 == 0)
        for h in range(heads_here)
    ]
    o_chunk = Chunk(links, places, r.wo_own, r.wo, lambda g: g * inner, 0, inner, False)
    in_chunks = [
        Chunk(links, places, r.win_own, r.win_all, lambda g: g * width, j * width // 2, width // 2, j == 0)
        for j in range(2)
    ]
    out_chunks = [
        Chunk(links, places, r.wout_own, r.wout, lambda g: g * hidden, j * hidden // 2, hidden // 2, j == 1)
        for j in range(2)
    ]

    own_qkv = quarter_of(r.wqkv, t, heads_here * span)
    core_qkv = links(own_qkv, own_qkv, places.core)
    core_o = links(r.wo_own, quarter_of(r.wo, t, inner), places.core)
    core_in = links(r.win_own, quarter_of(r.win_all, t, width), places.core)
    core_out = links(r.wout_own, quarter_of(r.wout, t, hidden), places.core)
    small = [r.bq, r.rb, r.bin]
    small_y = [links(a.at[t], a.at[t], places.y) for a in small]
    small_core = [links(a.at[t], a.at[t], places.core) for a in small]
    small_far = [links(a.at[places.y_t], a.at[places.y_t], places.core) for a in small]
    keep = [
        here(r.wo_own, quarter_of(r.wo, t, inner)),
        here(r.wout_own, quarter_of(r.wout, t, hidden)),
    ]

    for copy in get_small:
        copy.wait()
    for p in range(3):
        r.bq[t, p * RANK_PAD : (p + 1) * RANK_PAD] = filled(r.b_qkv[p], RANK_PAD)
    pick = lax.broadcasted_iota(jnp.int32, (16, heads_here), 0)
    pick = pick == lax.broadcasted_iota(jnp.int32, (16, heads_here), 1)
    r.rb[t] = nn(pick.astype(F32).astype(BF16), r.table[...]).astype(BF16)
    r.bin[t] = filled(r.b_in[...], PAD)
    for copy in get_qkv:
        copy.wait()
    pl.semaphore_wait(barrier, len(known))
    qkv_chunks[0].start()
    core_qkv.start()
    small_core[0].start()
    small_core[1].start()
    qkv_chunks[1].start()
    qkv_chunks[2].start()
    o_chunk.start()
    small_y[0].start()
    small_y[1].start()
    get_c.start()
    keep[0].start()
    for p in range(3):
        r.wsm[p * PAD : (p + 1) * PAD, :] = filled(r.at[p], PAD)
    spots = lax.broadcasted_iota(jnp.int32, (PAD, experts), 0) // rank
    spots = spots == lax.broadcasted_iota(jnp.int32, (PAD, experts), 1)
    r.wsm[3 * PAD :, :] = nn(spots.astype(F32).astype(BF16), r.router[...]).astype(BF16)
    r.ao[...] = filled(r.a_o[...], PAD)
    r.bo[...] = filled(r.b_o[...], PAD)
    r.ain[...] = filled(r.at[3], PAD)
    r.bout[...] = filled(r.b_out[...], PAD)
    for j in range(groups):
        r.aout[j] = filled(r.a_out[:, j * hidden : (j + 1) * hidden], PAD)
    g1 = r.g1[...].reshape(1, width)
    g2 = r.g2[...].reshape(1, width)

    tb = 256
    get_x.wait()

    def norm(i, c):
        rows = ds(i * tb, tb)
        x = r.xy[rows, :].astype(F32)
        n1 = (x * lax.rsqrt(jnp.mean(x * x, axis=1, keepdims=True) + EPS) * g1).astype(BF16)
        r.n1[rows, :] = n1
        lines = nt(r.wsm[...], n1)
        low = lines[: 3 * PAD]
        logits = lines[3 * PAD :]
        valid = lax.broadcasted_iota(jnp.int32, logits.shape, 0) < cols
        logits = jnp.where(valid, logits, -jnp.inf)
        ex = jnp.exp(logits - jnp.max(logits, axis=0, keepdims=True))
        gate = ex / (jnp.sum(ex, axis=0, keepdims=True) * (1.0 / rank))
        r.low[:, rows] = low
        r.gate[:, rows] = gate
        for p in range(3):
            r.gated[p * PAD : (p + 1) * PAD, rows] = (low[p * PAD : (p + 1) * PAD] * gate).astype(BF16)
        return c

    lax.fori_loop(0, tokens // tb, norm, 0)

    maskrow = jnp.where(lax.broadcasted_iota(jnp.int32, (16, seq), 1) < r.lens[seqs - 1], 0.0, NEG)
    maskrow = jnp.where(lax.broadcasted_iota(jnp.int32, (16, seq), 0) == 0, maskrow, 0.0).astype(BF16)
    onerow = (lax.broadcasted_iota(jnp.int32, (16, seq), 0) == 0).astype(F32).astype(BF16)

    def head_row(n):
        return (group_at(t, n // heads_here) * heads_here + n % heads_here) * span

    def next_group(k):
        g = group_at(t, k)
        u = nn(r.rb[g], r.onehot[...]) * LOG2E
        for h in range(heads_here):
            r.urow[k * heads_here + h] = u[h : h + 1]
            for p in range(3):
                block = r.bq[g, p * RANK_PAD : (p + 1) * RANK_PAD, h * hd : (h + 1) * hd]
                r.bh[h, p * PAD : p * PAD + RANK_PAD, :] = block

    def project(n):
        row = head_row(n)
        h = n % heads_here
        out = nt(r.wqkv[ds(row, span), :], r.n1[...])
        for p in range(3):
            up = tn(r.bh[h, p * PAD : p * PAD + RANK_PAD, :], r.gated[p * PAD : p * PAD + RANK_PAD, :])
            r.qkv[ds(row + p * hd, hd), :] = (out[p * hd : (p + 1) * hd] + up).astype(BF16)

    def spread_bias(n):
        line = jnp.broadcast_to(r.urow[n], (128, 2 * seq))
        r.brow[n % 2] = pltpu.roll(line, 0, 1, stride=1, stride_axis=0)[:, : 2 * seq - 128]

    qb = 256
    parts = seq // qb

    def score_place(i):
        return slice((i % 2) * seq, (i % 2 + 1) * seq), slice((i // 2 % 3) * qb, (i // 2 % 3 + 1) * qb)

    blocks = [(s, b) for s in range(seqs) for b in range(parts)]

    def keys_of(n, s):
        row = head_row(n)
        token = slice(s * seq, (s + 1) * seq)
        q = r.qkv[ds(row, hd), token]
        k = r.qkv[ds(row + hd, hd), token].astype(F32) * LOG2E
        high = k.astype(BF16)
        keys = [high, (k - high.astype(F32)).astype(BF16)]
        queries = [q, q]
        if s > 0:
            keys.append(maskrow)
            queries.append(onerow)
        return jnp.concatenate(keys, axis=0), jnp.concatenate(queries, axis=0)

    def values_of(n):
        row = head_row(n)
        return [
            jnp.concatenate([r.qkv[ds(row + 2 * hd, hd), s * seq : (s + 1) * seq], onerow], axis=0)
            for s in range(seqs)
        ]

    def score(n, i, made):
        s, b = blocks[i]
        if b == 0:
            made[s] = keys_of(n, s)
        keys, queries = made[s]
        top = None
        rows, lanes = score_place(i)
        for kc in range(seq // 256):
            st = tn(keys[:, kc * 256 : (kc + 1) * 256], queries[:, b * qb : (b + 1) * qb])
            for kk in range(2):
                kb = kc * 2 + kk
                shift = seq - 128 - 128 * kb + b * qb
                st_b = st[kk * 128 : (kk + 1) * 128] + r.brow[n % 2, :, shift : shift + qb]
                r.acc[rows.start + kb * 128 : rows.start + (kb + 1) * 128, lanes] = st_b
                peak = jnp.max(st_b, axis=0, keepdims=True)
                top = peak if top is None else jnp.maximum(top, peak)
        return top

    def soft(n, i, top, values):
        s, b = blocks[i]
        rows, lanes = score_place(i)
        token = slice(s * seq + b * qb, s * seq + (b + 1) * qb)
        for kb in range(seq // 128):
            st = r.acc[rows.start + kb * 128 : rows.start + (kb + 1) * 128, lanes]
            r.e[n * seqs + s, kb * 128 : (kb + 1) * 128, b * qb : (b + 1) * qb] = jnp.exp2(st - top).astype(BF16)
        o = nn(values[s], r.e[n * seqs + s, :, b * qb : (b + 1) * qb])
        recip = 1.0 / o[hd : hd + 1]
        r.recip[n, :, token] = recip
        r.ctx[ds(head_row(n) // 3, hd), token] = (o[:hd] * recip).astype(BF16)

    def forward_step(step):
        if step == 0:
            qkv_chunks[0].relay()
        if step == 1:
            in_chunks[0].start()
        if step == 2:
            qkv_chunks[1].relay()
            core_qkv.wait_recv()
            small_core[0].wait_recv()
            small_core[1].wait_recv()
            core_o.start()
        if step == 3:
            qkv_chunks[2].relay()
            qkv_chunks[0].forward()
            in_chunks[1].start()
        if step == 4:
            qkv_chunks[1].forward()
        if step == 5:
            qkv_chunks[0].close()
            qkv_chunks[2].forward()
            small_y[0].wait_recv()
            small_y[1].wait_recv()
            small_far[0].start()
            small_far[1].start()
            o_chunk.relay()
        if step == 6:
            qkv_chunks[1].close()
            out_chunks[0].start()
        if step == 7:
            qkv_chunks[2].close()
            o_chunk.forward()
            in_chunks[0].relay()
            core_in.start()
            small_y[2].start()
            small_core[2].start()
        if step == 8:
            small_far[0].wait_recv()
            small_far[1].wait_recv()
            qkv_chunks[0].whole_here()
            out_chunks[1].start()
        if step == 9:
            qkv_chunks[1].whole_here()
            o_chunk.close()
            in_chunks[1].relay()
        if step == 10:
            qkv_chunks[2].whole_here()
            core_out.start()
            keep[1].start()
        if step == 11:
            in_chunks[0].forward()
            out_chunks[0].relay()

    def first_step(step):
        if step == 1:
            in_chunks[1].forward()
            out_chunks[1].relay()

    def forward_head(n, tops):
        for step in range(12):
            pl.when(n == step)(lambda step=step: forward_step(step))
        follow = jnp.minimum(n + 1, heads - 1)

        @pl.when(jnp.logical_and(follow % heads_here == 0, n < heads - 1))
        def _():
            next_group(follow // heads_here)

        values = values_of(n)
        project(follow)
        spread_bias(follow)
        made, fresh = {}, []
        behind = 2
        for i in range(len(blocks)):
            soft(n, i, tops[i], values)
            if i + 1 >= behind:
                fresh.append(score(follow, i + 1 - behind, made))
        for i in range(len(fresh), len(blocks)):
            fresh.append(score(follow, i, made))
        return tuple(fresh)

    next_group(0)
    project(0)
    spread_bias(0)
    made = {}
    lax.fori_loop(0, heads, forward_head, tuple(score(0, i, made) for i in range(len(blocks))))

    core_o.wait_recv()
    keep[0].wait()
    o_chunk.whole_here()
    get_c.wait()
    win_first = here(r.win_own, r.win.at[0])
    win_first.start()

    def first(i, c):
        pl.when(i == 1)(lambda: first_step(1))
        for j in range(2):
            rows = ds((2 * i + j) * tb, tb)
            gate = r.gate[:, rows]
            ctx = r.ctx[:, rows]
            low = nn(r.ao[...], ctx)
            r.low_o[:, rows] = low
            gated = (low * gate).astype(BF16)
            h1 = r.xy[rows, :].astype(F32) + tn(ctx, r.wo[...]) + tn(gated, r.bo[...])
            r.h1[rows, :] = h1
            n2 = (h1 * lax.rsqrt(jnp.mean(h1 * h1, axis=1, keepdims=True) + EPS) * g2).astype(BF16)
            r.n2[rows, :] = n2
            low = nt(r.ain[...], n2)
            r.low_in[:, rows] = low
            r.gin[:, rows] = (low * gate).astype(BF16)
            low = nt(r.bout[...], r.cot[rows, :])
            r.d_low_out[:, rows] = low
            r.dgo[:, rows] = (low * gate).astype(BF16)
        return c

    lax.fori_loop(0, tokens // tb // 2, first, 0)
    r.acc[...] = jnp.zeros_like(r.acc)
    r.dn2[...] = jnp.zeros_like(r.dn2)
    r.low_out[...] = jnp.zeros_like(r.low_out)
    r.d_low_in[...] = jnp.zeros_like(r.d_low_in)
    r.part[...] = jnp.zeros_like(r.part)

    wide = 512
    steps = tokens // wide
    win_next = [here(quarter_of(r.win_all, group_at(t, k), width), r.win.at[k % 2]) for k in range(1, groups)]

    def feed_step(step):
        if step == 0:
            keep[1].wait()
            win_first.wait()
            in_chunks[0].close()
            out_chunks[0].forward()
            core_in.wait_recv()
            win_next[0].start()
            small_y[2].wait_recv()
            small_far[2].start()
        if step == 1:
            in_chunks[1].close()
            out_chunks[1].forward()
        if step == 2:
            out_chunks[0].close()
            core_out.wait_recv()
            small_core[2].wait_recv()
            win_next[0].wait()
            win_next[1].start()
        if step == 3:
            out_chunks[1].close()
        if step == 4:
            for chunk in in_chunks:
                chunk.whole_here()
            win_next[1].wait()
            win_next[2].start()
        if step == 6:
            small_far[2].wait_recv()
            for chunk in out_chunks:
                chunk.whole_here()
            win_next[2].wait()

    active, d_pre = r.xy.at[:wide], r.xy.at[wide : 2 * wide]
    third = hidden // 3

    def chunk(step, c):
        for point in range(7):
            pl.when(step == point)(lambda point=point: feed_step(point))
        n = step // steps
        rows = ds((step % steps) * wide, wide)
        g = group_at(t, n)
        slot = n % 2
        gin, dgo = r.gin[:, rows], r.dgo[:, rows]
        for j in range(3):
            cs = slice(j * third, (j + 1) * third)
            pre = nn(r.n2[rows, :], r.win[slot, :, cs]) + tn(gin, r.bin[g, :, cs])
            da = nt(r.cot[rows, :], r.wout[ds(g * hidden + j * third, third), :]) + tn(dgo, r.aout[g, :, cs])
            sig = 1.0 / (1.0 + jnp.exp(-pre))
            act = pre * sig
            active[:, cs] = act.astype(BF16)
            d_pre[:, cs] = (da * (sig + act * (1.0 - sig))).astype(BF16)
        r.acc[rows, :] += nn(active[...], r.wout[ds(g * hidden, hidden), :])
        r.dn2[rows, :] += nt(d_pre[...], r.win[slot])
        r.low_out[:, rows] += nt(r.aout[g], active[...])
        r.d_low_in[:, rows] += nt(r.bin[g], d_pre[...])
        r.part[g, :cols] += nn(dgo, active[...])[:cols]
        r.part[g, 2 * cols : 3 * cols] += nn(gin, d_pre[...])[:cols]
        return c

    lax.fori_loop(0, groups * steps, chunk, 0)

    def last(i, c):
        for j in range(2):
            rows = ds((2 * i + j) * tb, tb)
            gate = r.gate[:, rows]
            cot, n2, ctx, h1 = r.cot[rows, :], r.n2[rows, :], r.ctx[:, rows], r.h1[rows, :]
            low_out, d_low_in = r.low_out[:, rows], r.d_low_in[:, rows]
            go = (low_out * gate).astype(BF16)
            r.xy[rows, :] = (h1 + r.acc[rows, :] + tn(go, r.bout[...])).astype(BF16)
            dgi = (d_low_in * gate).astype(BF16)
            up = (r.dn2[rows, :] + tn(dgi, r.ain[...])) * g2
            r.part[2, cols : 2 * cols] += nn(go, cot)[:cols]
            r.part[3, cols : 2 * cols] += nn(dgi, n2)[:cols]
            inv = lax.rsqrt(jnp.mean(h1 * h1, axis=1, keepdims=True) + EPS)
            dh = cot.astype(F32) + inv * up - h1 * (inv * inv * inv * jnp.mean(h1 * up, axis=1, keepdims=True))
            r.h1[rows, :] = dh
            da = dh.astype(BF16)
            d_low = nt(r.bo[...], da)
            low = r.low_o[:, rows]
            dgo = (d_low * gate).astype(BF16)
            r.part[1, cols : 2 * cols] += nn((low * gate).astype(BF16), da)[:cols]
            r.part[0, cols : 2 * cols] += nt(dgo, ctx)[:cols]
            r.dctx[:, rows] = (nt(r.wo[...], da) + tn(r.ao[...], dgo)).astype(BF16)
            r.zed[:, rows] = d_low * low + d_low_in * r.low_in[:, rows] + r.d_low_out[:, rows] * low_out
        return c

    lax.fori_loop(0, tokens // tb // 2, last, 0)
    put_y = here(r.xy, r.y)
    put_y.start()

    rows_half = 64
    mine, other = ds(half * rows_half, rows_half), ds((1 - half) * rows_half, rows_half)
    shared = 2 * cols
    to_core = links(r.cot.at[:256], r.core_in, places.core)
    to_y = links(r.y_out, r.y_in, places.y)
    to_x = links(r.x_out, r.x_in, places.x)
    to_z = [links(r.z_out, r.z_all.at[ds(z * 64, 64)], dev) for dev in z_peers]
    keep_z = here(r.z_out, r.z_all.at[ds(z * 64, 64)])
    get_z = [here(r.z_all.at[i * 64 : (i + batch) * 64], r.z_in) for i in range(0, zs, batch)]
    all_x = links(r.full.at[t, mine], r.full.at[t, mine], places.x)
    all_y = links(r.full.at[t, :shared], r.full.at[t, :shared], places.y)
    all_core = [
        links(r.full.at[j, :shared], r.full.at[j, :shared], places.core) for j in (t, places.y_t)
    ]
    share = r.small_in.shape[1]
    b_share = r.b_in_sum.shape[1]
    me = half * 4 + t
    give = []
    for j, dev in block_peers:
        give.append(links(r.small_out.at[ds(j * share, share)], r.small_in.at[me], dev))
    b_give = []
    for g in (t, places.core_t, places.y_t, places.far_t):
        there = [(1 - half, (flip(d, 1), g))] + ([(half, (d, g))] if b_give else [])
        b_give.append(
            [links(r.b_all.at[g, ds(h * b_share, b_share)], r.b_in_sum.at[me], dev) for h, dev in there]
        )
    cross = [links(r.small_z.at[z], r.small_z.at[z], dev) for dev in z_peers]
    b_cross = [links(r.b_z.at[z], r.b_z.at[z], dev) for dev in z_peers]
    back = [links(r.small_full.at[me], r.small_full.at[me], dev) for _, dev in block_peers]
    b_back = links(r.b_full.at[half], r.b_full.at[half], places.x)

    def sum_step(step):
        if step == 0:
            r.core_out[0][...] = r.part[places.core_t].astype(BF16)
            r.core_out[1][...] = r.part[places.far_t].astype(BF16)
            to_core.start()
        if step == 2:
            to_core.wait_recv()
            r.y_out[...] = (r.part[places.y_t] + r.core_in[128:].astype(F32)).astype(BF16)
            to_y.start()
            r.part[t] += r.core_in[:128].astype(F32)
            put_y.wait()
            get_x_again.start()
        if step == 6:
            to_y.wait_recv()
            r.part[t] += r.y_in[...].astype(F32)
            r.x_out[...] = r.part[t, other, :].astype(BF16)
            to_x.start()
        if step == 9:
            to_x.wait_recv()
            r.z_out[...] = (r.part[t, mine, :] + r.x_in[...].astype(F32)).astype(BF16)
            keep_z.start()
            for copy in to_z:
                copy.start()

    def sum_z():
        for copy in to_z:
            copy.wait_recv()
        keep_z.wait()
        total = None
        for copy in get_z:
            copy.start()
            copy.wait()
            for i in range(batch):
                term = r.z_in[i * 64 : (i + 1) * 64].astype(F32)
                total = term if total is None else total + term
        r.full[t, mine] = total.astype(BF16)
        all_x.start()

    get_x_again = here(r.x, r.xy)

    def attend_back(n):
        row = head_row(n)
        full = ds(row // 3, hd)
        blocks = [(s, b) for s in range(seqs) for b in range(parts)]
        sent, sums = {}, {}

        def ds_place(i):
            return slice((i % 2) * seq, (i % 2 + 1) * seq), slice((i // 2 % 3) * qb, (i // 2 % 3 + 1) * qb)

        def score(i):
            s, b = blocks[i]
            token = slice(s * seq + b * qb, s * seq + (b + 1) * qb)
            do = (r.dctx[full, token].astype(F32) * r.recip[n, :, token]).astype(BF16)
            delta = jnp.sum(do.astype(F32) * r.ctx[full, token].astype(F32), axis=0, keepdims=True)
            sent[i] = do
            v = r.qkv[ds(row + 2 * hd, hd), s * seq : (s + 1) * seq]
            rows, lanes = ds_place(i)
            for kc in range(seq // 256):
                keys = slice(kc * 256, (kc + 1) * 256)
                dp = tn(v[:, keys], do)
                e = r.e[n * seqs + s, keys, b * qb : (b + 1) * qb].astype(F32)
                r.n2[rows.start + kc * 256 : rows.start + (kc + 1) * 256, lanes] = (e * (dp - delta)).astype(BF16)

        def grads(i):
            s, b = blocks[i]
            token = slice(s * seq + b * qb, s * seq + (b + 1) * qb)
            whole = slice(s * seq, (s + 1) * seq)
            k = r.qkv[ds(row + hd, hd), whole]
            q = r.qkv[ds(row, hd), token]
            rows, lanes = ds_place(i)
            dsc = r.n2[rows, lanes]
            dk = nt(q, dsc)
            dv = nt(sent[i], r.e[n * seqs + s, :, b * qb : (b + 1) * qb])
            r.qkv[ds(row, hd), token] = nn(k, dsc).astype(BF16)
            if b > 0:
                dk, dv = sums[s][0] + dk, sums[s][1] + dv
            sums[s] = dk, dv
            if b == parts - 1:
                r.qkv[ds(row + hd, hd), whole] = dk.astype(BF16)
                r.qkv[ds(row + 2 * hd, hd), whole] = dv.astype(BF16)

        ahead = 2
        for i in range(ahead):
            score(i)
        for i in range(len(blocks)):
            if i + ahead < len(blocks):
                score(i + ahead)
            grads(i)

    def adapters(k):
        g = group_at(t, k)
        block = []
        for p in range(3):
            dp = [
                r.qkv[ds((g * heads_here + h) * span + p * hd, hd), :] for h in range(heads_here)
            ]
            dp = jnp.concatenate(dp, axis=0)
            r.d_low[p][:RANK_PAD, :] += nn(r.bq[g, p * RANK_PAD : (p + 1) * RANK_PAD], dp)
            block.append(nt(r.gated[p * PAD : (p + 1) * PAD, :], dp)[:cols])
        block.append(jnp.zeros((r.b_all.shape[1] - 3 * cols, inner), F32))
        r.b_all[g] = jnp.concatenate(block, axis=0).astype(BF16)
        if k < groups - 1:
            for copy in b_give[k]:
                copy.start()

    for p in range(3):
        r.d_low[p][...] = jnp.zeros(r.d_low[p].shape, F32)

    def backward_head(n, c):
        for k in range(groups - 1):
            pl.when(n == (k + 1) * heads_here)(lambda k=k: adapters(k))
        for step in (0, 2, 6, 9):
            pl.when(n == step)(lambda step=step: sum_step(step))
        attend_back(n)
        return c

    lax.fori_loop(0, heads, backward_head, 0)
    adapters(groups - 1)

    gsm = r.acc.at[: 4 * PAD]
    gate = r.gate[...]
    prod = r.zed[...]
    for p in range(3):
        part = slice(p * PAD, (p + 1) * PAD)
        prod = prod + r.d_low[p][...] * r.low[part, :]
        r.dsmall[part, :] = (r.d_low[p][...] * gate).astype(BF16)
    high = prod.astype(BF16)
    low = (prod - high.astype(F32)).astype(BF16)
    same = lax.broadcasted_iota(jnp.int32, (PAD, PAD), 0) // rank
    same = same == lax.broadcasted_iota(jnp.int32, (PAD, PAD), 1) // rank
    same = jnp.logical_and(same, lax.broadcasted_iota(jnp.int32, (PAD, PAD), 1) < cols).astype(F32).astype(BF16)
    d_gate = nn(same, high) + nn(same, low)
    d_logit = gate * (d_gate - jnp.sum(gate * prod, axis=0, keepdims=True))
    row = lax.broadcasted_iota(jnp.int32, d_logit.shape, 0)
    chosen = jnp.logical_and(row % rank == 0, row < cols)
    r.dsmall[3 * PAD :, :] = jnp.where(chosen, d_logit, 0.0).astype(BF16)
    gsm[...] = nn(r.dsmall[...], r.n1[...])
    lines = [gsm[p * PAD : p * PAD + cols, :] for p in range(3)]
    lines.append(jnp.concatenate([gsm[3 * PAD + rank * e : 3 * PAD + rank * e + 1, :] for e in range(16)], axis=0))
    count = 3 * cols + 16
    tall = -(-count // 16) * 16
    lines.append(jnp.zeros((tall - count, width), F32))
    lines = jnp.concatenate(lines, axis=0).astype(BF16)
    strips = width // 128
    for i in range(strips):
        r.small_out[i * tall : (i + 1) * tall, :] = lines[:, i * 128 : (i + 1) * 128]
    r.small_out[strips * tall :, :] = jnp.zeros((r.small_out.shape[0] - strips * tall, 128), BF16)
    for copy in give + b_give[groups - 1]:
        copy.start()
    get_x_again.wait()

    def finish(i, c):
        rows = ds(i * tb, tb)
        dn = tn(r.qkv[:, rows], r.wqkv[...]) + tn(r.dsmall[:, rows], r.wsm[...])
        x = r.xy[rows, :].astype(F32)
        inv = lax.rsqrt(jnp.mean(x * x, axis=1, keepdims=True) + EPS)
        up = dn * g1
        r.h1[rows, :] += inv * up - x * (inv * inv * inv * jnp.mean(x * up, axis=1, keepdims=True))
        return c

    part_rows = tokens // 2
    put_x = [here(r.h1.at[i * part_rows : (i + 1) * part_rows], r.gx.at[i * part_rows : (i + 1) * part_rows]) for i in range(2)]
    lax.fori_loop(0, tokens // tb // 2, finish, 0)
    put_x[0].start()
    sum_z()
    for copy in give:
        copy.wait_recv()
    r.small_in[me] = r.small_out[ds(me * share, share), :]
    total = r.small_in[0].astype(F32)
    for i in range(1, 8):
        total = total + r.small_in[i].astype(F32)
    r.small_z[z] = total.astype(BF16)
    for copy in cross:
        copy.start()
    for copies in b_give:
        for copy in copies:
            copy.wait_recv()
    r.b_in_sum[me] = r.b_all[t, ds(half * b_share, b_share), :]
    total = r.b_in_sum[0].astype(F32)
    for i in range(1, 8):
        total = total + r.b_in_sum[i].astype(F32)
    r.b_z[z] = total.astype(BF16)
    for copy in b_cross:
        copy.start()
    lax.fori_loop(tokens // tb // 2, tokens // tb, finish, 0)
    put_x[1].start()
    all_x.wait_recv()
    all_y.start()
    all_core[0].start()
    for copy in cross:
        copy.wait_recv()
    total = r.small_z[0].astype(F32)
    for i in range(1, zs):
        total = total + r.small_z[i].astype(F32)
    r.small_full[me] = total.astype(BF16)
    for copy in back:
        copy.start()
    for copy in b_cross:
        copy.wait_recv()
    total = r.b_z[0].astype(F32)
    for i in range(1, zs):
        total = total + r.b_z[i].astype(F32)
    r.b_full[half] = total.astype(BF16)
    b_back.start()
    all_y.wait_recv()
    all_core[1].start()
    for copy in all_core:
        copy.wait_recv()
    results = [here(r.full, r.full_out), here(r.full.at[t, 2 * cols :], r.own_out)]
    for copy in results:
        copy.start()
    for copy in back + [b_back]:
        copy.wait_recv()
    late = [here(r.small_full, r.small_res), here(r.b_full, r.b_res)]
    for copy in late:
        copy.start()
    for copy in results + late:
        copy.wait()
    for copy in put_x:
        copy.wait()
    for copy in links.made:
        copy.wait_send()


def hand_out(cols, experts, *refs):
    y, gx, full, own, small, b_full = refs[:6]
    y_out, gx_out, g_router, g_a_in, g_a_o, g_a_out, g_b_qkv, g_b_o, g_b_in, g_b_out = refs[6:16]
    y_buf, x_buf, sems = refs[16:]
    pieces = [(y, y_buf, y_out, 0, y.shape[0])]
    part = gx.shape[0] // 4
    pieces += [(gx, x_buf, gx_out, i * part, (i + 1) * part) for i in range(4)]
    get = [
        pltpu.make_async_copy(a.at[lo:hi], b.at[lo:hi], sems.at[i]) for i, (a, b, _, lo, hi) in enumerate(pieces)
    ]
    put = [
        pltpu.make_async_copy(b.at[lo:hi], c.at[lo:hi], sems.at[5 + i]) for i, (_, b, c, lo, hi) in enumerate(pieces)
    ]
    for copy in get:
        copy.start()
    for one, two in zip(get, put):
        one.wait()
        two.start()
    groups = full.shape[0]
    hidden = g_a_out.shape[1] // groups
    g_b_in[...] = own[...].astype(F32)[:cols]
    for j in range(groups):
        block = full[j].astype(F32)
        g_a_out[:, j * hidden : (j + 1) * hidden] = block[:cols]
        target = (g_a_o, g_b_o, g_b_out, g_a_in.at[3])[j]
        target[...] = block[cols : 2 * cols]
    count = 3 * cols + 16
    tall = -(-count // 16) * 16
    flat = small[...].reshape(small.shape[0] * small.shape[1], 128)
    for i in range(g_router.shape[1] // 128):
        block = flat[i * tall : (i + 1) * tall].astype(F32)
        lanes = slice(i * 128, (i + 1) * 128)
        for p in range(3):
            g_a_in[p, :, lanes] = block[p * cols : (p + 1) * cols]
        g_router[:, lanes] = block[3 * cols : 3 * cols + experts]
    block = b_full[...].reshape(b_full.shape[0] * b_full.shape[1], b_full.shape[2]).astype(F32)
    for p in range(3):
        g_b_qkv[p] = block[p * cols : (p + 1) * cols]
    for copy in put:
        copy.wait()


def shards(
    layer_inputs, lengths, first_gain, second_gain, router, wqkv, bias_table, wo, win, wout,
    a_in, a_o, a_out, b_qkv, b_o, b_in, b_out, cotangent,
):
    groups = lax.axis_size("tensor")
    zs = lax.axis_size("dp") // 2
    seqs, seq, width = layer_inputs.shape
    tokens = seqs * seq
    inner = wo.shape[0]
    heads_here = bias_table.shape[1]
    heads = heads_here * groups
    hd = inner // heads_here
    hidden = win.shape[1]
    experts = router.shape[1]
    cols = a_in.shape[2]
    sizes = (tokens, width, seq, seqs, groups, inner, heads_here, hd, hidden, cols, experts, zs)
    ins = {
        "lens": (lengths, pltpu.SMEM),
        "g1": (first_gain, pl.ANY),
        "g2": (second_gain, pl.ANY),
        "at": (jnp.swapaxes(a_in, 1, 2), pl.ANY),
        "router": (router.T, pl.ANY),
        "onehot": (jnp.asarray(bucket_lines(seq), BF16), pl.ANY),
        "b_qkv": (b_qkv, pl.ANY),
        "table": (bias_table.T, pl.ANY),
        "b_in": (b_in, pl.ANY),
        "a_o": (a_o.T, pl.ANY),
        "b_o": (b_o, pl.ANY),
        "a_out": (a_out.T, pl.ANY),
        "b_out": (b_out, pl.ANY),
        "x": (layer_inputs.reshape(tokens, width), pl.ANY),
        "c": (cotangent.reshape(tokens, width), pl.ANY),
        "wqkv_own": (jnp.swapaxes(wqkv, 1, 2), pl.ANY),
        "wo_own": (wo, pl.ANY),
        "win_own": (win, pl.ANY),
        "wout_own": (wout, pl.ANY),
    }
    landing = {n: (ins[n][0].shape, ins[n][0].dtype) for n in SMALL}
    ins = {n + "_far" if n in SMALL else n: v for n, v in ins.items()}
    outs = {
        "y": ((tokens, width), BF16, pl.ANY),
        "gx": ((tokens, width), F32, pl.ANY),
        "full_out": ((groups, 128, width), BF16, pl.ANY),
        "own_out": ((128 - 2 * cols, width), BF16, pl.ANY),
        "small_res": ((8, 112, 128), BF16, pl.ANY),
        "b_res": ((2, 64, inner), BF16, pl.ANY),
        "win_all": ((groups * width, hidden), BF16, pl.ANY),
        "z_all": ((zs * 64, width), BF16, pl.ANY),
    }
    given = [
        ((tokens, width), BF16, pl.ANY),
        ((tokens, width), F32, pl.ANY),
        ((experts, width), F32, pltpu.VMEM),
        ((4, cols, width), F32, pltpu.VMEM),
        ((cols, width), F32, pltpu.VMEM),
        ((cols, groups * hidden), F32, pltpu.VMEM),
        ((3, cols, inner), F32, pltpu.VMEM),
        ((cols, width), F32, pltpu.VMEM),
        ((cols, hidden), F32, pltpu.VMEM),
        ((cols, width), F32, pltpu.VMEM),
    ]
    line = (PAD, tokens)
    scratch = {
        "xy": ((tokens, width), BF16),
        "cot": ((tokens, width), BF16),
        "n1": ((tokens, width), BF16),
        "low": ((3 * PAD, tokens), F32),
        "gate": (line, F32),
        "gated": ((3 * PAD, tokens), BF16),
        "wqkv": ((3 * groups * inner, width), BF16),
        "qkv": ((3 * groups * inner, tokens), BF16),
        "e": ((heads * seqs, seq, seq), BF16),
        "recip": ((heads, 1, tokens), F32),
        "ctx": ((groups * inner, tokens), BF16),
        "wsm": ((4 * PAD, width), BF16),
        "bq": ((groups, 3 * RANK_PAD, inner), BF16),
        "bh": ((heads_here, 3 * PAD, hd), BF16),
        "rb": ((groups, 16, NB), BF16),
        "bin": ((groups, PAD, hidden), BF16),
        "urow": ((heads, 1, 2 * seq), F32),
        "brow": ((2, 128, 2 * seq - 128), F32),
        "wo": ((groups * inner, width), BF16),
        "win": ((2, width, hidden), BF16),
        "wout": ((groups * hidden, width), BF16),
        "h1": ((tokens, width), F32),
        "n2": ((tokens, width), BF16),
        "acc": ((tokens, width), F32),
        "dn2": ((tokens, width), F32),
        "gin": (line, BF16),
        "dgo": (line, BF16),
        "low_o": (line, F32),
        "low_in": (line, F32),
        "low_out": (line, F32),
        "d_low_in": (line, F32),
        "d_low_out": (line, F32),
        "dctx": ((groups * inner, tokens), BF16),
        "part": ((groups, 128, width), F32),
        "ao": ((PAD, width), BF16),
        "bo": ((PAD, width), BF16),
        "ain": ((PAD, width), BF16),
        "bout": ((PAD, width), BF16),
        "aout": ((groups, PAD, hidden), BF16),
        "core_in": ((256, width), BF16),
        "y_in": ((128, width), BF16),
        "x_in": ((64, width), BF16),
        "full": ((groups, 128, width), BF16),
        "small_out": ((896, 128), BF16),
        "small_in": ((8, 112, 128), BF16),
        "small_z": ((zs, 112, 128), BF16),
        "small_full": ((8, 112, 128), BF16),
        "b_all": ((groups, 128, inner), BF16),
        "b_in_sum": ((8, 64, inner), BF16),
        "b_z": ((zs, 64, inner), BF16),
        "b_full": ((2, 64, inner), BF16),
    }
    scratch.update(landing)
    copies = 9 * 8 + 40 + 3 * zs
    shapes = [pltpu.VMEM(*v) for v in scratch.values()]
    shapes += [pltpu.SemaphoreType.DMA((copies,)), pltpu.SemaphoreType.DMA((copies,)), pltpu.SemaphoreType.DMA((64,))]
    names = list(ins) + list(outs) + list(scratch) + ["send", "recv", "local"]
    flops = 2 * tokens * (8 * width * hidden * groups + 24 * width * width)
    results = pl.pallas_call(
        lambda *refs: layer(names, sizes, *refs),
        name="encoder_layer",
        out_shape=[jax.ShapeDtypeStruct(o[0], o[1]) for o in outs.values()],
        in_specs=[pl.BlockSpec(memory_space=i[1]) for i in ins.values()],
        out_specs=[pl.BlockSpec(memory_space=o[2]) for o in outs.values()],
        scratch_shapes=shapes,
        cost_estimate=pl.CostEstimate(flops=flops, bytes_accessed=30 * 2**20, transcendentals=0),
        compiler_params=pltpu.CompilerParams(
            vmem_limit_bytes=VMEM_LIMIT, collective_id=0, has_side_effects=True
        ),
    )(*[i[0] for i in ins.values()])
    y, gx, g_router, g_in, g_ao, g_aout, g_bqkv, g_bo, g_bin, g_bout = pl.pallas_call(
        lambda *refs: hand_out(cols, experts, *refs),
        name="hand_out",
        out_shape=[jax.ShapeDtypeStruct(o[0], o[1]) for o in given],
        in_specs=[pl.BlockSpec(memory_space=pl.ANY)] * 2 + [pl.BlockSpec(memory_space=pltpu.VMEM)] * 4,
        out_specs=[pl.BlockSpec(memory_space=o[2]) for o in given],
        scratch_shapes=[
            pltpu.VMEM((tokens, width), BF16),
            pltpu.VMEM((tokens, width), F32),
            pltpu.SemaphoreType.DMA((10,)),
        ],
        compiler_params=pltpu.CompilerParams(vmem_limit_bytes=VMEM_LIMIT),
    )(*results[:6])
    return (
        y.reshape(layer_inputs.shape),
        gx.reshape(layer_inputs.shape),
        g_router.T,
        jnp.swapaxes(g_in, 1, 2),
        g_ao.T,
        g_aout.T,
        g_bqkv,
        g_bo,
        g_bin,
        g_bout,
    )


def solution(mesh):
    rows = P(("dp", "tensor"), None, None)
    placed = (
        rows, P(("dp", "tensor")), P(), P(), P(), P(None, None, "tensor"), P(None, "tensor"), P("tensor", None),
        P(None, "tensor"), P("tensor", None), P(), P(), P(), P(None, None, "tensor"), P(), P(None, "tensor"), P(), rows,
    )
    return jax.shard_map(
        shards,
        mesh=mesh,
        in_specs=placed,
        out_specs=(rows, rows, P(), P(), P(), P(), P(None, None, "tensor"), P(), P(None, "tensor"), P()),
        check_vma=False,
    )
```

```python
import jax
import jax.numpy as jnp
import numpy as np
from jax import lax
from jax.experimental import pallas as pl
from jax.experimental.pallas import tpu as pltpu
from jax.sharding import PartitionSpec as P

NB = 32
MAX_DIST = 128
EPS = 1e-06
NEG = -1000000000.0
LOG2E = 1.4426950408889634
F32 = jnp.float32
BF16 = jnp.bfloat16
PAD = 64
RANK_PAD = 48
VMEM_LIMIT = 63 * 1024 * 1024
MESH = pl.DeviceIdType.MESH


def filled(a, rows):
    wide = jnp.concatenate([a.astype(F32), jnp.zeros((rows - a.shape[0], a.shape[1]), F32)], axis=0)
    return wide.astype(a.dtype)


def nn(a, b):
    return lax.dot_general(a, b, (((1,), (0,)), ((), ())), preferred_element_type=F32)


def nt(a, b):
    return lax.dot_general(a, b, (((1,), (1,)), ((), ())), preferred_element_type=F32)


def tn(a, b):
    return lax.dot_general(a, b, (((0,), (0,)), ((), ())), preferred_element_type=F32)


def ds(start, size):
    return pl.ds(pl.multiple_of(start, 16), size)


def flip(index, bit):
    return index + (1 - 2 * ((index // bit) % 2)) * bit


def group_at(member, step):
    high = (member // 2 + step // 2) % 2
    low = (member % 2 + step % 2) % 2
    return 2 * high + low


class Links:
    def __init__(self, send, recv):
        self.send, self.recv, self.made = send, recv, []

    def __call__(self, src, dst, device):
        n = len(self.made)
        copy = pltpu.make_async_remote_copy(
            src_ref=src, dst_ref=dst, send_sem=self.send.at[n], recv_sem=self.recv.at[n],
            device_id=device, device_id_type=MESH,
        )
        self.made.append(copy)
        return copy


class Places:
    def __init__(self):
        d, t = lax.axis_index("dp"), lax.axis_index("tensor")
        self.d, self.t = d, t
        self.half = d % 2
        self.quarter = d % 4
        self.core_t, self.y_t = flip(t, 1), flip(t, 2)
        self.far_t = flip(self.core_t, 2)
        self.core = (d, self.core_t)
        self.y = (d, self.y_t)
        self.across = (d, self.far_t)
        self.x = (flip(d, 1), t)
        self.z = (flip(d, 2), t)


class Chunk:
    def __init__(self, links, places, own, whole, first, base, rows, over_x):
        part = rows // 4
        q = places.quarter
        qx, qz = flip(q, 1), flip(q, 2)
        qd = flip(qx, 2)
        g, g2 = places.t, places.y_t

        def at(group, quarter):
            return whole.at[ds(first(group) + base + quarter * part, part)]

        def pass_on(quarter, device):
            return links(at(g2, quarter), at(g2, quarter), device)

        self.y = links(own.at[ds(base + q * part, part)], at(g, q), places.y)
        self.one = [pass_on(q, places.x), pass_on(q, places.z), pass_on(q, places.core)]
        self.two = [pass_on(qz, places.x) if over_x else pass_on(qx, places.z)]
        self.two += [pass_on(qx, places.core), pass_on(qz, places.core)]
        self.three = pass_on(qd, places.core)

    def start(self):
        self.y.start()

    def relay(self):
        self.y.wait_recv()
        for copy in self.one:
            copy.start()

    def forward(self):
        self.one[0].wait_recv()
        self.one[1].wait_recv()
        for copy in self.two:
            copy.start()

    def close(self):
        self.two[0].wait_recv()
        self.three.start()

    def whole_here(self):
        for copy in (self.one[2], self.two[1], self.two[2], self.three):
            copy.wait_recv()


def bucket_of(relative):
    half = NB // 2
    exact = half // 2
    distance = np.abs(relative)
    scaled = np.log(np.maximum(distance, 1) / exact) / np.log(MAX_DIST / exact) * (half - exact)
    far = np.minimum(exact + scaled.astype(np.int32), half - 1)
    return ((relative > 0) * half + np.where(distance < exact, distance, far)).astype(np.int32)


def bucket_lines(seq):
    m = np.arange(2 * seq)
    rel = seq - 128 - m
    rel = np.where(rel < -seq, rel + 2 * seq, rel)
    rel = np.clip(rel, -(seq - 1), seq - 1)
    ids = bucket_of(rel)
    return (ids[None, :] == np.arange(NB)[:, None]).astype(np.float32)


SMALL = ("b_qkv", "table", "b_in", "g1", "g2", "at", "router", "onehot", "a_o", "b_o", "a_out", "b_out")


class Names:
    def __init__(self, **refs):
        self.__dict__.update(refs)


def layer(names, sizes, *refs):
    r = Names(**dict(zip(names, refs)))
    tokens, width, seq, seqs, groups, inner, heads_here, hd, hidden, cols, experts, zs = sizes
    heads = groups * heads_here
    span = 3 * hd
    rank = cols // experts
    places = Places()
    t, d, half = places.t, places.d, places.half
    z = d // 2
    links = Links(r.send, r.recv)

    r.zed = r.low_in
    r.dsmall = r.dctx.at[: 4 * PAD]
    r.d_low = [r.low_out, r.d_low_in, r.d_low_out]
    r.core_out = [r.cot.at[:128], r.cot.at[128:256]]
    r.y_out, r.x_out, r.z_out = r.cot.at[256:384], r.cot.at[384:448], r.cot.at[448:512]
    batch = min(zs, 4)
    r.z_in = r.cot.at[512 : 512 + 64 * batch]

    local = [0]

    def here(src, dst):
        local[0] += 1
        return pltpu.make_async_copy(src, dst, r.local.at[local[0] - 1])

    get_small = [here(getattr(r, n + "_far"), getattr(r, n)) for n in SMALL]
    get_x = here(r.x, r.xy)
    get_c = here(r.c, r.cot)
    get_qkv = [
        here(
            r.wqkv_own.at[p, h * hd : (h + 1) * hd],
            r.wqkv.at[ds(t * heads_here * span + h * span + p * hd, hd)],
        )
        for h in range(heads_here)
        for p in range(3)
    ]
    for copy in get_qkv:
        copy.start()
    for copy in get_small:
        copy.start()
    get_x.start()

    z_peers = [((z + i) % zs * 2 + half, t) for i in range(1, zs)]
    same_x = [(half * 4 + j, (d, j)) for j in (places.core_t, places.y_t, places.far_t)]
    other_x = [((1 - half) * 4 + j, (flip(d, 1), j)) for j in (places.core_t, places.y_t, places.far_t, t)]
    block_peers = same_x + other_x
    barrier = pltpu.get_barrier_semaphore()
    known = [dev for _, dev in block_peers] + z_peers
    for dev in known:
        pl.semaphore_signal(barrier, inc=1, device_id=dev, device_id_type=MESH)

    def quarter_of(ref, g, rows):
        return ref.at[ds(g * rows, rows)]

    def qkv_row(g):
        return g * heads_here * span

    qkv_chunks = [
        Chunk(links, places, quarter_of(r.wqkv, t, heads_here * span), r.wqkv, qkv_row, h * span, span, h % 2 == 0)
        for h in range(heads_here)
    ]
    o_chunk = Chunk(links, places, r.wo_own, r.wo, lambda g: g * inner, 0, inner, False)
    in_chunks = [
        Chunk(links, places, r.win_own, r.win_all, lambda g: g * width, j * width // 2, width // 2, j == 0)
        for j in range(2)
    ]
    out_chunks = [
        Chunk(links, places, r.wout_own, r.wout, lambda g: g * hidden, j * hidden // 2, hidden // 2, j == 1)
        for j in range(2)
    ]

    own_qkv = quarter_of(r.wqkv, t, heads_here * span)
    core_qkv = links(own_qkv, own_qkv, places.core)
    core_o = links(r.wo_own, quarter_of(r.wo, t, inner), places.core)
    core_in = links(r.win_own, quarter_of(r.win_all, t, width), places.core)
    core_out = links(r.wout_own, quarter_of(r.wout, t, hidden), places.core)
    small = [r.bq, r.rb, r.bin]
    small_y = [links(a.at[t], a.at[t], places.y) for a in small]
    small_core = [links(a.at[t], a.at[t], places.core) for a in small]
    small_far = [links(a.at[places.y_t], a.at[places.y_t], places.core) for a in small]
    keep = [
        here(r.wo_own, quarter_of(r.wo, t, inner)),
        here(r.wout_own, quarter_of(r.wout, t, hidden)),
    ]

    for copy in get_small:
        copy.wait()
    for p in range(3):
        r.bq[t, p * RANK_PAD : (p + 1) * RANK_PAD] = filled(r.b_qkv[p], RANK_PAD)
    pick = lax.broadcasted_iota(jnp.int32, (16, heads_here), 0)
    pick = pick == lax.broadcasted_iota(jnp.int32, (16, heads_here), 1)
    r.rb[t] = nn(pick.astype(F32).astype(BF16), r.table[...]).astype(BF16)
    r.bin[t] = filled(r.b_in[...], PAD)
    for copy in get_qkv:
        copy.wait()
    pl.semaphore_wait(barrier, len(known))
    qkv_chunks[0].start()
    core_qkv.start()
    small_core[0].start()
    small_core[1].start()
    qkv_chunks[1].start()
    qkv_chunks[2].start()
    o_chunk.start()
    small_y[0].start()
    small_y[1].start()
    get_c.start()
    keep[0].start()
    for p in range(3):
        r.wsm[p * PAD : (p + 1) * PAD, :] = filled(r.at[p], PAD)
    spots = lax.broadcasted_iota(jnp.int32, (PAD, experts), 0) // rank
    spots = spots == lax.broadcasted_iota(jnp.int32, (PAD, experts), 1)
    r.wsm[3 * PAD :, :] = nn(spots.astype(F32).astype(BF16), r.router[...]).astype(BF16)
    r.ao[...] = filled(r.a_o[...], PAD)
    r.bo[...] = filled(r.b_o[...], PAD)
    r.ain[...] = filled(r.at[3], PAD)
    r.bout[...] = filled(r.b_out[...], PAD)
    for j in range(groups):
        r.aout[j] = filled(r.a_out[:, j * hidden : (j + 1) * hidden], PAD)
    g1 = r.g1[...].reshape(1, width)
    g2 = r.g2[...].reshape(1, width)

    tb = 256
    get_x.wait()

    def norm(i, c):
        rows = ds(i * tb, tb)
        x = r.xy[rows, :].astype(F32)
        n1 = (x * lax.rsqrt(jnp.mean(x * x, axis=1, keepdims=True) + EPS) * g1).astype(BF16)
        r.n1[rows, :] = n1
        lines = nt(r.wsm[...], n1)
        low = lines[: 3 * PAD]
        logits = lines[3 * PAD :]
        valid = lax.broadcasted_iota(jnp.int32, logits.shape, 0) < cols
        logits = jnp.where(valid, logits, -jnp.inf)
        ex = jnp.exp(logits - jnp.max(logits, axis=0, keepdims=True))
        gate = ex / (jnp.sum(ex, axis=0, keepdims=True) * (1.0 / rank))
        r.low[:, rows] = low
        r.gate[:, rows] = gate
        for p in range(3):
            r.gated[p * PAD : (p + 1) * PAD, rows] = (low[p * PAD : (p + 1) * PAD] * gate).astype(BF16)
        return c

    lax.fori_loop(0, tokens // tb, norm, 0)

    maskrow = jnp.where(lax.broadcasted_iota(jnp.int32, (16, seq), 1) < r.lens[seqs - 1], 0.0, NEG)
    maskrow = jnp.where(lax.broadcasted_iota(jnp.int32, (16, seq), 0) == 0, maskrow, 0.0).astype(BF16)
    onerow = (lax.broadcasted_iota(jnp.int32, (16, seq), 0) == 0).astype(F32).astype(BF16)

    def head_row(n):
        return (group_at(t, n // heads_here) * heads_here + n % heads_here) * span

    def next_group(k):
        g = group_at(t, k)
        u = nn(r.rb[g], r.onehot[...]) * LOG2E
        for h in range(heads_here):
            r.urow[k * heads_here + h] = u[h : h + 1]
            for p in range(3):
                block = r.bq[g, p * RANK_PAD : (p + 1) * RANK_PAD, h * hd : (h + 1) * hd]
                r.bh[h, p * PAD : p * PAD + RANK_PAD, :] = block

    def project(n):
        row = head_row(n)
        h = n % heads_here
        out = nt(r.wqkv[ds(row, span), :], r.n1[...])
        for p in range(3):
            up = tn(r.bh[h, p * PAD : p * PAD + RANK_PAD, :], r.gated[p * PAD : p * PAD + RANK_PAD, :])
            r.qkv[ds(row + p * hd, hd), :] = (out[p * hd : (p + 1) * hd] + up).astype(BF16)

    def spread_bias(n):
        line = jnp.broadcast_to(r.urow[n], (128, 2 * seq))
        r.brow[n % 2] = pltpu.roll(line, 0, 1, stride=1, stride_axis=0)[:, : 2 * seq - 128]

    qb = 256
    parts = seq // qb

    def score_place(i):
        return slice((i % 2) * seq, (i % 2 + 1) * seq), slice((i // 2 % 3) * qb, (i // 2 % 3 + 1) * qb)

    blocks = [(s, b) for s in range(seqs) for b in range(parts)]

    def keys_of(n, s):
        row = head_row(n)
        token = slice(s * seq, (s + 1) * seq)
        q = r.qkv[ds(row, hd), token]
        k = r.qkv[ds(row + hd, hd), token].astype(F32) * LOG2E
        high = k.astype(BF16)
        keys = [high, (k - high.astype(F32)).astype(BF16)]
        queries = [q, q]
        if s > 0:
            keys.append(maskrow)
            queries.append(onerow)
        return jnp.concatenate(keys, axis=0), jnp.concatenate(queries, axis=0)

    def values_of(n):
        row = head_row(n)
        return [
            jnp.concatenate([r.qkv[ds(row + 2 * hd, hd), s * seq : (s + 1) * seq], onerow], axis=0)
            for s in range(seqs)
        ]

    def score(n, i, made):
        s, b = blocks[i]
        if b == 0:
            made[s] = keys_of(n, s)
        keys, queries = made[s]
        top = None
        rows, lanes = score_place(i)
        for kc in range(seq // 256):
            st = tn(keys[:, kc * 256 : (kc + 1) * 256], queries[:, b * qb : (b + 1) * qb])
            for kk in range(2):
                kb = kc * 2 + kk
                shift = seq - 128 - 128 * kb + b * qb
                st_b = st[kk * 128 : (kk + 1) * 128] + r.brow[n % 2, :, shift : shift + qb]
                r.acc[rows.start + kb * 128 : rows.start + (kb + 1) * 128, lanes] = st_b
                peak = jnp.max(st_b, axis=0, keepdims=True)
                top = peak if top is None else jnp.maximum(top, peak)
        return top

    def soft(n, i, top, values):
        s, b = blocks[i]
        rows, lanes = score_place(i)
        token = slice(s * seq + b * qb, s * seq + (b + 1) * qb)
        for kb in range(seq // 128):
            st = r.acc[rows.start + kb * 128 : rows.start + (kb + 1) * 128, lanes]
            r.e[n * seqs + s, kb * 128 : (kb + 1) * 128, b * qb : (b + 1) * qb] = jnp.exp2(st - top).astype(BF16)
        o = nn(values[s], r.e[n * seqs + s, :, b * qb : (b + 1) * qb])
        recip = 1.0 / o[hd : hd + 1]
        r.recip[n, :, token] = recip
        r.ctx[ds(head_row(n) // 3, hd), token] = (o[:hd] * recip).astype(BF16)

    def forward_step(step):
        if step == 0:
            qkv_chunks[0].relay()
        if step == 1:
            qkv_chunks[1].relay()
            in_chunks[0].start()
        if step == 2:
            qkv_chunks[2].relay()
            core_qkv.wait_recv()
            small_core[0].wait_recv()
            small_core[1].wait_recv()
            core_o.start()
        if step == 3:
            qkv_chunks[0].forward()
            in_chunks[1].start()
        if step == 4:
            qkv_chunks[1].forward()
        if step == 5:
            qkv_chunks[0].close()
            qkv_chunks[2].forward()
            small_y[0].wait_recv()
            small_y[1].wait_recv()
            small_far[0].start()
            small_far[1].start()
            o_chunk.relay()
        if step == 6:
            qkv_chunks[1].close()
            out_chunks[0].start()
        if step == 7:
            qkv_chunks[2].close()
            o_chunk.forward()
            in_chunks[0].relay()
            core_in.start()
            small_y[2].start()
            small_core[2].start()
        if step == 8:
            small_far[0].wait_recv()
            small_far[1].wait_recv()
            qkv_chunks[0].whole_here()
            out_chunks[1].start()
        if step == 9:
            qkv_chunks[1].whole_here()
            o_chunk.close()
            in_chunks[1].relay()
        if step == 10:
            qkv_chunks[2].whole_here()
            core_out.start()
            keep[1].start()
        if step == 11:
            in_chunks[0].forward()
            out_chunks[0].relay()

    def first_step(step):
        if step == 1:
            in_chunks[1].forward()
            out_chunks[1].relay()

    def forward_head(n, tops):
        for step in range(12):
            pl.when(n == step)(lambda step=step: forward_step(step))
        follow = jnp.minimum(n + 1, heads - 1)

        @pl.when(jnp.logical_and(follow % heads_here == 0, n < heads - 1))
        def _():
            next_group(follow // heads_here)

        values = values_of(n)
        project(follow)
        spread_bias(follow)
        made, fresh = {}, []
        behind = 2
        for i in range(len(blocks)):
            soft(n, i, tops[i], values)
            if i + 1 >= behind:
                fresh.append(score(follow, i + 1 - behind, made))
        for i in range(len(fresh), len(blocks)):
            fresh.append(score(follow, i, made))
        return tuple(fresh)

    next_group(0)
    project(0)
    spread_bias(0)
    made = {}
    lax.fori_loop(0, heads, forward_head, tuple(score(0, i, made) for i in range(len(blocks))))

    core_o.wait_recv()
    keep[0].wait()
    o_chunk.whole_here()
    get_c.wait()
    win_first = here(r.win_own, r.win.at[0])
    win_first.start()

    def first(i, c):
        pl.when(i == 1)(lambda: first_step(1))
        for j in range(2):
            rows = ds((2 * i + j) * tb, tb)
            gate = r.gate[:, rows]
            ctx = r.ctx[:, rows]
            low = nn(r.ao[...], ctx)
            r.low_o[:, rows] = low
            gated = (low * gate).astype(BF16)
            h1 = r.xy[rows, :].astype(F32) + tn(ctx, r.wo[...]) + tn(gated, r.bo[...])
            r.h1[rows, :] = h1
            r.acc[rows, :] = h1
            r.dn2[rows, :] = jnp.zeros_like(h1)
            n2 = (h1 * lax.rsqrt(jnp.mean(h1 * h1, axis=1, keepdims=True) + EPS) * g2).astype(BF16)
            r.n2[rows, :] = n2
            low = nt(r.ain[...], n2)
            r.low_in[:, rows] = low
            r.gin[:, rows] = (low * gate).astype(BF16)
            low = nt(r.bout[...], r.cot[rows, :])
            r.d_low_out[:, rows] = low
            r.dgo[:, rows] = (low * gate).astype(BF16)
        return c

    lax.fori_loop(0, tokens // tb // 2, first, 0)
    r.low_out[...] = jnp.zeros_like(r.low_out)
    r.d_low_in[...] = jnp.zeros_like(r.d_low_in)
    r.part[...] = jnp.zeros_like(r.part)

    wide = 512
    steps = tokens // wide
    win_next = [here(quarter_of(r.win_all, group_at(t, k), width), r.win.at[k % 2]) for k in range(1, groups)]

    def feed_step(step):
        if step == 0:
            keep[1].wait()
            win_first.wait()
            in_chunks[0].close()
            out_chunks[0].forward()
            core_in.wait_recv()
            win_next[0].start()
            small_y[2].wait_recv()
            small_far[2].start()
        if step == 1:
            in_chunks[1].close()
            out_chunks[1].forward()
        if step == 2:
            out_chunks[0].close()
            core_out.wait_recv()
            small_core[2].wait_recv()
            win_next[0].wait()
            win_next[1].start()
        if step == 3:
            out_chunks[1].close()
        if step == 4:
            for chunk in in_chunks:
                chunk.whole_here()
            win_next[1].wait()
            win_next[2].start()
        if step == 6:
            small_far[2].wait_recv()
            for chunk in out_chunks:
                chunk.whole_here()
            win_next[2].wait()

    active, d_pre = r.xy.at[:wide], r.xy.at[wide : 2 * wide]
    third = hidden // 3

    def chunk(step, c):
        for point in range(7):
            pl.when(step == point)(lambda point=point: feed_step(point))
        n = step // steps
        rows = ds((step % steps) * wide, wide)
        g = group_at(t, n)
        slot = n % 2
        gin, dgo = r.gin[:, rows], r.dgo[:, rows]
        for j in range(3):
            cs = slice(j * third, (j + 1) * third)
            pre = nn(r.n2[rows, :], r.win[slot, :, cs]) + tn(gin, r.bin[g, :, cs])
            da = nt(r.cot[rows, :], r.wout[ds(g * hidden + j * third, third), :]) + tn(dgo, r.aout[g, :, cs])
            sig = 1.0 / (1.0 + jnp.exp(-pre))
            act = pre * sig
            active[:, cs] = act.astype(BF16)
            d_pre[:, cs] = (da * (sig + act * (1.0 - sig))).astype(BF16)
        r.acc[rows, :] += nn(active[...], r.wout[ds(g * hidden, hidden), :])
        r.dn2[rows, :] += nt(d_pre[...], r.win[slot])
        r.low_out[:, rows] += nt(r.aout[g], active[...])
        r.d_low_in[:, rows] += nt(r.bin[g], d_pre[...])
        r.part[g, :cols] += nn(dgo, active[...])[:cols]
        r.part[g, 2 * cols : 3 * cols] += nn(gin, d_pre[...])[:cols]
        return c

    lax.fori_loop(0, groups * steps, chunk, 0)

    def last(i, c):
        for j in range(2):
            rows = ds((2 * i + j) * tb, tb)
            gate = r.gate[:, rows]
            cot, n2, ctx, h1 = r.cot[rows, :], r.n2[rows, :], r.ctx[:, rows], r.h1[rows, :]
            low_out, d_low_in = r.low_out[:, rows], r.d_low_in[:, rows]
            go = (low_out * gate).astype(BF16)
            r.xy[rows, :] = (r.acc[rows, :] + tn(go, r.bout[...])).astype(BF16)
            dgi = (d_low_in * gate).astype(BF16)
            up = (r.dn2[rows, :] + tn(dgi, r.ain[...])) * g2
            r.part[2, cols : 2 * cols] += nn(go, cot)[:cols]
            r.part[3, cols : 2 * cols] += nn(dgi, n2)[:cols]
            inv = lax.rsqrt(jnp.mean(h1 * h1, axis=1, keepdims=True) + EPS)
            dh = cot.astype(F32) + inv * up - h1 * (inv * inv * inv * jnp.mean(h1 * up, axis=1, keepdims=True))
            r.h1[rows, :] = dh
            da = dh.astype(BF16)
            d_low = nt(r.bo[...], da)
            low = r.low_o[:, rows]
            dgo = (d_low * gate).astype(BF16)
            r.part[1, cols : 2 * cols] += nn((low * gate).astype(BF16), da)[:cols]
            r.part[0, cols : 2 * cols] += nt(dgo, ctx)[:cols]
            r.dctx[:, rows] = (nt(r.wo[...], da) + tn(r.ao[...], dgo)).astype(BF16)
            r.zed[:, rows] = d_low * low + d_low_in * r.low_in[:, rows] + r.d_low_out[:, rows] * low_out
        return c

    lax.fori_loop(0, tokens // tb // 2, last, 0)
    put_y = here(r.xy, r.y)
    put_y.start()

    rows_half = 64
    mine, other = ds(half * rows_half, rows_half), ds((1 - half) * rows_half, rows_half)
    shared = 2 * cols
    to_core = links(r.cot.at[:256], r.core_in, places.core)
    to_y = links(r.y_out, r.y_in, places.y)
    to_x = links(r.x_out, r.x_in, places.x)
    to_z = [links(r.z_out, r.z_all.at[ds(z * 64, 64)], dev) for dev in z_peers]
    keep_z = here(r.z_out, r.z_all.at[ds(z * 64, 64)])
    get_z = [here(r.z_all.at[i * 64 : (i + batch) * 64], r.z_in) for i in range(0, zs, batch)]
    all_x = links(r.full.at[t, mine], r.full.at[t, mine], places.x)
    all_y = links(r.full.at[t, :shared], r.full.at[t, :shared], places.y)
    all_core = [
        links(r.full.at[j, :shared], r.full.at[j, :shared], places.core) for j in (t, places.y_t)
    ]
    share = r.small_in.shape[1]
    b_share = r.b_in_sum.shape[1]
    me = half * 4 + t
    give = []
    for j, dev in block_peers:
        give.append(links(r.small_out.at[ds(j * share, share)], r.small_in.at[me], dev))
    b_give = []
    for g in (t, places.core_t, places.y_t, places.far_t):
        there = [(1 - half, (flip(d, 1), g))] + ([(half, (d, g))] if b_give else [])
        b_give.append(
            [links(r.b_all.at[g, ds(h * b_share, b_share)], r.b_in_sum.at[me], dev) for h, dev in there]
        )
    cross = [links(r.small_z.at[z], r.small_z.at[z], dev) for dev in z_peers]
    b_cross = [links(r.b_z.at[z], r.b_z.at[z], dev) for dev in z_peers]
    back = [links(r.small_full.at[me], r.small_full.at[me], dev) for _, dev in block_peers]
    b_back = links(r.b_full.at[half], r.b_full.at[half], places.x)

    def sum_step(step):
        if step == 0:
            r.core_out[0][...] = r.part[places.core_t].astype(BF16)
            r.core_out[1][...] = r.part[places.far_t].astype(BF16)
            to_core.start()
        if step == 2:
            to_core.wait_recv()
            r.y_out[...] = (r.part[places.y_t] + r.core_in[128:].astype(F32)).astype(BF16)
            to_y.start()
            r.part[t] += r.core_in[:128].astype(F32)
            put_y.wait()
            get_x_again.start()
        if step == 6:
            to_y.wait_recv()
            r.part[t] += r.y_in[...].astype(F32)
            r.x_out[...] = r.part[t, other, :].astype(BF16)
            to_x.start()
        if step == 9:
            to_x.wait_recv()
            r.z_out[...] = (r.part[t, mine, :] + r.x_in[...].astype(F32)).astype(BF16)
            keep_z.start()
            for copy in to_z:
                copy.start()

    def sum_z():
        for copy in to_z:
            copy.wait_recv()
        keep_z.wait()
        total = None
        for copy in get_z:
            copy.start()
            copy.wait()
            for i in range(batch):
                term = r.z_in[i * 64 : (i + 1) * 64].astype(F32)
                total = term if total is None else total + term
        r.full[t, mine] = total.astype(BF16)
        all_x.start()

    get_x_again = here(r.x, r.xy)

    def attend_back(n):
        row = head_row(n)
        full = ds(row // 3, hd)
        blocks = [(s, b) for s in range(seqs) for b in range(parts)]
        sent, sums = {}, {}

        def ds_place(i):
            return slice((i % 2) * seq, (i % 2 + 1) * seq), slice((i // 2 % 3) * qb, (i // 2 % 3 + 1) * qb)

        def score(i):
            s, b = blocks[i]
            token = slice(s * seq + b * qb, s * seq + (b + 1) * qb)
            do = (r.dctx[full, token].astype(F32) * r.recip[n, :, token]).astype(BF16)
            delta = jnp.sum(do.astype(F32) * r.ctx[full, token].astype(F32), axis=0, keepdims=True)
            sent[i] = do
            v = r.qkv[ds(row + 2 * hd, hd), s * seq : (s + 1) * seq]
            rows, lanes = ds_place(i)
            for kc in range(seq // 256):
                keys = slice(kc * 256, (kc + 1) * 256)
                dp = tn(v[:, keys], do)
                e = r.e[n * seqs + s, keys, b * qb : (b + 1) * qb].astype(F32)
                r.n2[rows.start + kc * 256 : rows.start + (kc + 1) * 256, lanes] = (e * (dp - delta)).astype(BF16)

        def grads(i):
            s, b = blocks[i]
            token = slice(s * seq + b * qb, s * seq + (b + 1) * qb)
            whole = slice(s * seq, (s + 1) * seq)
            k = r.qkv[ds(row + hd, hd), whole]
            q = r.qkv[ds(row, hd), token]
            rows, lanes = ds_place(i)
            dsc = r.n2[rows, lanes]
            dk = nt(q, dsc)
            dv = nt(sent[i], r.e[n * seqs + s, :, b * qb : (b + 1) * qb])
            r.qkv[ds(row, hd), token] = nn(k, dsc).astype(BF16)
            if b > 0:
                dk, dv = sums[s][0] + dk, sums[s][1] + dv
            sums[s] = dk, dv
            if b == parts - 1:
                r.qkv[ds(row + hd, hd), whole] = dk.astype(BF16)
                r.qkv[ds(row + 2 * hd, hd), whole] = dv.astype(BF16)

        ahead = 2
        for i in range(ahead):
            score(i)
        for i in range(len(blocks)):
            if i + ahead < len(blocks):
                score(i + ahead)
            grads(i)

    def adapters(k):
        g = group_at(t, k)
        block = []
        for p in range(3):
            dp = [
                r.qkv[ds((g * heads_here + h) * span + p * hd, hd), :] for h in range(heads_here)
            ]
            dp = jnp.concatenate(dp, axis=0)
            r.d_low[p][:RANK_PAD, :] += nn(r.bq[g, p * RANK_PAD : (p + 1) * RANK_PAD], dp)
            block.append(nt(r.gated[p * PAD : (p + 1) * PAD, :], dp)[:cols])
        block.append(jnp.zeros((r.b_all.shape[1] - 3 * cols, inner), F32))
        r.b_all[g] = jnp.concatenate(block, axis=0).astype(BF16)
        if k < groups - 1:
            for copy in b_give[k]:
                copy.start()

    for p in range(3):
        r.d_low[p][...] = jnp.zeros(r.d_low[p].shape, F32)

    def backward_head(n, c):
        for k in range(groups - 1):
            pl.when(n == (k + 1) * heads_here)(lambda k=k: adapters(k))
        for step in (0, 2, 6, 9):
            pl.when(n == step)(lambda step=step: sum_step(step))
        attend_back(n)
        return c

    lax.fori_loop(0, heads, backward_head, 0)
    adapters(groups - 1)

    gsm = r.acc.at[: 4 * PAD]
    gate = r.gate[...]
    prod = r.zed[...]
    for p in range(3):
        part = slice(p * PAD, (p + 1) * PAD)
        prod = prod + r.d_low[p][...] * r.low[part, :]
        r.dsmall[part, :] = (r.d_low[p][...] * gate).astype(BF16)
    high = prod.astype(BF16)
    low = (prod - high.astype(F32)).astype(BF16)
    same = lax.broadcasted_iota(jnp.int32, (PAD, PAD), 0) // rank
    same = same == lax.broadcasted_iota(jnp.int32, (PAD, PAD), 1) // rank
    same = jnp.logical_and(same, lax.broadcasted_iota(jnp.int32, (PAD, PAD), 1) < cols).astype(F32).astype(BF16)
    d_gate = nn(same, high) + nn(same, low)
    d_logit = gate * (d_gate - jnp.sum(gate * prod, axis=0, keepdims=True))
    row = lax.broadcasted_iota(jnp.int32, d_logit.shape, 0)
    chosen = jnp.logical_and(row % rank == 0, row < cols)
    r.dsmall[3 * PAD :, :] = jnp.where(chosen, d_logit, 0.0).astype(BF16)
    gsm[...] = nn(r.dsmall[...], r.n1[...])
    lines = [gsm[p * PAD : p * PAD + cols, :] for p in range(3)]
    lines.append(jnp.concatenate([gsm[3 * PAD + rank * e : 3 * PAD + rank * e + 1, :] for e in range(16)], axis=0))
    count = 3 * cols + 16
    tall = -(-count // 16) * 16
    lines.append(jnp.zeros((tall - count, width), F32))
    lines = jnp.concatenate(lines, axis=0).astype(BF16)
    strips = width // 128
    for i in range(strips):
        r.small_out[i * tall : (i + 1) * tall, :] = lines[:, i * 128 : (i + 1) * 128]
    r.small_out[strips * tall :, :] = jnp.zeros((r.small_out.shape[0] - strips * tall, 128), BF16)
    for copy in give + b_give[groups - 1]:
        copy.start()
    get_x_again.wait()

    def finish(i, c):
        rows = ds(i * tb, tb)
        dn = tn(r.qkv[:, rows], r.wqkv[...]) + tn(r.dsmall[:, rows], r.wsm[...])
        x = r.xy[rows, :].astype(F32)
        inv = lax.rsqrt(jnp.mean(x * x, axis=1, keepdims=True) + EPS)
        up = dn * g1
        r.h1[rows, :] += inv * up - x * (inv * inv * inv * jnp.mean(x * up, axis=1, keepdims=True))
        return c

    part_rows = tokens // 2
    put_x = [here(r.h1.at[i * part_rows : (i + 1) * part_rows], r.gx.at[i * part_rows : (i + 1) * part_rows]) for i in range(2)]
    lax.fori_loop(0, tokens // tb // 2, finish, 0)
    put_x[0].start()
    sum_z()
    for copy in give:
        copy.wait_recv()
    r.small_in[me] = r.small_out[ds(me * share, share), :]
    total = r.small_in[0].astype(F32)
    for i in range(1, 8):
        total = total + r.small_in[i].astype(F32)
    r.small_z[z] = total.astype(BF16)
    for copy in cross:
        copy.start()
    for copies in b_give:
        for copy in copies:
            copy.wait_recv()
    r.b_in_sum[me] = r.b_all[t, ds(half * b_share, b_share), :]
    total = r.b_in_sum[0].astype(F32)
    for i in range(1, 8):
        total = total + r.b_in_sum[i].astype(F32)
    r.b_z[z] = total.astype(BF16)
    for copy in b_cross:
        copy.start()
    lax.fori_loop(tokens // tb // 2, tokens // tb, finish, 0)
    put_x[1].start()
    all_x.wait_recv()
    all_y.start()
    all_core[0].start()
    late_sends = cross + b_cross + back + [b_back, all_x, all_y] + all_core
    for copy in links.made:
        if not any(copy is x for x in late_sends):
            copy.wait_send()
    for copy in cross:
        copy.wait_recv()
    total = r.small_z[0].astype(F32)
    for i in range(1, zs):
        total = total + r.small_z[i].astype(F32)
    r.small_full[me] = total.astype(BF16)
    for copy in back:
        copy.start()
    for copy in b_cross:
        copy.wait_recv()
    total = r.b_z[0].astype(F32)
    for i in range(1, zs):
        total = total + r.b_z[i].astype(F32)
    r.b_full[half] = total.astype(BF16)
    b_back.start()
    all_y.wait_recv()
    all_core[1].start()
    for copy in all_core:
        copy.wait_recv()
    results = [here(r.full, r.full_out), here(r.full.at[t, 2 * cols :], r.own_out)]
    for copy in results:
        copy.start()
    for copy in back + [b_back]:
        copy.wait_recv()
    late = [here(r.small_full, r.small_res), here(r.b_full, r.b_res)]
    for copy in late:
        copy.start()
    for copy in results + late:
        copy.wait()
    for copy in put_x:
        copy.wait()
    for copy in late_sends:
        copy.wait_send()


def hand_out(cols, experts, *refs):
    y, gx = refs[:2]
    y_out, gx_out = refs[6:8]
    y_buf, x_buf = refs[16:18]
    full, own, small, b_full = refs[18:22]
    g_router, g_a_in, g_a_o, g_a_out, g_b_qkv, g_b_o, g_b_in, g_b_out = refs[22:30]
    sems = refs[30]
    load = [pltpu.make_async_copy(a, b, sems.at[20 + i]) for i, (a, b) in enumerate(zip(refs[2:6], refs[18:22]))]
    store = [pltpu.make_async_copy(b, a, sems.at[24 + i]) for i, (a, b) in enumerate(zip(refs[8:16], refs[22:30]))]
    for copy in load:
        copy.start()
    pieces = [(y, y_buf, y_out, 0, y.shape[0])]
    part = gx.shape[0] // 4
    pieces += [(gx, x_buf, gx_out, i * part, (i + 1) * part) for i in range(4)]
    get = [
        pltpu.make_async_copy(a.at[lo:hi], b.at[lo:hi], sems.at[i]) for i, (a, b, _, lo, hi) in enumerate(pieces)
    ]
    put = [
        pltpu.make_async_copy(b.at[lo:hi], c.at[lo:hi], sems.at[10 + i]) for i, (_, b, c, lo, hi) in enumerate(pieces)
    ]
    for copy in get:
        copy.start()
    for copy in load:
        copy.wait()
    groups = full.shape[0]
    hidden = g_a_out.shape[1] // groups
    g_b_in[...] = own[...].astype(F32)[:cols]
    for j in range(groups):
        block = full[j].astype(F32)
        g_a_out[:, j * hidden : (j + 1) * hidden] = block[:cols]
        target = (g_a_o, g_b_o, g_b_out, g_a_in.at[3])[j]
        target[...] = block[cols : 2 * cols]
    count = 3 * cols + 16
    tall = -(-count // 16) * 16
    flat = small[...].reshape(small.shape[0] * small.shape[1], 128)
    for i in range(g_router.shape[1] // 128):
        block = flat[i * tall : (i + 1) * tall].astype(F32)
        lanes = slice(i * 128, (i + 1) * 128)
        for p in range(3):
            g_a_in[p, :, lanes] = block[p * cols : (p + 1) * cols]
        g_router[:, lanes] = block[3 * cols : 3 * cols + experts]
    block = b_full[...].reshape(b_full.shape[0] * b_full.shape[1], b_full.shape[2]).astype(F32)
    for p in range(3):
        g_b_qkv[p] = block[p * cols : (p + 1) * cols]
    for copy in store:
        copy.start()
    for one, two in zip(get, put):
        one.wait()
        two.start()
    for copy in put + store:
        copy.wait()


def shards(
    layer_inputs, lengths, first_gain, second_gain, router, wqkv, bias_table, wo, win, wout,
    a_in, a_o, a_out, b_qkv, b_o, b_in, b_out, cotangent,
):
    groups = lax.axis_size("tensor")
    zs = lax.axis_size("dp") // 2
    seqs, seq, width = layer_inputs.shape
    tokens = seqs * seq
    inner = wo.shape[0]
    heads_here = bias_table.shape[1]
    heads = heads_here * groups
    hd = inner // heads_here
    hidden = win.shape[1]
    experts = router.shape[1]
    cols = a_in.shape[2]
    sizes = (tokens, width, seq, seqs, groups, inner, heads_here, hd, hidden, cols, experts, zs)
    ins = {
        "lens": (lengths, pltpu.SMEM),
        "g1": (first_gain, pl.ANY),
        "g2": (second_gain, pl.ANY),
        "at": (jnp.swapaxes(a_in, 1, 2), pl.ANY),
        "router": (router.T, pl.ANY),
        "onehot": (jnp.asarray(bucket_lines(seq), BF16), pl.ANY),
        "b_qkv": (b_qkv, pl.ANY),
        "table": (bias_table.T, pl.ANY),
        "b_in": (b_in, pl.ANY),
        "a_o": (a_o.T, pl.ANY),
        "b_o": (b_o, pl.ANY),
        "a_out": (a_out.T, pl.ANY),
        "b_out": (b_out, pl.ANY),
        "x": (layer_inputs.reshape(tokens, width), pl.ANY),
        "c": (cotangent.reshape(tokens, width), pl.ANY),
        "wqkv_own": (jnp.swapaxes(wqkv, 1, 2), pl.ANY),
        "wo_own": (wo, pl.ANY),
        "win_own": (win, pl.ANY),
        "wout_own": (wout, pl.ANY),
    }
    landing = {n: (ins[n][0].shape, ins[n][0].dtype) for n in SMALL}
    ins = {n + "_far" if n in SMALL else n: v for n, v in ins.items()}
    outs = {
        "y": ((tokens, width), BF16, pl.ANY),
        "gx": ((tokens, width), F32, pl.ANY),
        "full_out": ((groups, 128, width), BF16, pl.ANY),
        "own_out": ((128 - 2 * cols, width), BF16, pl.ANY),
        "small_res": ((8, 112, 128), BF16, pl.ANY),
        "b_res": ((2, 64, inner), BF16, pl.ANY),
        "win_all": ((groups * width, hidden), BF16, pl.ANY),
        "z_all": ((zs * 64, width), BF16, pl.ANY),
    }
    given = [
        ((tokens, width), BF16, pl.ANY),
        ((tokens, width), F32, pl.ANY),
        ((experts, width), F32, pl.ANY),
        ((4, cols, width), F32, pltpu.VMEM),
        ((cols, width), F32, pltpu.VMEM),
        ((cols, groups * hidden), F32, pltpu.VMEM),
        ((3, cols, inner), F32, pltpu.VMEM),
        ((cols, width), F32, pltpu.VMEM),
        ((cols, hidden), F32, pltpu.VMEM),
        ((cols, width), F32, pltpu.VMEM),
    ]
    moved = [given[0][:2], given[1][:2]] + [outs[n][:2] for n in ("full_out", "own_out", "small_res", "b_res")]
    moved += [g[:2] for g in given[2:]]
    line = (PAD, tokens)
    scratch = {
        "xy": ((tokens, width), BF16),
        "cot": ((tokens, width), BF16),
        "n1": ((tokens, width), BF16),
        "low": ((3 * PAD, tokens), F32),
        "gate": (line, F32),
        "gated": ((3 * PAD, tokens), BF16),
        "wqkv": ((3 * groups * inner, width), BF16),
        "qkv": ((3 * groups * inner, tokens), BF16),
        "e": ((heads * seqs, seq, seq), BF16),
        "recip": ((heads, 1, tokens), F32),
        "ctx": ((groups * inner, tokens), BF16),
        "wsm": ((4 * PAD, width), BF16),
        "bq": ((groups, 3 * RANK_PAD, inner), BF16),
        "bh": ((heads_here, 3 * PAD, hd), BF16),
        "rb": ((groups, 16, NB), BF16),
        "bin": ((groups, PAD, hidden), BF16),
        "urow": ((heads, 1, 2 * seq), F32),
        "brow": ((2, 128, 2 * seq - 128), F32),
        "wo": ((groups * inner, width), BF16),
        "win": ((2, width, hidden), BF16),
        "wout": ((groups * hidden, width), BF16),
        "h1": ((tokens, width), F32),
        "n2": ((tokens, width), BF16),
        "acc": ((tokens, width), F32),
        "dn2": ((tokens, width), F32),
        "gin": (line, BF16),
        "dgo": (line, BF16),
        "low_o": (line, F32),
        "low_in": (line, F32),
        "low_out": (line, F32),
        "d_low_in": (line, F32),
        "d_low_out": (line, F32),
        "dctx": ((groups * inner, tokens), BF16),
        "part": ((groups, 128, width), F32),
        "ao": ((PAD, width), BF16),
        "bo": ((PAD, width), BF16),
        "ain": ((PAD, width), BF16),
        "bout": ((PAD, width), BF16),
        "aout": ((groups, PAD, hidden), BF16),
        "core_in": ((256, width), BF16),
        "y_in": ((128, width), BF16),
        "x_in": ((64, width), BF16),
        "full": ((groups, 128, width), BF16),
        "small_out": ((896, 128), BF16),
        "small_in": ((8, 112, 128), BF16),
        "small_z": ((zs, 112, 128), BF16),
        "small_full": ((8, 112, 128), BF16),
        "b_all": ((groups, 128, inner), BF16),
        "b_in_sum": ((8, 64, inner), BF16),
        "b_z": ((zs, 64, inner), BF16),
        "b_full": ((2, 64, inner), BF16),
    }
    scratch.update(landing)
    copies = 9 * 8 + 40 + 3 * zs
    shapes = [pltpu.VMEM(*v) for v in scratch.values()]
    shapes += [pltpu.SemaphoreType.DMA((copies,)), pltpu.SemaphoreType.DMA((copies,)), pltpu.SemaphoreType.DMA((64,))]
    names = list(ins) + list(outs) + list(scratch) + ["send", "recv", "local"]
    flops = 2 * tokens * (8 * width * hidden * groups + 24 * width * width)
    results = pl.pallas_call(
        lambda *refs: layer(names, sizes, *refs),
        name="encoder_layer",
        out_shape=[jax.ShapeDtypeStruct(o[0], o[1]) for o in outs.values()],
        in_specs=[pl.BlockSpec(memory_space=i[1]) for i in ins.values()],
        out_specs=[pl.BlockSpec(memory_space=o[2]) for o in outs.values()],
        scratch_shapes=shapes,
        cost_estimate=pl.CostEstimate(flops=flops, bytes_accessed=30 * 2**20, transcendentals=0),
        compiler_params=pltpu.CompilerParams(
            vmem_limit_bytes=VMEM_LIMIT, collective_id=0, has_side_effects=True
        ),
    )(*[i[0] for i in ins.values()])
    y, gx, g_router, g_in, g_ao, g_aout, g_bqkv, g_bo, g_bin, g_bout = pl.pallas_call(
        lambda *refs: hand_out(cols, experts, *refs),
        name="hand_out",
        out_shape=[jax.ShapeDtypeStruct(o[0], o[1]) for o in given],
        in_specs=[pl.BlockSpec(memory_space=pl.ANY)] * 6,
        out_specs=[pl.BlockSpec(memory_space=pl.ANY)] * len(given),
        scratch_shapes=[pltpu.VMEM(*v) for v in moved] + [pltpu.SemaphoreType.DMA((32,))],
        compiler_params=pltpu.CompilerParams(vmem_limit_bytes=VMEM_LIMIT),
    )(*results[:6])
    return (
        y.reshape(layer_inputs.shape),
        gx.reshape(layer_inputs.shape),
        g_router.T,
        jnp.swapaxes(g_in, 1, 2),
        g_ao.T,
        g_aout.T,
        g_bqkv,
        g_bo,
        g_bin,
        g_bout,
    )


def solution(mesh):
    rows = P(("dp", "tensor"), None, None)
    placed = (
        rows, P(("dp", "tensor")), P(), P(), P(), P(None, None, "tensor"), P(None, "tensor"), P("tensor", None),
        P(None, "tensor"), P("tensor", None), P(), P(), P(), P(None, None, "tensor"), P(), P(None, "tensor"), P(), rows,
    )
    return jax.shard_map(
        shards,
        mesh=mesh,
        in_specs=placed,
        out_specs=(rows, rows, P(), P(), P(), P(), P(None, None, "tensor"), P(), P(None, "tensor"), P()),
        check_vma=False,
    )
```

```python
import jax
import jax.numpy as jnp
import numpy as np
from jax import lax
from jax.experimental import pallas as pl
from jax.experimental.pallas import tpu as pltpu
from jax.sharding import PartitionSpec as P

NB = 32
MAX_DIST = 128
EPS = 1e-06
NEG = -1000000000.0
LOG2E = 1.4426950408889634
F32 = jnp.float32
BF16 = jnp.bfloat16
PAD = 64
RANK_PAD = 48
VMEM_LIMIT = 63 * 1024 * 1024
MESH = pl.DeviceIdType.MESH


def filled(a, rows):
    wide = jnp.concatenate([a.astype(F32), jnp.zeros((rows - a.shape[0], a.shape[1]), F32)], axis=0)
    return wide.astype(a.dtype)


def nn(a, b):
    return lax.dot_general(a, b, (((1,), (0,)), ((), ())), preferred_element_type=F32)


def nt(a, b):
    return lax.dot_general(a, b, (((1,), (1,)), ((), ())), preferred_element_type=F32)


def tn(a, b):
    return lax.dot_general(a, b, (((0,), (0,)), ((), ())), preferred_element_type=F32)


def ds(start, size):
    return pl.ds(pl.multiple_of(start, 16), size)


def flip(index, bit):
    return index + (1 - 2 * ((index // bit) % 2)) * bit


def group_at(member, step):
    high = (member // 2 + step // 2) % 2
    low = (member % 2 + step % 2) % 2
    return 2 * high + low


class Links:
    def __init__(self, send, recv):
        self.send, self.recv, self.made = send, recv, []

    def __call__(self, src, dst, device):
        n = len(self.made)
        copy = pltpu.make_async_remote_copy(
            src_ref=src, dst_ref=dst, send_sem=self.send.at[n], recv_sem=self.recv.at[n],
            device_id=device, device_id_type=MESH,
        )
        self.made.append(copy)
        return copy


class Places:
    def __init__(self):
        d, t = lax.axis_index("dp"), lax.axis_index("tensor")
        self.d, self.t = d, t
        self.half = d % 2
        self.quarter = d % 4
        self.core_t, self.y_t = flip(t, 1), flip(t, 2)
        self.far_t = flip(self.core_t, 2)
        self.core = (d, self.core_t)
        self.y = (d, self.y_t)
        self.across = (d, self.far_t)
        self.x = (flip(d, 1), t)
        self.z = (flip(d, 2), t)


class Chunk:
    def __init__(self, links, places, own, whole, first, base, rows, over_x):
        part = rows // 4
        q = places.quarter
        qx, qz = flip(q, 1), flip(q, 2)
        qd = flip(qx, 2)
        g, g2 = places.t, places.y_t

        def at(group, quarter):
            return whole.at[ds(first(group) + base + quarter * part, part)]

        def pass_on(quarter, device):
            return links(at(g2, quarter), at(g2, quarter), device)

        self.y = links(own.at[ds(base + q * part, part)], at(g, q), places.y)
        self.one = [pass_on(q, places.x), pass_on(q, places.z), pass_on(q, places.core)]
        self.two = [pass_on(qz, places.x) if over_x else pass_on(qx, places.z)]
        self.two += [pass_on(qx, places.core), pass_on(qz, places.core)]
        self.three = pass_on(qd, places.core)

    def start(self):
        self.y.start()

    def relay(self):
        self.y.wait_recv()
        for copy in self.one:
            copy.start()

    def forward(self):
        self.one[0].wait_recv()
        self.one[1].wait_recv()
        for copy in self.two:
            copy.start()

    def close(self):
        self.two[0].wait_recv()
        self.three.start()

    def whole_here(self):
        for copy in (self.one[2], self.two[1], self.two[2], self.three):
            copy.wait_recv()


def bucket_of(relative):
    half = NB // 2
    exact = half // 2
    distance = np.abs(relative)
    scaled = np.log(np.maximum(distance, 1) / exact) / np.log(MAX_DIST / exact) * (half - exact)
    far = np.minimum(exact + scaled.astype(np.int32), half - 1)
    return ((relative > 0) * half + np.where(distance < exact, distance, far)).astype(np.int32)


def bucket_lines(seq):
    m = np.arange(2 * seq)
    rel = seq - 128 - m
    rel = np.where(rel < -seq, rel + 2 * seq, rel)
    rel = np.clip(rel, -(seq - 1), seq - 1)
    ids = bucket_of(rel)
    return (ids[None, :] == np.arange(NB)[:, None]).astype(np.float32)


SMALL = ("b_qkv", "table", "b_in", "g1", "g2", "at", "router", "onehot", "a_o", "b_o", "a_out", "b_out")


class Names:
    def __init__(self, **refs):
        self.__dict__.update(refs)


def layer(names, sizes, *refs):
    r = Names(**dict(zip(names, refs)))
    tokens, width, seq, seqs, groups, inner, heads_here, hd, hidden, cols, experts, zs = sizes
    heads = groups * heads_here
    span = 3 * hd
    rank = cols // experts
    places = Places()
    t, d, half = places.t, places.d, places.half
    z = d // 2
    links = Links(r.send, r.recv)

    r.zed = r.low_in
    r.dsmall = r.dctx.at[: 4 * PAD]
    r.d_low = [r.low_out, r.d_low_in, r.d_low_out]
    r.core_out = [r.cot.at[:128], r.cot.at[128:256]]
    r.y_out, r.x_out, r.z_out = r.cot.at[256:384], r.cot.at[384:448], r.cot.at[448:512]
    batch = min(zs, 4)
    r.z_in = r.cot.at[512 : 512 + 64 * batch]

    local = [0]

    def here(src, dst):
        local[0] += 1
        return pltpu.make_async_copy(src, dst, r.local.at[local[0] - 1])

    get_small = [here(getattr(r, n + "_far"), getattr(r, n)) for n in SMALL]
    get_x = here(r.x, r.xy)
    get_c = here(r.c, r.cot)
    get_qkv = [
        here(
            r.wqkv_own.at[p, h * hd : (h + 1) * hd],
            r.wqkv.at[ds(t * heads_here * span + h * span + p * hd, hd)],
        )
        for h in range(heads_here)
        for p in range(3)
    ]
    for copy in get_qkv:
        copy.start()
    for copy in get_small:
        copy.start()
    get_x.start()

    z_peers = [((z + i) % zs * 2 + half, t) for i in range(1, zs)]
    same_x = [(half * 4 + j, (d, j)) for j in (places.core_t, places.y_t, places.far_t)]
    other_x = [((1 - half) * 4 + j, (flip(d, 1), j)) for j in (places.core_t, places.y_t, places.far_t, t)]
    block_peers = same_x + other_x
    barrier = pltpu.get_barrier_semaphore()
    known = [dev for _, dev in block_peers] + z_peers
    for dev in known:
        pl.semaphore_signal(barrier, inc=1, device_id=dev, device_id_type=MESH)

    def quarter_of(ref, g, rows):
        return ref.at[ds(g * rows, rows)]

    def qkv_row(g):
        return g * heads_here * span

    qkv_chunks = [
        Chunk(links, places, quarter_of(r.wqkv, t, heads_here * span), r.wqkv, qkv_row, h * span, span, h % 2 == 0)
        for h in range(heads_here)
    ]
    o_chunk = Chunk(links, places, r.wo_own, r.wo, lambda g: g * inner, 0, inner, False)
    in_chunks = [
        Chunk(links, places, r.win_own, r.win_all, lambda g: g * width, j * width // 2, width // 2, j == 0)
        for j in range(2)
    ]
    out_chunks = [
        Chunk(links, places, r.wout_own, r.wout, lambda g: g * hidden, j * hidden // 2, hidden // 2, j == 1)
        for j in range(2)
    ]

    own_qkv = quarter_of(r.wqkv, t, heads_here * span)
    core_qkv = links(own_qkv, own_qkv, places.core)
    core_o = links(r.wo_own, quarter_of(r.wo, t, inner), places.core)
    core_in = links(r.win_own, quarter_of(r.win_all, t, width), places.core)
    core_out = links(r.wout_own, quarter_of(r.wout, t, hidden), places.core)
    small = [r.bq, r.rb, r.bin]
    small_y = [links(a.at[t], a.at[t], places.y) for a in small]
    small_core = [links(a.at[t], a.at[t], places.core) for a in small]
    small_far = [links(a.at[places.y_t], a.at[places.y_t], places.core) for a in small]
    keep = [
        here(r.wo_own, quarter_of(r.wo, t, inner)),
        here(r.wout_own, quarter_of(r.wout, t, hidden)),
    ]

    for copy in get_small:
        copy.wait()
    for p in range(3):
        r.bq[t, p * RANK_PAD : (p + 1) * RANK_PAD] = filled(r.b_qkv[p], RANK_PAD)
    pick = lax.broadcasted_iota(jnp.int32, (16, heads_here), 0)
    pick = pick == lax.broadcasted_iota(jnp.int32, (16, heads_here), 1)
    r.rb[t] = nn(pick.astype(F32).astype(BF16), r.table[...]).astype(BF16)
    r.bin[t] = filled(r.b_in[...], PAD)
    for copy in get_qkv:
        copy.wait()
    pl.semaphore_wait(barrier, len(known))
    qkv_chunks[0].start()
    core_qkv.start()
    small_core[0].start()
    small_core[1].start()
    qkv_chunks[1].start()
    qkv_chunks[2].start()
    o_chunk.start()
    small_y[0].start()
    small_y[1].start()
    get_c.start()
    keep[0].start()
    for p in range(3):
        r.wsm[p * PAD : (p + 1) * PAD, :] = filled(r.at[p], PAD)
    spots = lax.broadcasted_iota(jnp.int32, (PAD, experts), 0) // rank
    spots = spots == lax.broadcasted_iota(jnp.int32, (PAD, experts), 1)
    r.wsm[3 * PAD :, :] = nn(spots.astype(F32).astype(BF16), r.router[...]).astype(BF16)
    r.ao[...] = filled(r.a_o[...], PAD)
    r.bo[...] = filled(r.b_o[...], PAD)
    r.ain[...] = filled(r.at[3], PAD)
    r.bout[...] = filled(r.b_out[...], PAD)
    for j in range(groups):
        r.aout[j] = filled(r.a_out[:, j * hidden : (j + 1) * hidden], PAD)
    g1 = r.g1[...].reshape(1, width)
    g2 = r.g2[...].reshape(1, width)

    tb = 256
    get_x.wait()

    def norm(i, c):
        rows = ds(i * tb, tb)
        x = r.xy[rows, :].astype(F32)
        n1 = (x * lax.rsqrt(jnp.mean(x * x, axis=1, keepdims=True) + EPS) * g1).astype(BF16)
        r.n1[rows, :] = n1
        lines = nt(r.wsm[...], n1)
        low = lines[: 3 * PAD]
        logits = lines[3 * PAD :]
        valid = lax.broadcasted_iota(jnp.int32, logits.shape, 0) < cols
        logits = jnp.where(valid, logits, -jnp.inf)
        ex = jnp.exp(logits - jnp.max(logits, axis=0, keepdims=True))
        gate = ex / (jnp.sum(ex, axis=0, keepdims=True) * (1.0 / rank))
        r.low[:, rows] = low
        r.gate[:, rows] = gate
        for p in range(3):
            r.gated[p * PAD : (p + 1) * PAD, rows] = (low[p * PAD : (p + 1) * PAD] * gate).astype(BF16)
        return c

    lax.fori_loop(0, tokens // tb, norm, 0)

    maskrow = jnp.where(lax.broadcasted_iota(jnp.int32, (16, seq), 1) < r.lens[seqs - 1], 0.0, NEG)
    maskrow = jnp.where(lax.broadcasted_iota(jnp.int32, (16, seq), 0) == 0, maskrow, 0.0).astype(BF16)
    onerow = (lax.broadcasted_iota(jnp.int32, (16, seq), 0) == 0).astype(F32).astype(BF16)

    def head_row(n):
        return (group_at(t, n // heads_here) * heads_here + n % heads_here) * span

    def next_group(k):
        g = group_at(t, k)
        u = nn(r.rb[g], r.onehot[...]) * LOG2E
        for h in range(heads_here):
            r.urow[k * heads_here + h] = u[h : h + 1]
            for p in range(3):
                block = r.bq[g, p * RANK_PAD : (p + 1) * RANK_PAD, h * hd : (h + 1) * hd]
                r.bh[h, p * PAD : p * PAD + RANK_PAD, :] = block

    def project(n):
        row = head_row(n)
        h = n % heads_here
        out = nt(r.wqkv[ds(row, span), :], r.n1[...])
        for p in range(3):
            up = tn(r.bh[h, p * PAD : p * PAD + RANK_PAD, :], r.gated[p * PAD : p * PAD + RANK_PAD, :])
            r.qkv[ds(row + p * hd, hd), :] = (out[p * hd : (p + 1) * hd] + up).astype(BF16)

    def spread_bias(n):
        line = jnp.broadcast_to(r.urow[n], (128, 2 * seq))
        r.brow[n % 2] = pltpu.roll(line, 0, 1, stride=1, stride_axis=0)[:, : 2 * seq - 128]

    qb = 256
    parts = seq // qb

    def score_place(i):
        return slice((i % 2) * seq, (i % 2 + 1) * seq), slice((i // 2 % 3) * qb, (i // 2 % 3 + 1) * qb)

    blocks = [(s, b) for s in range(seqs) for b in range(parts)]

    def keys_of(n, s):
        row = head_row(n)
        token = slice(s * seq, (s + 1) * seq)
        q = r.qkv[ds(row, hd), token]
        k = r.qkv[ds(row + hd, hd), token].astype(F32) * LOG2E
        high = k.astype(BF16)
        keys = [high, (k - high.astype(F32)).astype(BF16)]
        queries = [q, q]
        if s > 0:
            keys.append(maskrow)
            queries.append(onerow)
        return jnp.concatenate(keys, axis=0), jnp.concatenate(queries, axis=0)

    def values_of(n):
        row = head_row(n)
        return [
            jnp.concatenate([r.qkv[ds(row + 2 * hd, hd), s * seq : (s + 1) * seq], onerow], axis=0)
            for s in range(seqs)
        ]

    def score(n, i, made):
        s, b = blocks[i]
        if b == 0:
            made[s] = keys_of(n, s)
        keys, queries = made[s]
        top = None
        rows, lanes = score_place(i)
        for kc in range(seq // 256):
            st = tn(keys[:, kc * 256 : (kc + 1) * 256], queries[:, b * qb : (b + 1) * qb])
            for kk in range(2):
                kb = kc * 2 + kk
                shift = seq - 128 - 128 * kb + b * qb
                st_b = st[kk * 128 : (kk + 1) * 128] + r.brow[n % 2, :, shift : shift + qb]
                r.acc[rows.start + kb * 128 : rows.start + (kb + 1) * 128, lanes] = st_b
                peak = jnp.max(st_b, axis=0, keepdims=True)
                top = peak if top is None else jnp.maximum(top, peak)
        return top

    def soft(n, i, top, values):
        s, b = blocks[i]
        rows, lanes = score_place(i)
        token = slice(s * seq + b * qb, s * seq + (b + 1) * qb)
        for kb in range(seq // 128):
            st = r.acc[rows.start + kb * 128 : rows.start + (kb + 1) * 128, lanes]
            r.e[n * seqs + s, kb * 128 : (kb + 1) * 128, b * qb : (b + 1) * qb] = jnp.exp2(st - top).astype(BF16)
        o = nn(values[s], r.e[n * seqs + s, :, b * qb : (b + 1) * qb])
        recip = 1.0 / o[hd : hd + 1]
        r.recip[n, :, token] = recip
        r.ctx[ds(head_row(n) // 3, hd), token] = (o[:hd] * recip).astype(BF16)

    def forward_step(step):
        if step == 0:
            qkv_chunks[0].relay()
        if step == 1:
            qkv_chunks[1].relay()
            in_chunks[0].start()
        if step == 2:
            qkv_chunks[2].relay()
            core_qkv.wait_recv()
            small_core[0].wait_recv()
            small_core[1].wait_recv()
            core_o.start()
        if step == 3:
            qkv_chunks[0].forward()
            in_chunks[1].start()
        if step == 4:
            qkv_chunks[1].forward()
        if step == 5:
            qkv_chunks[0].close()
            qkv_chunks[2].forward()
            small_y[0].wait_recv()
            small_y[1].wait_recv()
            small_far[0].start()
            small_far[1].start()
            o_chunk.relay()
        if step == 6:
            qkv_chunks[1].close()
            out_chunks[0].start()
        if step == 7:
            qkv_chunks[2].close()
            o_chunk.forward()
            in_chunks[0].relay()
            core_in.start()
            small_y[2].start()
            small_core[2].start()
        if step == 8:
            small_far[0].wait_recv()
            small_far[1].wait_recv()
            qkv_chunks[0].whole_here()
            out_chunks[1].start()
        if step == 9:
            qkv_chunks[1].whole_here()
            o_chunk.close()
            in_chunks[1].relay()
        if step == 10:
            qkv_chunks[2].whole_here()
            core_out.start()
            keep[1].start()
        if step == 11:
            in_chunks[0].forward()
            out_chunks[0].relay()

    def first_step(step):
        if step == 1:
            in_chunks[1].forward()
            out_chunks[1].relay()

    def forward_head(n, tops):
        for step in range(12):
            pl.when(n == step)(lambda step=step: forward_step(step))
        follow = jnp.minimum(n + 1, heads - 1)

        @pl.when(jnp.logical_and(follow % heads_here == 0, n < heads - 1))
        def _():
            next_group(follow // heads_here)

        values = values_of(n)
        project(follow)
        spread_bias(follow)
        made, fresh = {}, []
        behind = 2
        for i in range(len(blocks)):
            soft(n, i, tops[i], values)
            if i + 1 >= behind:
                fresh.append(score(follow, i + 1 - behind, made))
        for i in range(len(fresh), len(blocks)):
            fresh.append(score(follow, i, made))
        return tuple(fresh)

    next_group(0)
    project(0)
    spread_bias(0)
    made = {}
    lax.fori_loop(0, heads, forward_head, tuple(score(0, i, made) for i in range(len(blocks))))

    core_o.wait_recv()
    keep[0].wait()
    o_chunk.whole_here()
    get_c.wait()
    win_first = here(r.win_own, r.win.at[0])
    win_first.start()

    def first(i, c):
        pl.when(i == 1)(lambda: first_step(1))
        for j in range(2):
            rows = ds((2 * i + j) * tb, tb)
            gate = r.gate[:, rows]
            ctx = r.ctx[:, rows]
            low = nn(r.ao[...], ctx)
            r.low_o[:, rows] = low
            gated = (low * gate).astype(BF16)
            h1 = r.xy[rows, :].astype(F32) + tn(ctx, r.wo[...]) + tn(gated, r.bo[...])
            r.h1[rows, :] = h1
            r.acc[rows, :] = h1
            r.dn2[rows, :] = jnp.zeros_like(h1)
            n2 = (h1 * lax.rsqrt(jnp.mean(h1 * h1, axis=1, keepdims=True) + EPS) * g2).astype(BF16)
            r.n2[rows, :] = n2
            low = nt(r.ain[...], n2)
            r.low_in[:, rows] = low
            r.gin[:, rows] = (low * gate).astype(BF16)
            low = nt(r.bout[...], r.cot[rows, :])
            r.d_low_out[:, rows] = low
            r.dgo[:, rows] = (low * gate).astype(BF16)
        return c

    lax.fori_loop(0, tokens // tb // 2, first, 0)
    r.low_out[...] = jnp.zeros_like(r.low_out)
    r.d_low_in[...] = jnp.zeros_like(r.d_low_in)
    r.part[...] = jnp.zeros_like(r.part)

    wide = 512
    steps = tokens // wide
    win_next = [here(quarter_of(r.win_all, group_at(t, k), width), r.win.at[k % 2]) for k in range(1, groups)]

    def feed_step(step):
        if step == 0:
            keep[1].wait()
            win_first.wait()
            in_chunks[0].close()
            out_chunks[0].forward()
            core_in.wait_recv()
            win_next[0].start()
            small_y[2].wait_recv()
            small_far[2].start()
        if step == 1:
            in_chunks[1].close()
            out_chunks[1].forward()
        if step == 2:
            out_chunks[0].close()
            core_out.wait_recv()
            small_core[2].wait_recv()
            win_next[0].wait()
            win_next[1].start()
        if step == 3:
            out_chunks[1].close()
        if step == 4:
            for chunk in in_chunks:
                chunk.whole_here()
            win_next[1].wait()
            win_next[2].start()
        if step == 6:
            small_far[2].wait_recv()
            for chunk in out_chunks:
                chunk.whole_here()
            win_next[2].wait()

    active, d_pre = r.xy.at[:wide], r.xy.at[wide : 2 * wide]
    third = hidden // 3

    def chunk(step, c):
        for point in range(7):
            pl.when(step == point)(lambda point=point: feed_step(point))
        n = step // steps
        rows = ds((step % steps) * wide, wide)
        g = group_at(t, n)
        slot = n % 2
        gin, dgo = r.gin[:, rows], r.dgo[:, rows]
        for j in range(3):
            cs = slice(j * third, (j + 1) * third)
            pre = nn(r.n2[rows, :], r.win[slot, :, cs]) + tn(gin, r.bin[g, :, cs])
            da = nt(r.cot[rows, :], r.wout[ds(g * hidden + j * third, third), :]) + tn(dgo, r.aout[g, :, cs])
            sig = 1.0 / (1.0 + jnp.exp(-pre))
            act = pre * sig
            active[:, cs] = act.astype(BF16)
            d_pre[:, cs] = (da * (sig + act * (1.0 - sig))).astype(BF16)
        r.acc[rows, :] += nn(active[...], r.wout[ds(g * hidden, hidden), :])
        r.dn2[rows, :] += nt(d_pre[...], r.win[slot])
        r.low_out[:, rows] += nt(r.aout[g], active[...])
        r.d_low_in[:, rows] += nt(r.bin[g], d_pre[...])
        r.part[g, :cols] += nn(dgo, active[...])[:cols]
        r.part[g, 2 * cols : 3 * cols] += nn(gin, d_pre[...])[:cols]
        return c

    lax.fori_loop(0, groups * steps, chunk, 0)

    def last(i, c):
        for j in range(2):
            rows = ds((2 * i + j) * tb, tb)
            gate = r.gate[:, rows]
            cot, n2, ctx, h1 = r.cot[rows, :], r.n2[rows, :], r.ctx[:, rows], r.h1[rows, :]
            low_out, d_low_in = r.low_out[:, rows], r.d_low_in[:, rows]
            go = (low_out * gate).astype(BF16)
            r.xy[rows, :] = (r.acc[rows, :] + tn(go, r.bout[...])).astype(BF16)
            dgi = (d_low_in * gate).astype(BF16)
            up = (r.dn2[rows, :] + tn(dgi, r.ain[...])) * g2
            r.part[2, cols : 2 * cols] += nn(go, cot)[:cols]
            r.part[3, cols : 2 * cols] += nn(dgi, n2)[:cols]
            inv = lax.rsqrt(jnp.mean(h1 * h1, axis=1, keepdims=True) + EPS)
            dh = cot.astype(F32) + inv * up - h1 * (inv * inv * inv * jnp.mean(h1 * up, axis=1, keepdims=True))
            r.h1[rows, :] = dh
            da = dh.astype(BF16)
            d_low = nt(r.bo[...], da)
            low = r.low_o[:, rows]
            dgo = (d_low * gate).astype(BF16)
            r.part[1, cols : 2 * cols] += nn((low * gate).astype(BF16), da)[:cols]
            r.part[0, cols : 2 * cols] += nt(dgo, ctx)[:cols]
            r.dctx[:, rows] = (nt(r.wo[...], da) + tn(r.ao[...], dgo)).astype(BF16)
            r.zed[:, rows] = d_low * low + d_low_in * r.low_in[:, rows] + r.d_low_out[:, rows] * low_out
        return c

    lax.fori_loop(0, tokens // tb // 2, last, 0)
    put_y = here(r.xy, r.y)
    put_y.start()

    rows_half = 64
    mine, other = ds(half * rows_half, rows_half), ds((1 - half) * rows_half, rows_half)
    shared = 2 * cols
    to_core = links(r.cot.at[:256], r.core_in, places.core)
    to_y = links(r.y_out, r.y_in, places.y)
    to_x = links(r.x_out, r.x_in, places.x)
    to_z = [links(r.z_out, r.z_all.at[ds(z * 64, 64)], dev) for dev in z_peers]
    keep_z = here(r.z_out, r.z_all.at[ds(z * 64, 64)])
    get_z = [here(r.z_all.at[i * 64 : (i + batch) * 64], r.z_in) for i in range(0, zs, batch)]
    all_x = links(r.full.at[t, mine], r.full.at[t, mine], places.x)
    all_y = links(r.full.at[t, :shared], r.full.at[t, :shared], places.y)
    all_core = [
        links(r.full.at[j, :shared], r.full.at[j, :shared], places.core) for j in (t, places.y_t)
    ]
    share = r.small_in.shape[1]
    b_share = r.b_in_sum.shape[1]
    me = half * 4 + t
    give = []
    for j, dev in block_peers:
        give.append(links(r.small_out.at[ds(j * share, share)], r.small_in.at[me], dev))
    b_give = []
    for g in (t, places.core_t, places.y_t, places.far_t):
        there = [(1 - half, (flip(d, 1), g))] + ([(half, (d, g))] if b_give else [])
        b_give.append(
            [links(r.b_all.at[g, ds(h * b_share, b_share)], r.b_in_sum.at[me], dev) for h, dev in there]
        )
    cross = [links(r.small_z.at[z], r.small_z.at[z], dev) for dev in z_peers]
    b_cross = [links(r.b_z.at[z], r.b_z.at[z], dev) for dev in z_peers]
    back = [links(r.small_full.at[me], r.small_full.at[me], dev) for _, dev in block_peers]
    b_back = links(r.b_full.at[half], r.b_full.at[half], places.x)

    def sum_step(step):
        if step == 0:
            r.core_out[0][...] = r.part[places.core_t].astype(BF16)
            r.core_out[1][...] = r.part[places.far_t].astype(BF16)
            to_core.start()
        if step == 2:
            to_core.wait_recv()
            r.y_out[...] = (r.part[places.y_t] + r.core_in[128:].astype(F32)).astype(BF16)
            to_y.start()
            r.part[t] += r.core_in[:128].astype(F32)
            put_y.wait()
            get_x_again.start()
        if step == 6:
            to_y.wait_recv()
            r.part[t] += r.y_in[...].astype(F32)
            r.x_out[...] = r.part[t, other, :].astype(BF16)
            to_x.start()
        if step == 9:
            to_x.wait_recv()
            r.z_out[...] = (r.part[t, mine, :] + r.x_in[...].astype(F32)).astype(BF16)
            keep_z.start()
            for copy in to_z:
                copy.start()

    def sum_z():
        for copy in to_z:
            copy.wait_recv()
        keep_z.wait()
        total = None
        for copy in get_z:
            copy.start()
            copy.wait()
            for i in range(batch):
                term = r.z_in[i * 64 : (i + 1) * 64].astype(F32)
                total = term if total is None else total + term
        r.full[t, mine] = total.astype(BF16)
        all_x.start()

    get_x_again = here(r.x, r.xy)

    def attend_back(n):
        row = head_row(n)
        full = ds(row // 3, hd)
        blocks = [(s, b) for s in range(seqs) for b in range(parts)]
        sent, sums = {}, {}

        def ds_place(i):
            return slice((i % 2) * seq, (i % 2 + 1) * seq), slice((i // 2 % 3) * qb, (i // 2 % 3 + 1) * qb)

        def score(i):
            s, b = blocks[i]
            token = slice(s * seq + b * qb, s * seq + (b + 1) * qb)
            do = (r.dctx[full, token].astype(F32) * r.recip[n, :, token]).astype(BF16)
            delta = jnp.sum(do.astype(F32) * r.ctx[full, token].astype(F32), axis=0, keepdims=True)
            sent[i] = do
            v = r.qkv[ds(row + 2 * hd, hd), s * seq : (s + 1) * seq]
            rows, lanes = ds_place(i)
            for kc in range(seq // 256):
                keys = slice(kc * 256, (kc + 1) * 256)
                dp = tn(v[:, keys], do)
                e = r.e[n * seqs + s, keys, b * qb : (b + 1) * qb].astype(F32)
                r.n2[rows.start + kc * 256 : rows.start + (kc + 1) * 256, lanes] = (e * (dp - delta)).astype(BF16)

        def grads(i):
            s, b = blocks[i]
            token = slice(s * seq + b * qb, s * seq + (b + 1) * qb)
            whole = slice(s * seq, (s + 1) * seq)
            k = r.qkv[ds(row + hd, hd), whole]
            q = r.qkv[ds(row, hd), token]
            rows, lanes = ds_place(i)
            dsc = r.n2[rows, lanes]
            dk = nt(q, dsc)
            dv = nt(sent[i], r.e[n * seqs + s, :, b * qb : (b + 1) * qb])
            r.qkv[ds(row, hd), token] = nn(k, dsc).astype(BF16)
            if b > 0:
                dk, dv = sums[s][0] + dk, sums[s][1] + dv
            sums[s] = dk, dv
            if b == parts - 1:
                r.qkv[ds(row + hd, hd), whole] = dk.astype(BF16)
                r.qkv[ds(row + 2 * hd, hd), whole] = dv.astype(BF16)

        ahead = 2
        for i in range(ahead):
            score(i)
        for i in range(len(blocks)):
            if i + ahead < len(blocks):
                score(i + ahead)
            grads(i)

    def adapters(k):
        g = group_at(t, k)
        block = []
        for p in range(3):
            dp = [
                r.qkv[ds((g * heads_here + h) * span + p * hd, hd), :] for h in range(heads_here)
            ]
            dp = jnp.concatenate(dp, axis=0)
            r.d_low[p][:RANK_PAD, :] += nn(r.bq[g, p * RANK_PAD : (p + 1) * RANK_PAD], dp)
            block.append(nt(r.gated[p * PAD : (p + 1) * PAD, :], dp)[:cols])
        block.append(jnp.zeros((r.b_all.shape[1] - 3 * cols, inner), F32))
        r.b_all[g] = jnp.concatenate(block, axis=0).astype(BF16)
        if k < groups - 1:
            for copy in b_give[k]:
                copy.start()

    for p in range(3):
        r.d_low[p][...] = jnp.zeros(r.d_low[p].shape, F32)

    def backward_head(n, c):
        for k in range(groups - 1):
            pl.when(n == (k + 1) * heads_here)(lambda k=k: adapters(k))
        for step in (0, 2, 6, 9):
            pl.when(n == step)(lambda step=step: sum_step(step))
        attend_back(n)
        return c

    lax.fori_loop(0, heads, backward_head, 0)
    adapters(groups - 1)

    gsm = r.acc.at[: 4 * PAD]
    gate = r.gate[...]
    prod = r.zed[...]
    for p in range(3):
        part = slice(p * PAD, (p + 1) * PAD)
        prod = prod + r.d_low[p][...] * r.low[part, :]
        r.dsmall[part, :] = (r.d_low[p][...] * gate).astype(BF16)
    high = prod.astype(BF16)
    low = (prod - high.astype(F32)).astype(BF16)
    same = lax.broadcasted_iota(jnp.int32, (PAD, PAD), 0) // rank
    same = same == lax.broadcasted_iota(jnp.int32, (PAD, PAD), 1) // rank
    same = jnp.logical_and(same, lax.broadcasted_iota(jnp.int32, (PAD, PAD), 1) < cols).astype(F32).astype(BF16)
    d_gate = nn(same, high) + nn(same, low)
    d_logit = gate * (d_gate - jnp.sum(gate * prod, axis=0, keepdims=True))
    row = lax.broadcasted_iota(jnp.int32, d_logit.shape, 0)
    chosen = jnp.logical_and(row % rank == 0, row < cols)
    r.dsmall[3 * PAD :, :] = jnp.where(chosen, d_logit, 0.0).astype(BF16)
    gsm[...] = nn(r.dsmall[...], r.n1[...])
    lines = [gsm[p * PAD : p * PAD + cols, :] for p in range(3)]
    lines.append(jnp.concatenate([gsm[3 * PAD + rank * e : 3 * PAD + rank * e + 1, :] for e in range(16)], axis=0))
    count = 3 * cols + 16
    tall = -(-count // 16) * 16
    lines.append(jnp.zeros((tall - count, width), F32))
    lines = jnp.concatenate(lines, axis=0).astype(BF16)
    strips = width // 128
    for i in range(strips):
        r.small_out[i * tall : (i + 1) * tall, :] = lines[:, i * 128 : (i + 1) * 128]
    r.small_out[strips * tall :, :] = jnp.zeros((r.small_out.shape[0] - strips * tall, 128), BF16)
    for copy in give + b_give[groups - 1]:
        copy.start()
    get_x_again.wait()

    def finish(i, c):
        rows = ds(i * tb, tb)
        dn = tn(r.qkv[:, rows], r.wqkv[...]) + tn(r.dsmall[:, rows], r.wsm[...])
        x = r.xy[rows, :].astype(F32)
        inv = lax.rsqrt(jnp.mean(x * x, axis=1, keepdims=True) + EPS)
        up = dn * g1
        r.h1[rows, :] += inv * up - x * (inv * inv * inv * jnp.mean(x * up, axis=1, keepdims=True))
        return c

    part_rows = tokens // 2
    put_x = [here(r.h1.at[i * part_rows : (i + 1) * part_rows], r.gx.at[i * part_rows : (i + 1) * part_rows]) for i in range(2)]
    lax.fori_loop(0, tokens // tb // 2, finish, 0)
    put_x[0].start()
    for copy in give:
        copy.wait_recv()
    r.small_in[me] = r.small_out[ds(me * share, share), :]
    total = r.small_in[0].astype(F32)
    for i in range(1, 8):
        total = total + r.small_in[i].astype(F32)
    r.small_z[z] = total.astype(BF16)
    for copy in cross:
        copy.start()
    sum_z()
    for copies in b_give:
        for copy in copies:
            copy.wait_recv()
    r.b_in_sum[me] = r.b_all[t, ds(half * b_share, b_share), :]
    total = r.b_in_sum[0].astype(F32)
    for i in range(1, 8):
        total = total + r.b_in_sum[i].astype(F32)
    r.b_z[z] = total.astype(BF16)
    for copy in b_cross:
        copy.start()
    lax.fori_loop(tokens // tb // 2, tokens // tb, finish, 0)
    put_x[1].start()
    all_x.wait_recv()
    all_y.start()
    all_core[0].start()
    late_sends = cross + b_cross + back + [b_back, all_x, all_y] + all_core
    for copy in links.made:
        if not any(copy is x for x in late_sends):
            copy.wait_send()
    for copy in cross:
        copy.wait_recv()
    total = r.small_z[0].astype(F32)
    for i in range(1, zs):
        total = total + r.small_z[i].astype(F32)
    r.small_full[me] = total.astype(BF16)
    for copy in back:
        copy.start()
    for copy in b_cross:
        copy.wait_recv()
    total = r.b_z[0].astype(F32)
    for i in range(1, zs):
        total = total + r.b_z[i].astype(F32)
    r.b_full[half] = total.astype(BF16)
    b_back.start()
    all_y.wait_recv()
    all_core[1].start()
    for copy in all_core:
        copy.wait_recv()
    results = [here(r.full, r.full_out), here(r.full.at[t, 2 * cols :], r.own_out)]
    for copy in results:
        copy.start()
    for copy in back + [b_back]:
        copy.wait_recv()
    late = [here(r.small_full, r.small_res), here(r.b_full, r.b_res)]
    for copy in late:
        copy.start()
    for copy in results + late:
        copy.wait()
    for copy in put_x:
        copy.wait()
    for copy in late_sends:
        copy.wait_send()


def hand_out(cols, experts, *refs):
    y, gx = refs[:2]
    y_out, gx_out = refs[6:8]
    y_buf, x_buf = refs[16:18]
    full, own, small, b_full = refs[18:22]
    g_router, g_a_in, g_a_o, g_a_out, g_b_qkv, g_b_o, g_b_in, g_b_out = refs[22:30]
    sems = refs[30]
    load = [pltpu.make_async_copy(a, b, sems.at[20 + i]) for i, (a, b) in enumerate(zip(refs[2:6], refs[18:22]))]
    store = [pltpu.make_async_copy(b, a, sems.at[24 + i]) for i, (a, b) in enumerate(zip(refs[8:16], refs[22:30]))]
    for copy in load:
        copy.start()
    pieces = [(y, y_buf, y_out, 0, y.shape[0])]
    part = gx.shape[0] // 4
    pieces += [(gx, x_buf, gx_out, i * part, (i + 1) * part) for i in range(4)]
    get = [
        pltpu.make_async_copy(a.at[lo:hi], b.at[lo:hi], sems.at[i]) for i, (a, b, _, lo, hi) in enumerate(pieces)
    ]
    put = [
        pltpu.make_async_copy(b.at[lo:hi], c.at[lo:hi], sems.at[10 + i]) for i, (_, b, c, lo, hi) in enumerate(pieces)
    ]
    for copy in get:
        copy.start()
    for copy in load:
        copy.wait()
    groups = full.shape[0]
    hidden = g_a_out.shape[1] // groups
    g_b_in[...] = own[...].astype(F32)[:cols]
    for j in range(groups):
        block = full[j].astype(F32)
        g_a_out[:, j * hidden : (j + 1) * hidden] = block[:cols]
        target = (g_a_o, g_b_o, g_b_out, g_a_in.at[3])[j]
        target[...] = block[cols : 2 * cols]
    count = 3 * cols + 16
    tall = -(-count // 16) * 16
    flat = small[...].reshape(small.shape[0] * small.shape[1], 128)
    for i in range(g_router.shape[1] // 128):
        block = flat[i * tall : (i + 1) * tall].astype(F32)
        lanes = slice(i * 128, (i + 1) * 128)
        for p in range(3):
            g_a_in[p, :, lanes] = block[p * cols : (p + 1) * cols]
        g_router[:, lanes] = block[3 * cols : 3 * cols + experts]
    block = b_full[...].reshape(b_full.shape[0] * b_full.shape[1], b_full.shape[2]).astype(F32)
    for p in range(3):
        g_b_qkv[p] = block[p * cols : (p + 1) * cols]
    for copy in store:
        copy.start()
    for one, two in zip(get, put):
        one.wait()
        two.start()
    for copy in put + store:
        copy.wait()


def shards(
    layer_inputs, lengths, first_gain, second_gain, router, wqkv, bias_table, wo, win, wout,
    a_in, a_o, a_out, b_qkv, b_o, b_in, b_out, cotangent,
):
    groups = lax.axis_size("tensor")
    zs = lax.axis_size("dp") // 2
    seqs, seq, width = layer_inputs.shape
    tokens = seqs * seq
    inner = wo.shape[0]
    heads_here = bias_table.shape[1]
    heads = heads_here * groups
    hd = inner // heads_here
    hidden = win.shape[1]
    experts = router.shape[1]
    cols = a_in.shape[2]
    sizes = (tokens, width, seq, seqs, groups, inner, heads_here, hd, hidden, cols, experts, zs)
    ins = {
        "lens": (lengths, pltpu.SMEM),
        "g1": (first_gain, pl.ANY),
        "g2": (second_gain, pl.ANY),
        "at": (jnp.swapaxes(a_in, 1, 2), pl.ANY),
        "router": (router.T, pl.ANY),
        "onehot": (jnp.asarray(bucket_lines(seq), BF16), pl.ANY),
        "b_qkv": (b_qkv, pl.ANY),
        "table": (bias_table.T, pl.ANY),
        "b_in": (b_in, pl.ANY),
        "a_o": (a_o.T, pl.ANY),
        "b_o": (b_o, pl.ANY),
        "a_out": (a_out.T, pl.ANY),
        "b_out": (b_out, pl.ANY),
        "x": (layer_inputs.reshape(tokens, width), pl.ANY),
        "c": (cotangent.reshape(tokens, width), pl.ANY),
        "wqkv_own": (jnp.swapaxes(wqkv, 1, 2), pl.ANY),
        "wo_own": (wo, pl.ANY),
        "win_own": (win, pl.ANY),
        "wout_own": (wout, pl.ANY),
    }
    landing = {n: (ins[n][0].shape, ins[n][0].dtype) for n in SMALL}
    ins = {n + "_far" if n in SMALL else n: v for n, v in ins.items()}
    outs = {
        "y": ((tokens, width), BF16, pl.ANY),
        "gx": ((tokens, width), F32, pl.ANY),
        "full_out": ((groups, 128, width), BF16, pl.ANY),
        "own_out": ((128 - 2 * cols, width), BF16, pl.ANY),
        "small_res": ((8, 112, 128), BF16, pl.ANY),
        "b_res": ((2, 64, inner), BF16, pl.ANY),
        "win_all": ((groups * width, hidden), BF16, pl.ANY),
        "z_all": ((zs * 64, width), BF16, pl.ANY),
    }
    given = [
        ((tokens, width), BF16, pl.ANY),
        ((tokens, width), F32, pl.ANY),
        ((experts, width), F32, pl.ANY),
        ((4, cols, width), F32, pltpu.VMEM),
        ((cols, width), F32, pltpu.VMEM),
        ((cols, groups * hidden), F32, pltpu.VMEM),
        ((3, cols, inner), F32, pltpu.VMEM),
        ((cols, width), F32, pltpu.VMEM),
        ((cols, hidden), F32, pltpu.VMEM),
        ((cols, width), F32, pltpu.VMEM),
    ]
    moved = [given[0][:2], given[1][:2]] + [outs[n][:2] for n in ("full_out", "own_out", "small_res", "b_res")]
    moved += [g[:2] for g in given[2:]]
    line = (PAD, tokens)
    scratch = {
        "xy": ((tokens, width), BF16),
        "cot": ((tokens, width), BF16),
        "n1": ((tokens, width), BF16),
        "low": ((3 * PAD, tokens), F32),
        "gate": (line, F32),
        "gated": ((3 * PAD, tokens), BF16),
        "wqkv": ((3 * groups * inner, width), BF16),
        "qkv": ((3 * groups * inner, tokens), BF16),
        "e": ((heads * seqs, seq, seq), BF16),
        "recip": ((heads, 1, tokens), F32),
        "ctx": ((groups * inner, tokens), BF16),
        "wsm": ((4 * PAD, width), BF16),
        "bq": ((groups, 3 * RANK_PAD, inner), BF16),
        "bh": ((heads_here, 3 * PAD, hd), BF16),
        "rb": ((groups, 16, NB), BF16),
        "bin": ((groups, PAD, hidden), BF16),
        "urow": ((heads, 1, 2 * seq), F32),
        "brow": ((2, 128, 2 * seq - 128), F32),
        "wo": ((groups * inner, width), BF16),
        "win": ((2, width, hidden), BF16),
        "wout": ((groups * hidden, width), BF16),
        "h1": ((tokens, width), F32),
        "n2": ((tokens, width), BF16),
        "acc": ((tokens, width), F32),
        "dn2": ((tokens, width), F32),
        "gin": (line, BF16),
        "dgo": (line, BF16),
        "low_o": (line, F32),
        "low_in": (line, F32),
        "low_out": (line, F32),
        "d_low_in": (line, F32),
        "d_low_out": (line, F32),
        "dctx": ((groups * inner, tokens), BF16),
        "part": ((groups, 128, width), F32),
        "ao": ((PAD, width), BF16),
        "bo": ((PAD, width), BF16),
        "ain": ((PAD, width), BF16),
        "bout": ((PAD, width), BF16),
        "aout": ((groups, PAD, hidden), BF16),
        "core_in": ((256, width), BF16),
        "y_in": ((128, width), BF16),
        "x_in": ((64, width), BF16),
        "full": ((groups, 128, width), BF16),
        "small_out": ((896, 128), BF16),
        "small_in": ((8, 112, 128), BF16),
        "small_z": ((zs, 112, 128), BF16),
        "small_full": ((8, 112, 128), BF16),
        "b_all": ((groups, 128, inner), BF16),
        "b_in_sum": ((8, 64, inner), BF16),
        "b_z": ((zs, 64, inner), BF16),
        "b_full": ((2, 64, inner), BF16),
    }
    scratch.update(landing)
    copies = 9 * 8 + 40 + 3 * zs
    shapes = [pltpu.VMEM(*v) for v in scratch.values()]
    shapes += [pltpu.SemaphoreType.DMA((copies,)), pltpu.SemaphoreType.DMA((copies,)), pltpu.SemaphoreType.DMA((64,))]
    names = list(ins) + list(outs) + list(scratch) + ["send", "recv", "local"]
    flops = 2 * tokens * (8 * width * hidden * groups + 24 * width * width)
    results = pl.pallas_call(
        lambda *refs: layer(names, sizes, *refs),
        name="encoder_layer",
        out_shape=[jax.ShapeDtypeStruct(o[0], o[1]) for o in outs.values()],
        in_specs=[pl.BlockSpec(memory_space=i[1]) for i in ins.values()],
        out_specs=[pl.BlockSpec(memory_space=o[2]) for o in outs.values()],
        scratch_shapes=shapes,
        cost_estimate=pl.CostEstimate(flops=flops, bytes_accessed=30 * 2**20, transcendentals=0),
        compiler_params=pltpu.CompilerParams(
            vmem_limit_bytes=VMEM_LIMIT, collective_id=0, has_side_effects=True
        ),
    )(*[i[0] for i in ins.values()])
    y, gx, g_router, g_in, g_ao, g_aout, g_bqkv, g_bo, g_bin, g_bout = pl.pallas_call(
        lambda *refs: hand_out(cols, experts, *refs),
        name="hand_out",
        out_shape=[jax.ShapeDtypeStruct(o[0], o[1]) for o in given],
        in_specs=[pl.BlockSpec(memory_space=pl.ANY)] * 6,
        out_specs=[pl.BlockSpec(memory_space=pl.ANY)] * len(given),
        scratch_shapes=[pltpu.VMEM(*v) for v in moved] + [pltpu.SemaphoreType.DMA((32,))],
        compiler_params=pltpu.CompilerParams(vmem_limit_bytes=VMEM_LIMIT),
    )(*results[:6])
    return (
        y.reshape(layer_inputs.shape),
        gx.reshape(layer_inputs.shape),
        g_router.T,
        jnp.swapaxes(g_in, 1, 2),
        g_ao.T,
        g_aout.T,
        g_bqkv,
        g_bo,
        g_bin,
        g_bout,
    )


def solution(mesh):
    rows = P(("dp", "tensor"), None, None)
    placed = (
        rows, P(("dp", "tensor")), P(), P(), P(), P(None, None, "tensor"), P(None, "tensor"), P("tensor", None),
        P(None, "tensor"), P("tensor", None), P(), P(), P(), P(None, None, "tensor"), P(), P(None, "tensor"), P(), rows,
    )
    return jax.shard_map(
        shards,
        mesh=mesh,
        in_specs=placed,
        out_specs=(rows, rows, P(), P(), P(), P(), P(None, None, "tensor"), P(), P(None, "tensor"), P()),
        check_vma=False,
    )
```
